32 devices in a mesh: members: 2 (over x), lat: 16 (over z, y, core).
Axes of the slice: x: 2, y: 2, z: 4, core: 2. Of those that a mesh axis runs over, the one named last changes fastest.
Arguments:
- tracer: float32 [16, 128, 1440], P(None, ('members', 'lat')), parts along dimension 1, may hold values from -6 to 6
- diffusivity: float32 [64, 1440], P('lat'), may hold values from 0.02 to 0.18
- direction: float32 [128, 1440], P(('members', 'lat')), parts along dimension 0, may hold values from -0.015625 to 0.015625
- column_depth: int32 [64, 1440], P('lat'), may hold values from 0 to 16
- density_class: int32 [16, 128, 1440], P(None, ('members', 'lat')), parts along dimension 1, may hold values from 0 to 71
- band_of_row: int32 [64], P('lat'), may hold values from 0 to 31, as said below
- weights: float32 [32, 72], replicated, may hold values from 0.02 to 0.2
Outputs:
- binned: float32 [64, 72], P(('members', 'lat')), parts along dimension 0
- gradient: float32 [128, 1440], P(('members', 'lat')), parts along dimension 0
The draws below stay inside these ranges and needn't reach their ends.
There are 2 independent parts, one for each index of `members`. The reference program is written for one: setup_inputs(seed, part) draws one part's arguments, and reference() takes and returns one part's arrays. A program takes and returns all parts, laid end to end along the dimension named above; an argument that names none is the same for every part. Nothing has to cross between parts.
Inputs may be any that keep to these rules, and one draw needn't show every extreme that they name: `band_of_row`: rows come in runs of 2 consecutive latitudes that share one band number, and each band number belongs to exactly one run.
All inputs are finite; a program needn't handle non-finite values.
Results may differ from the reference program's by a relative error of at most 0.00013.
Values sent between devices are 32-bit elements; how exact they have to be, the bound alone decides.
No kernel may reach another device: no remote copies, remote signals or barrier semaphores. Data moves between devices by JAX's collectives and lax.ppermute only.
A program may use at most 64 MiB of HBM per device.

```python
import math
import jax
import jax.numpy as jnp

LEVELS = 16
NLON = 1440
NCLASS = 72
STEPS = 3
NLAT = 64
BANDS = 32


def draw_band_of_row(key, part):
    key = jax.random.fold_in(key, 5)
    owners = jax.random.permutation(key, BANDS).astype(jnp.int32)
    run_index = jnp.arange(NLAT, dtype=jnp.int32) // (NLAT // BANDS)
    return owners[run_index].astype(jnp.int32)


def set_ends(entries, rng, low, largest):
    longest = entries.shape.index(max(entries.shape))
    spots = []
    for shift in (0, 1):
        where = [jax.random.randint(jax.random.fold_in(rng, axis), (), 0, length) for axis, length in enumerate(entries.shape)]
        where[longest] = (where[longest] + shift) % entries.shape[longest]
        spots.append(tuple(where))
    return entries.at[spots[0]].set(low).at[spots[1]].set(largest)


def block_levels(key, dims, pieces, smallest, top_value):
    gain = 1.0
    for axis_at, shards_of in pieces:
        heights = jax.random.uniform(jax.random.fold_in(jax.random.fold_in(key, 6), axis_at), (shards_of,), jnp.float32, smallest / len(pieces), top_value / len(pieces))
        gain = gain * jnp.repeat(jnp.exp(heights), dims[axis_at] // shards_of).reshape((-1,) + (1,) * (len(dims) - 1 - axis_at))
    return gain


def noise(stream_key, shape, scale, bound, shards=(), kind=jnp.bfloat16):
    values = jax.random.normal(stream_key, shape, jnp.float32) * scale
    if len(shards) > 0:
        values = block_levels(stream_key, shape, shards, -0.22, 0.18) * values
    return jnp.clip(values, min=-bound, max=bound).astype(kind)


def setup_inputs(seed: int = 0, part: int = 0) -> dict:
    key_list = jax.random.split(jax.random.key(seed), 8)
    part_keys = jax.random.split(jax.random.fold_in(key_list[7], part), 8)
    return {
        "tracer": noise(part_keys[0], (LEVELS, NLAT, NLON), 1.0, 6.0, ((1, 16),), jnp.float32),
        "diffusivity": jnp.clip(jnp.exp(math.log(0.18) - 2.1972246 * jax.random.uniform(key_list[1], (NLAT, NLON), jnp.float32) ** block_levels(key_list[1], (NLAT, NLON), ((0, 16),), -0.2, 0.2)), 0.02, 0.18),
        "direction": noise(part_keys[2], (NLAT, NLON), 0.003, 0.015625, ((0, 16),), jnp.float32),
        "column_depth": set_ends(jax.random.randint(key_list[3], (NLAT, NLON), 0, LEVELS + 1), jax.random.fold_in(key_list[3], 1), 0, LEVELS).astype(jnp.int32),
        "density_class": set_ends(jax.random.randint(part_keys[4], (LEVELS, NLAT, NLON), 0, NCLASS), jax.random.fold_in(part_keys[4], 1), 0, NCLASS - 1).astype(jnp.int32),
        "band_of_row": draw_band_of_row(jax.random.fold_in(key_list[7], 71), part),
        "weights": jnp.clip(jnp.exp(jax.random.uniform(key_list[6], (BANDS, NCLASS), jnp.float32, math.log(0.02), math.log(0.2))), 0.02, 0.2),
    }


vertical_mix = 0.05


def lateral(tracer_field, mixing, wetness):
    east_mix = 0.5 * (mixing + jnp.roll(mixing, -1, axis=-1))
    east_flux = east_mix * wetness * jnp.roll(wetness, -1, axis=-1) * (jnp.roll(tracer_field, -1, axis=-1) - tracer_field)
    east_part = east_flux - jnp.roll(east_flux, 1, axis=-1)
    north_mix = 0.5 * (mixing[:-1] + mixing[1:])
    north_flux = north_mix * wetness[:, :-1] * wetness[:, 1:] * (tracer_field[:, 1:] - tracer_field[:, :-1])
    return east_part[:, 1:-1] + north_flux[:, 1:] - north_flux[:, :-1]


def columns(tracer_field, wetness):
    level_flux = vertical_mix * wetness[1:] * (tracer_field[1:] - tracer_field[:-1])
    zeros_top = jnp.zeros_like(level_flux[:1])
    flux_below = jnp.concatenate([level_flux, zeros_top], axis=0)
    flux_above = jnp.concatenate([zeros_top, level_flux], axis=0)
    return (flux_below - flux_above)[:, 1:-1]


def advance(tracer_field, mixing, wetness):
    return tracer_field[:, 1:-1] + lateral(tracer_field, mixing, wetness) + columns(tracer_field, wetness)


def sensitivity(base_field, adjoint_field, wetness):
    east_term = wetness * jnp.roll(wetness, -1, axis=-1) * (jnp.roll(base_field, -1, axis=-1) - base_field) * (jnp.roll(adjoint_field, -1, axis=-1) - adjoint_field)
    east_sum = jnp.sum(east_term[:, 1:-1], axis=0)
    north_term = wetness[:, :-1] * wetness[:, 1:] * (base_field[:, 1:] - base_field[:, :-1]) * (adjoint_field[:, 1:] - adjoint_field[:, :-1])
    north_sum = jnp.sum(north_term, axis=0)
    return -0.5 * (east_sum + jnp.roll(east_sum, 1, axis=-1) + north_sum[1:] + north_sum[:-1])


def border(values):
    return jnp.pad(values, [(0, 0)] * (values.ndim - 2) + [(1, 1), (0, 0)])


def reference(tracer, diffusivity, direction, column_depth, density_class, band_of_row, weights):
    wetness = (jnp.arange(LEVELS, dtype=jnp.int32)[:, None, None] < column_depth[None]).astype(jnp.float32)
    wet_pad = border(wetness)
    mix_pad = border(diffusivity)
    dir_pad = border(direction)
    base_field = tracer
    stored = []
    tangent = None
    for step_index in range(STEPS):
        base_ext = border(base_field)
        stored.append(base_ext)
        heading = lateral(base_ext, dir_pad, wet_pad)
        if step_index == 0:
            tangent = heading
        else:
            tangent = advance(border(tangent), mix_pad, wet_pad) + heading
        if step_index + 1 < STEPS:
            base_field = advance(base_ext, mix_pad, wet_pad)
    latitude = jnp.arange(NLAT, dtype=jnp.int32)[None, :, None]
    cell_bins = (latitude * NCLASS + density_class).astype(jnp.int32)
    row_sums = jax.ops.segment_sum((wetness * tangent).reshape(-1), cell_bins.reshape(-1), num_segments=NLAT * NCLASS).reshape(NLAT, NCLASS)
    binned = jax.ops.segment_sum(row_sums, band_of_row.astype(jnp.int32), num_segments=BANDS)
    weighted = weights * binned
    adjoint = wetness * weighted[band_of_row.astype(jnp.int32)].reshape(-1)[cell_bins]
    gradient = jnp.zeros((NLAT, NLON), jnp.float32)
    for step_index in reversed(range(STEPS)):
        adjoint_ext = border(adjoint)
        gradient = gradient + sensitivity(stored[step_index], adjoint_ext, wet_pad)
        if step_index > 0:
            adjoint = advance(adjoint_ext, mix_pad, wet_pad)
    return binned, gradient
```

```python
import functools

import jax
import jax.numpy as jnp
from jax import lax
from jax.experimental import pallas as pl
from jax.experimental.pallas import tpu as pltpu
from jax.sharding import PartitionSpec as P

STEPS = 3
vertical_mix = 0.05

LANES = 128
GHOST = 4
OWN = LANES - 2 * GHOST
HIGH_COUNT = 5
LOW_COUNT = 16
LOW_SHIFT = 4
VMEM_LIMIT = 50 * 1024 * 1024


def strip_of(row, j, lon_count):
    first = OWN * j - GHOST
    last = first + LANES
    if first < 0:
        return jnp.concatenate([row[:, first + lon_count :], row[:, :last]], axis=1)
    if last > lon_count:
        return jnp.concatenate([row[:, first:], row[:, : last - lon_count]], axis=1)
    return row[:, first:last]


def is_odd():
    return lax.rem(lax.axis_index("lat"), 2) == 1


def oriented(ref, t, odd):
    last = ref.shape[1] - 1
    return jnp.where(odd, ref[:, last - t, :], ref[:, t, :])


def pack_fields(tracer, mix, heading, depth, own, own_maps, near, far):
    levels, rows, lon_count = tracer.shape
    strips = lon_count // OWN
    odd = is_odd()
    for t in range(rows):
        field = oriented(tracer, t, odd)
        for j in range(strips):
            strip = strip_of(field, j, lon_count)
            own[j, t * levels : (t + 1) * levels, :] = strip
            if t < STEPS:
                at = (j * STEPS + STEPS - 1 - t) * levels
                far[at : at + levels, :] = strip
            if t > 0:
                at = (j * STEPS + rows - 1 - t) * levels
                near[at : at + levels, :] = strip
    base = strips * STEPS * levels
    for a, ref in enumerate((mix, heading, depth)):
        field = ref[...].astype(jnp.float32)
        flipped = jnp.concatenate([field[r : r + 1] for r in reversed(range(rows))], axis=0)
        up = jnp.where(odd, flipped, field)
        down = jnp.where(odd, field, flipped)
        for j in range(strips):
            own_maps[j, a * 4 : a * 4 + 4, :] = strip_of(up, j, lon_count)
            strip = strip_of(down, j, lon_count)
            at = base + (3 * j + a) * STEPS
            near[at : at + STEPS, :] = strip[:STEPS]
            far[at : at + STEPS, :] = strip[1:]
    own_maps[:, 12:, :] = jnp.zeros_like(own_maps[:, 12:, :])


def pack_classes(classes, own, near, far):
    levels, rows, lon_count = classes.shape
    strips = lon_count // OWN
    odd = is_odd()
    for t in range(rows):
        field = oriented(classes, t, odd)
        for j in range(strips):
            strip = strip_of(field, j, lon_count)
            own[j, t * levels : (t + 1) * levels, :] = strip
            if t < STEPS:
                at = (j * STEPS + STEPS - 1 - t) * levels
                far[at : at + levels, :] = strip
            if t > 0:
                at = (j * STEPS + rows - 1 - t) * levels
                near[at : at + levels, :] = strip


def east(x):
    return pltpu.roll(x, LANES - 1, 1)


def west(x):
    return pltpu.roll(x, 1, 1)


class Coefficients:
    def __init__(self, maps, work, levels, with_direction):
        self.level = lax.broadcasted_iota(jnp.int32, (levels, LANES), 0).astype(jnp.float32)
        self.levels = levels
        mix, heading, depth = maps[0:16, :], maps[16:32, :], maps[32:48, :]

        def north(x):
            return pltpu.roll(x, 15, 0)

        work[0:16, :] = jnp.minimum(depth, east(depth))
        work[16:32, :] = jnp.minimum(depth, north(depth))
        work[32:48, :] = 0.5 * (mix + east(mix))
        work[48:64, :] = 0.5 * (mix + north(mix))
        if with_direction:
            work[64:80, :] = 0.5 * (heading + east(heading))
            work[80:96, :] = 0.5 * (heading + north(heading))
        self.maps = maps
        self.work = work
        self.cache = {}

    def row(self, ref, block, t):
        at = 16 * block + t + STEPS
        return jnp.broadcast_to(ref[at : at + 1, :], (self.levels, LANES))

    def get(self, kind, t):
        if (kind, t) not in self.cache:
            zero = jnp.zeros((self.levels, LANES), jnp.float32)
            if kind == "wet":
                value = self.level < self.row(self.maps, 2, t)
            elif kind == "column":
                inside = self.level + 1.0 < self.row(self.maps, 2, t)
                value = jnp.where(inside, vertical_mix, zero)
            elif kind == "east_open":
                value = self.level < self.row(self.work, 0, t)
            elif kind == "north_open":
                value = self.level < self.row(self.work, 1, t)
            else:
                block, side = {
                    "east_mix": (2, "east_open"),
                    "north_mix": (3, "north_open"),
                    "east_dir": (4, "east_open"),
                    "north_dir": (5, "north_open"),
                }[kind]
                value = jnp.where(self.get(side, t), self.row(self.work, block, t), zero)
            self.cache[kind, t] = value
        return self.cache[kind, t]


def column(field, coefficient):
    levels = field.shape[0]
    flux = coefficient * (pltpu.roll(field, levels - 1, 0) - field)
    return flux - pltpu.roll(flux, 1, 0)


def gaps(field, rows):
    across = {t: east(field[t]) - field[t] for t in rows}
    along = {t: field[t + 1] - field[t] for t in range(rows[0] - 1, rows[-1] + 1)}
    return across, along


def spread(across, along, t):
    return (across[t] - west(across[t])) + (along[t] - along[t - 1])


def forward(
    weights, band_of_row, own, own_maps, near, far, classes,
    sums, maps, later, work, grams,
):
    strips, _, _ = own.shape
    levels = own.shape[1] // 4
    odd = is_odd()
    base = strips * STEPS * levels
    has_far = jnp.logical_and(lax.axis_index("lat") != 0, lax.axis_index("lat") != lax.axis_size("lat") - 1)
    keep = jnp.where(has_far, 1.0, 0.0)
    for j in range(strips):
        for a in range(3):
            at = base + (3 * j + a) * STEPS
            low = far[at : at + STEPS, :]
            if a == 2:
                low = low * keep
            high = near[at : at + STEPS, :]
            maps[j, 16 * a : 16 * a + 16, :] = jnp.concatenate(
                [low, own_maps[j, 4 * a : 4 * a + 4, :], high, high, high], axis=0
            )
    grams[...] = jnp.zeros_like(grams)
    lane = lax.broadcasted_iota(jnp.int32, (levels, LANES), 1)
    inner = jnp.logical_and(lane >= GHOST, lane < LANES - GHOST)

    def strip(j, carry):
        coef = Coefficients(maps.at[j], work, levels, True)
        field = {}
        for s in range(STEPS):
            at = pl.multiple_of((j * STEPS + s) * levels, levels)
            field[s - STEPS] = far[pl.ds(at, levels), :]
            field[4 + s] = near[pl.ds(at, levels), :]
        for t in range(4):
            field[t] = own[j, t * levels : (t + 1) * levels, :]
        tangent = None
        for n in range(STEPS):
            rows = list(range(n + 1 - STEPS, 4 + STEPS - n - 1))
            faces = [rows[0] - 1] + rows
            across, along = gaps(field, rows)
            push_e = {t: coef.get("east_dir", t) * across[t] for t in rows}
            push_n = {t: coef.get("north_dir", t) * along[t] for t in faces}
            if n > 0:
                t_across, t_along = gaps(tangent, rows)
                push_e = {t: push_e[t] + coef.get("east_mix", t) * t_across[t] for t in rows}
                push_n = {t: push_n[t] + coef.get("north_mix", t) * t_along[t] for t in faces}
            following = {}
            for t in rows:
                value = spread(push_e, push_n, t)
                if n > 0:
                    value = value + tangent[t] + column(tangent[t], coef.get("column", t))
                following[t] = value
            tangent = following
            if n + 1 < STEPS:
                flux_e = {t: coef.get("east_mix", t) * across[t] for t in rows}
                flux_n = {t: coef.get("north_mix", t) * along[t] for t in faces}
                field = {
                    t: field[t] + spread(flux_e, flux_n, t) + column(field[t], coef.get("column", t))
                    for t in rows
                }
                for t in range(-1, 5):
                    at = (n * 6 + t + 1) * levels
                    later[j, at : at + levels, :] = field[t]
        for pair in range(2):
            tops, bottoms, ones = [], [], []
            for t in (2 * pair, 2 * pair + 1):
                chosen = jnp.logical_and(inner, coef.get("wet", t))
                value = jnp.where(chosen, tangent[t], 0.0)
                top = value.astype(jnp.bfloat16)
                bottom = (value - top.astype(jnp.float32)).astype(jnp.bfloat16)
                label = classes[j, t * levels : (t + 1) * levels, :]
                high = (label >> LOW_SHIFT).astype(jnp.float32).astype(jnp.bfloat16)
                low = (label & (LOW_COUNT - 1)).astype(jnp.float32).astype(jnp.bfloat16)
                none = jnp.zeros((levels, LANES), jnp.bfloat16)
                one = jnp.ones((levels, LANES), jnp.bfloat16)
                picks = [high == jnp.bfloat16(h) for h in range(HIGH_COUNT)]
                tops.append(
                    jnp.concatenate(
                        [jnp.where(p, top, none) for p in picks] + [jnp.where(p, bottom, none) for p in picks],
                        axis=0,
                    )
                )
                ones.append(
                    jnp.concatenate(
                        [jnp.where(low == jnp.bfloat16(l), one, none) for l in range(LOW_COUNT)], axis=0
                    )
                )
            grams[pair] += lax.dot_general(
                jnp.concatenate(tops, axis=1),
                jnp.concatenate(ones, axis=1),
                (((1,), (1,)), ((), ())),
                preferred_element_type=jnp.float32,
            )
        return carry

    lax.fori_loop(0, strips, strip, 0)

    width = LOW_COUNT * levels
    own_level = lax.broadcasted_iota(jnp.int32, (levels, width), 0)
    other_level = lax.broadcasted_iota(jnp.int32, (levels, width), 1) % levels
    diagonal = own_level == other_level
    label = lax.broadcasted_iota(jnp.int32, (8, LANES), 1)
    here = lax.broadcasted_iota(jnp.int32, (8, LANES), 0)
    table_rows = []
    for pair in range(2):
        sheets = []
        for h in range(HIGH_COUNT):
            both = (
                grams[pair, h * levels : (h + 1) * levels, :]
                + grams[pair, (HIGH_COUNT + h) * levels : (HIGH_COUNT + h + 1) * levels, :]
            )
            sheets.append(jnp.sum(jnp.where(diagonal, both, 0.0), axis=0, keepdims=True))
        sheets.append(jnp.zeros((8 - HIGH_COUNT, width), jnp.float32))
        sheet = jnp.concatenate(sheets, axis=0)
        shift = 1
        while shift < levels:
            sheet = sheet + pltpu.roll(sheet, width - shift, 1)
            shift *= 2
        low = label % LOW_COUNT
        half = LANES // levels
        spot = (low % half) * levels
        left = jnp.take_along_axis(sheet[:, :LANES], spot, axis=1)
        right = jnp.take_along_axis(sheet[:, LANES:], spot, axis=1)
        picked = jnp.where(low < half, left, right)
        picked = jnp.where(here == label // LOW_COUNT, picked, 0.0)
        table_rows.append(jnp.sum(picked, axis=0, keepdims=True))
    band_count, class_count = weights.shape
    label = lax.broadcasted_iota(jnp.int32, (1, LANES), 1)
    weighted_rows, total_rows = [], []
    for pair in range(2):
        row = jnp.where(odd, 3 - 2 * pair, 2 * pair)
        band = band_of_row[row]
        scale = weights[pl.ds(band, 1), :]
        scale = jnp.concatenate([scale, jnp.zeros((1, LANES - class_count), jnp.float32)], axis=1)
        weighted_rows.append(scale * table_rows[pair])
        total_rows.append(jnp.where(label == LANES - 1, band.astype(jnp.float32), table_rows[pair]))
    sums[...] = jnp.concatenate(
        total_rows + weighted_rows + [jnp.zeros((4, LANES), jnp.float32)], axis=0
    )


def adjoint_part(
    own, near, far, maps, later, own_classes, near_classes, far_classes,
    own_sums, near_sums, far_sums, gradient, work, strips_out,
):
    strips = own.shape[0]
    levels = own.shape[1] // 4
    rows, lon_count = gradient.shape
    odd = is_odd()

    def strip(j, carry):
        coef = Coefficients(maps.at[j], work, levels, False)
        fields = [{t: own[j, t * levels : (t + 1) * levels, :] for t in range(4)}]
        at = pl.multiple_of((j * STEPS + STEPS - 1) * levels, levels)
        fields[0][-1] = far[pl.ds(at, levels), :]
        at = pl.multiple_of(j * STEPS * levels, levels)
        fields[0][4] = near[pl.ds(at, levels), :]
        for n in range(STEPS - 1):
            fields.append(
                {t: later[j, (n * 6 + t + 1) * levels : (n * 6 + t + 2) * levels, :] for t in range(-1, 5)}
            )
        adjoint = {}
        for t in range(-STEPS, 4 + STEPS):
            if t < 0:
                at = pl.multiple_of((j * STEPS + t + STEPS) * levels, levels)
                label = far_classes[pl.ds(at, levels), :]
                source, row = far_sums, 2 + (-1 - t) // 2
            elif t < 4:
                label = own_classes[j, t * levels : (t + 1) * levels, :]
                source, row = own_sums, 2 + t // 2
            else:
                at = pl.multiple_of((j * STEPS + t - 4) * levels, levels)
                label = near_classes[pl.ds(at, levels), :]
                source, row = near_sums, 2 + (7 - t) // 2
            table = jnp.broadcast_to(source[row : row + 1, :], (8, LANES))
            value = jnp.concatenate(
                [jnp.take_along_axis(table, label[k : k + 8, :], axis=1) for k in range(0, levels, 8)], axis=0
            )
            adjoint[t] = jnp.where(coef.get("wet", t), value, 0.0)
        east_total = {t: jnp.zeros((levels, LANES), jnp.float32) for t in range(4)}
        north_total = {t: jnp.zeros((levels, LANES), jnp.float32) for t in range(-1, 4)}
        for n in reversed(range(STEPS)):
            margin = n
            rows_out = list(range(-margin, 4 + margin))
            across, along = gaps(adjoint, rows_out)
            f_across, f_along = gaps(fields[n], list(range(4)))
            for t in range(4):
                east_total[t] = east_total[t] + f_across[t] * across[t]
            for t in range(-1, 4):
                north_total[t] = north_total[t] + f_along[t] * along[t]
            if n > 0:
                faces = [rows_out[0] - 1] + rows_out
                flux_e = {t: coef.get("east_mix", t) * across[t] for t in rows_out}
                flux_n = {t: coef.get("north_mix", t) * along[t] for t in faces}
                adjoint = {
                    t: adjoint[t] + spread(flux_e, flux_n, t) + column(adjoint[t], coef.get("column", t))
                    for t in rows_out
                }
        north_total = {t: jnp.where(coef.get("north_open", t), north_total[t], 0.0) for t in north_total}
        out = []
        for t in range(4):
            part = jnp.where(coef.get("east_open", t), east_total[t], 0.0)
            part = part + west(part) + north_total[t] + north_total[t - 1]
            out.append(-0.5 * jnp.sum(part, axis=0, keepdims=True))
        up = jnp.concatenate(out, axis=0)
        down = jnp.concatenate(out[::-1], axis=0)
        strips_out[j, 0:4, :] = jnp.where(odd, down, up)
        return carry

    lax.fori_loop(0, strips, strip, 0)
    gradient[...] = jnp.concatenate(
        [strips_out[j, 0:4, GHOST : LANES - GHOST] for j in range(strips)], axis=1
    )


def near_pairs(count):
    return [(i, i ^ 1) for i in range(count)]


def far_pairs(members, count):
    pairs = []
    for m in range(members):
        for i in range(1, count - 1, 2):
            pairs += [(m * count + i, m * count + i + 1), (m * count + i + 1, m * count + i)]
        for i in (0, count - 1):
            pairs.append((m * count + i, (m ^ 1) * count + i))
    return pairs


def vmem(count):
    return [pl.BlockSpec(memory_space=pltpu.VMEM)] * count


def body(tracer, diffusivity, direction, column_depth, density_class, band_of_row, weights):
    levels, rows, lon_count = tracer.shape
    strips = lon_count // OWN
    count = lax.axis_size("lat")
    members = lax.axis_size("members")
    params = pltpu.CompilerParams(vmem_limit_bytes=VMEM_LIMIT)
    f32, i32 = jnp.float32, jnp.int32
    halo = strips * STEPS * levels
    payload = halo + strips * 9

    def to_near(x):
        return lax.ppermute(x, "lat", near_pairs(count))

    def to_far(x):
        return lax.ppermute(x, ("members", "lat"), far_pairs(members, count))

    own, own_maps, near_out, far_out = pl.pallas_call(
        pack_fields,
        name="pack_fields",
        out_shape=(
            jax.ShapeDtypeStruct((strips, rows * levels, LANES), f32),
            jax.ShapeDtypeStruct((strips, 16, LANES), f32),
            jax.ShapeDtypeStruct((payload, LANES), f32),
            jax.ShapeDtypeStruct((payload, LANES), f32),
        ),
        in_specs=vmem(4),
        out_specs=tuple(vmem(4)),
        compiler_params=params,
    )(tracer, diffusivity, direction, column_depth)
    far = to_far(far_out)
    near = to_near(near_out)

    own_classes, near_classes_out, far_classes_out = pl.pallas_call(
        pack_classes,
        name="pack_classes",
        out_shape=(
            jax.ShapeDtypeStruct((strips, rows * levels, LANES), i32),
            jax.ShapeDtypeStruct((halo, LANES), i32),
            jax.ShapeDtypeStruct((halo, LANES), i32),
        ),
        in_specs=vmem(1),
        out_specs=tuple(vmem(3)),
        compiler_params=params,
    )(density_class)
    near_classes_out, far_classes_out, near, far = lax.optimization_barrier(
        (near_classes_out, far_classes_out, near, far)
    )
    far_classes = to_far(far_classes_out)
    near_classes = to_near(near_classes_out)

    sums, maps, later = pl.pallas_call(
        forward,
        name="forward",
        out_shape=(
            jax.ShapeDtypeStruct((8, LANES), f32),
            jax.ShapeDtypeStruct((strips, 48, LANES), f32),
            jax.ShapeDtypeStruct((strips, 12 * levels, LANES), f32),
        ),
        in_specs=vmem(1) + [pl.BlockSpec(memory_space=pltpu.SMEM)] + vmem(5),
        out_specs=tuple(vmem(3)),
        scratch_shapes=[
            pltpu.VMEM((96, LANES), f32),
            pltpu.VMEM((2, 2 * HIGH_COUNT * levels, LOW_COUNT * levels), f32),
        ],
        compiler_params=params,
    )(weights, band_of_row, own, own_maps, near, far, own_classes)

    near_sums = to_near(sums)
    far_sums = to_far(sums)
    gathered = jnp.concatenate([sums, near_sums], axis=0)

    gradient = pl.pallas_call(
        adjoint_part,
        name="adjoint_part",
        out_shape=jax.ShapeDtypeStruct((rows, lon_count), f32),
        in_specs=vmem(11),
        out_specs=pl.BlockSpec(memory_space=pltpu.VMEM),
        scratch_shapes=[
            pltpu.VMEM((96, LANES), f32),
            pltpu.VMEM((strips, 8, LANES), f32),
        ],
        compiler_params=params,
    )(own, near, far, maps, later, own_classes, near_classes, far_classes, sums, near_sums, far_sums)

    step = 2
    while step < count:
        other = lax.ppermute(gathered, "lat", [(i, i ^ step) for i in range(count)])
        gathered = jnp.concatenate([gathered, other], axis=0)
        step *= 2
    band_own = weights.shape[0] // count
    finished = gathered.reshape(count, 8, LANES)[:, :2]
    wanted = lax.axis_index("lat") * band_own + jnp.arange(band_own)
    hits = finished[None, :, :, LANES - 1] == wanted[:, None, None].astype(f32)
    binned = jnp.sum(
        jnp.where(hits[..., None], finished[None, :, :, : weights.shape[1]], 0.0), axis=(1, 2)
    )
    return binned, gradient


def solution(mesh):
    placed = (
        P(None, ("members", "lat"), None),
        P("lat", None),
        P(("members", "lat"), None),
        P("lat", None),
        P(None, ("members", "lat"), None),
        P("lat"),
        P(),
    )
    return jax.shard_map(
        body,
        mesh=mesh,
        in_specs=placed,
        out_specs=(P(("members", "lat"), None), P(("members", "lat"), None)),
        check_vma=False,
    )
```

```python
import functools

import jax
import jax.numpy as jnp
from jax import lax
from jax.experimental import pallas as pl
from jax.experimental.pallas import tpu as pltpu
from jax.sharding import PartitionSpec as P

STEPS = 3
vertical_mix = 0.05

LANES = 128
GHOST = 4
OWN = LANES - 2 * GHOST
HIGH_COUNT = 5
LOW_COUNT = 16
LOW_SHIFT = 4
GROUP = 3
VMEM_LIMIT = 50 * 1024 * 1024


def strip_of(row, j, lon_count):
    first = OWN * j - GHOST
    last = first + LANES
    if first < 0:
        return jnp.concatenate([row[:, first + lon_count :], row[:, :last]], axis=1)
    if last > lon_count:
        return jnp.concatenate([row[:, first:], row[:, : last - lon_count]], axis=1)
    return row[:, first:last]


def is_odd():
    return lax.rem(lax.axis_index("lat"), 2) == 1


def oriented(ref, t, odd):
    last = ref.shape[1] - 1
    order = level_order(ref.shape[0])
    up = jnp.concatenate([ref[k, t : t + 1, :] for k in order], axis=0)
    down = jnp.concatenate([ref[k, last - t : last - t + 1, :] for k in order], axis=0)
    return jnp.where(odd, down, up)


def pack_fields(tracer, mix, heading, depth, own, own_maps, near, far):
    levels, rows, lon_count = tracer.shape
    strips = lon_count // OWN
    odd = is_odd()
    for t in range(rows):
        field = oriented(tracer, t, odd)
        for j in range(strips):
            strip = strip_of(field, j, lon_count)
            own[j, t * levels : (t + 1) * levels, :] = strip
            if t < STEPS:
                at = (j * STEPS + STEPS - 1 - t) * levels
                far[at : at + levels, :] = strip
            if t > 0:
                at = (j * STEPS + rows - 1 - t) * levels
                near[at : at + levels, :] = strip
    base = strips * STEPS * levels
    for a, ref in enumerate((mix, heading, depth)):
        field = ref[...].astype(jnp.float32)
        flipped = jnp.concatenate([field[r : r + 1] for r in reversed(range(rows))], axis=0)
        up = jnp.where(odd, flipped, field)
        down = jnp.where(odd, field, flipped)
        for j in range(strips):
            own_maps[j, a * 4 : a * 4 + 4, :] = strip_of(up, j, lon_count)
            strip = strip_of(down, j, lon_count)
            at = base + (3 * j + a) * STEPS
            near[at : at + STEPS, :] = strip[:STEPS]
            far[at : at + STEPS, :] = strip[1:]
    own_maps[:, 12:, :] = jnp.zeros_like(own_maps[:, 12:, :])


def pack_classes(classes, weights, band_of_row, own, near, far, scales):
    levels, rows, lon_count = classes.shape
    strips = lon_count // OWN
    odd = is_odd()
    for t in range(rows):
        field = oriented(classes, t, odd)
        for j in range(strips):
            strip = strip_of(field, j, lon_count)
            own[j, t * levels : (t + 1) * levels, :] = strip
            if t < STEPS:
                at = (j * STEPS + STEPS - 1 - t) * levels
                far[at : at + levels, :] = strip
            if t > 0:
                at = (j * STEPS + rows - 1 - t) * levels
                near[at : at + levels, :] = strip
    class_count = weights.shape[1]
    label = lax.broadcasted_iota(jnp.int32, (1, LANES), 1)
    scale_rows, band_rows = [], []
    for pair in range(2):
        band = band_of_row[jnp.where(odd, 3 - 2 * pair, 2 * pair)]
        scale = weights[pl.ds(band, 1), :]
        scale_rows.append(jnp.concatenate([scale, jnp.zeros((1, LANES - class_count), jnp.float32)], axis=1))
        band_rows.append(jnp.where(label == LANES - 1, band.astype(jnp.float32), 0.0))
    scales[...] = jnp.concatenate(
        scale_rows + band_rows + [jnp.zeros((4, LANES), jnp.float32)], axis=0
    )


def east(x):
    return pltpu.roll(x, LANES - 1, 1)


def west(x):
    return pltpu.roll(x, 1, 1)


MAP_FIELDS = 10


def level_order(levels):
    half = levels // 2
    return [2 * (i % half) + i // half for i in range(levels)]


class Coefficients:
    blocks = {
        "wet": 0, "east_open": 1, "west_open": 2, "north_open": 3,
        "east_mix": 4, "west_mix": 5, "north_mix": 6,
        "east_dir": 7, "west_dir": 8, "north_dir": 9,
    }

    def __init__(self, maps, j, levels):
        order = lax.broadcasted_iota(jnp.int32, (levels, LANES), 0)
        half = levels // 2
        self.level = (2 * (order & (half - 1)) + jnp.where(order < half, 0, 1)).astype(jnp.float32)
        self.levels = levels
        self.maps = maps
        self.j = j
        self.cache = {}

    def row(self, kind, t):
        at = 16 * self.blocks[kind] + t + STEPS
        return jnp.broadcast_to(self.maps[self.j, at : at + 1, :], (self.levels, LANES))

    def get(self, kind, t):
        if (kind, t) not in self.cache:
            side, _, what = kind.partition("_")
            if kind == "column":
                value = jnp.where(self.level + 1.0 < self.row("wet", t), vertical_mix, 0.0)
            elif kind == "wet" or what == "open":
                value = self.level < self.row(kind, t)
            else:
                value = jnp.where(self.get(side + "_open", t), self.row(kind, t), 0.0)
            self.cache[kind, t] = value
        return self.cache[kind, t]


def column(field, coefficient):
    half = field.shape[0] // 2
    even, odd = field[:half], field[half:]
    after_even = coefficient[:half] * (odd - even)
    after_odd = coefficient[half:] * (pltpu.roll(even, half - 1, 0) - odd)
    return jnp.concatenate([after_even - pltpu.roll(after_odd, 1, 0), after_odd - after_even], axis=0)


def gaps(field, rows):
    to_east = {t: east(field[t]) - field[t] for t in rows}
    to_west = {t: west(field[t]) - field[t] for t in rows}
    to_north = {t: field[t + 1] - field[t] for t in range(rows[0] - 1, rows[-1] + 1)}
    return to_east, to_west, to_north


def spread(coef, kind, steps, rows):
    to_east, to_west, to_north = steps
    flux = {t: coef.get("north_" + kind, t) * to_north[t] for t in range(rows[0] - 1, rows[-1] + 1)}
    return {
        t: coef.get("east_" + kind, t) * to_east[t]
        + coef.get("west_" + kind, t) * to_west[t]
        + (flux[t] - flux[t - 1])
        for t in rows
    }


def advance(coef, field, steps, rows):
    moved = spread(coef, "mix", steps, rows)
    return {t: field[t] + moved[t] + column(field[t], coef.get("column", t)) for t in rows}


def face_maps(own_maps, near, far, maps, base):
    strips = own_maps.shape[0]
    count, edge = lax.axis_size("lat"), lax.axis_index("lat")
    keep = jnp.where(jnp.logical_and(edge != 0, edge != count - 1), 1.0, 0.0)

    def north(x):
        return pltpu.roll(x, 15, 0)

    for j in range(strips):
        whole = []
        for a in range(3):
            at = base + (3 * j + a) * STEPS
            low = far[at : at + STEPS, :]
            if a == 2:
                low = low * keep
            high = near[at : at + STEPS, :]
            whole.append(jnp.concatenate([low, own_maps[j, 4 * a : 4 * a + 4, :], high, high, high], axis=0))
        mix, heading, depth = whole
        blocks = [depth] + [jnp.minimum(depth, f(depth)) for f in (east, west, north)]
        blocks += [0.5 * (x + f(x)) for x in (mix, heading) for f in (east, west, north)]
        for i, block in enumerate(blocks):
            maps[j, 16 * i : 16 * i + 16, :] = block


def class_hits(value, label, levels):
    top = value.astype(jnp.bfloat16)
    bottom = (value - top.astype(jnp.float32)).astype(jnp.bfloat16)
    high = (label >> LOW_SHIFT).astype(jnp.float32).astype(jnp.bfloat16)
    low = (label & (LOW_COUNT - 1)).astype(jnp.float32).astype(jnp.bfloat16)
    none = jnp.zeros((levels, LANES), jnp.bfloat16)
    one = jnp.ones((levels, LANES), jnp.bfloat16)
    picks = [high == jnp.bfloat16(h) for h in range(HIGH_COUNT)]
    left = [jnp.where(p, part, none) for part in (top, bottom) for p in picks]
    right = [jnp.where(low == jnp.bfloat16(l), one, none) for l in range(LOW_COUNT)]
    return jnp.concatenate(left, axis=0), jnp.concatenate(right, axis=0)


def forward(scales, own, own_maps, near, far, classes, sums, maps, later, grams):
    strips, _, _ = own.shape
    levels = own.shape[1] // 4
    face_maps(own_maps, near, far, maps, strips * STEPS * levels)
    grams[...] = jnp.zeros_like(grams)
    lane = lax.broadcasted_iota(jnp.int32, (levels, LANES), 1)
    inner = jnp.logical_and(lane >= GHOST, lane < LANES - GHOST)

    def some_strips(i, carry):
        group = [i * GROUP + u for u in range(GROUP)]
        coefs = [Coefficients(maps, j, levels) for j in group]
        fields, tangents = [], [None] * GROUP
        for j in group:
            field = {}
            for s in range(STEPS):
                at = pl.multiple_of((j * STEPS + s) * levels, levels)
                field[s - STEPS] = far[pl.ds(at, levels), :]
                field[4 + s] = near[pl.ds(at, levels), :]
            for t in range(4):
                field[t] = own[j, t * levels : (t + 1) * levels, :]
            fields.append(field)
        for n in range(STEPS):
            rows = list(range(n + 1 - STEPS, 4 + STEPS - n - 1))
            for u, j in enumerate(group):
                steps = gaps(fields[u], rows)
                pushed = spread(coefs[u], "dir", steps, rows)
                if n > 0:
                    carried = advance(coefs[u], tangents[u], gaps(tangents[u], rows), rows)
                    pushed = {t: pushed[t] + carried[t] for t in rows}
                tangents[u] = pushed
                if n + 1 < STEPS:
                    fields[u] = advance(coefs[u], fields[u], steps, rows)
                    for t in range(-1, 5):
                        at = (n * 6 + t + 1) * levels
                        later[j, at : at + levels, :] = fields[u][t]
        for pair in range(2):
            lefts, rights = [], []
            for u, j in enumerate(group):
                for t in (2 * pair, 2 * pair + 1):
                    chosen = jnp.logical_and(inner, coefs[u].get("wet", t))
                    value = jnp.where(chosen, tangents[u][t], 0.0)
                    left, right = class_hits(value, classes[j, t * levels : (t + 1) * levels, :], levels)
                    lefts.append(left)
                    rights.append(right)
            grams[pair] += lax.dot_general(
                jnp.concatenate(lefts, axis=1),
                jnp.concatenate(rights, axis=1),
                (((1,), (1,)), ((), ())),
                preferred_element_type=jnp.float32,
            )
        return carry

    lax.fori_loop(0, strips // GROUP, some_strips, 0)

    width = LOW_COUNT * levels
    own_level = lax.broadcasted_iota(jnp.int32, (levels, width), 0)
    other_level = lax.broadcasted_iota(jnp.int32, (levels, width), 1) & (levels - 1)
    diagonal = own_level == other_level
    sheets = []
    for pair in range(2):
        for h in range(HIGH_COUNT):
            both = (
                grams[pair, h * levels : (h + 1) * levels, :]
                + grams[pair, (HIGH_COUNT + h) * levels : (HIGH_COUNT + h + 1) * levels, :]
            )
            sheets.append(jnp.sum(jnp.where(diagonal, both, 0.0), axis=0, keepdims=True))
        sheets.append(jnp.zeros((8 - HIGH_COUNT, width), jnp.float32))
    rest = jnp.concatenate(sheets, axis=0)
    parts = []
    for _ in range(3):
        part = rest.astype(jnp.bfloat16)
        rest = rest - part.astype(jnp.float32)
        parts.append(part)
    at_low = lax.broadcasted_iota(jnp.int32, (width, LANES), 0) >> (levels.bit_length() - 1)
    of_low = lax.broadcasted_iota(jnp.int32, (width, LANES), 1) & (LOW_COUNT - 1)
    gather = jnp.where(at_low == of_low, 1.0, 0.0).astype(jnp.bfloat16)
    added = jnp.dot(jnp.concatenate(parts, axis=0), gather, preferred_element_type=jnp.float32)
    added = (added[32:48] + added[16:32]) + added[0:16]
    here = lax.broadcasted_iota(jnp.int32, (8, LANES), 0)
    label = lax.broadcasted_iota(jnp.int32, (8, LANES), 1)
    totals = [
        jnp.sum(
            jnp.where(here == (label >> LOW_SHIFT), added[8 * p : 8 * p + 8], 0.0), axis=0, keepdims=True
        )
        for p in range(2)
    ]
    finish_sums(scales, totals, sums)


def finish_sums(scales, totals, sums):
    weighted = [scales[p : p + 1, :] * totals[p] for p in range(2)]
    sums[...] = jnp.concatenate(
        [totals[p] + scales[2 + p : 3 + p, :] for p in range(2)]
        + weighted
        + [jnp.zeros((4, LANES), jnp.float32)],
        axis=0,
    )


def adjoint_part(
    own, near, far, maps, later, own_classes, near_classes, far_classes,
    own_sums, near_sums, far_sums, gradient, strips_out,
):
    strips = own.shape[0]
    levels = own.shape[1] // 4
    rows, lon_count = gradient.shape
    odd = is_odd()

    def some_strips(i, carry):
        group = [i * GROUP + u for u in range(GROUP)]
        coefs = [Coefficients(maps, j, levels) for j in group]
        fields, adjoints = [], []
        for u, j in enumerate(group):
            field = [{t: own[j, t * levels : (t + 1) * levels, :] for t in range(4)}]
            at = pl.multiple_of((j * STEPS + STEPS - 1) * levels, levels)
            field[0][-1] = far[pl.ds(at, levels), :]
            at = pl.multiple_of(j * STEPS * levels, levels)
            field[0][4] = near[pl.ds(at, levels), :]
            for n in range(STEPS - 1):
                field.append(
                    {t: later[j, (n * 6 + t + 1) * levels : (n * 6 + t + 2) * levels, :] for t in range(-1, 5)}
                )
            fields.append(field)
            adjoint = {}
            for t in range(-STEPS, 4 + STEPS):
                if t < 0:
                    at = pl.multiple_of((j * STEPS + t + STEPS) * levels, levels)
                    label = far_classes[pl.ds(at, levels), :]
                    source, row = far_sums, 2 + (-1 - t) // 2
                elif t < 4:
                    label = own_classes[j, t * levels : (t + 1) * levels, :]
                    source, row = own_sums, 2 + t // 2
                else:
                    at = pl.multiple_of((j * STEPS + t - 4) * levels, levels)
                    label = near_classes[pl.ds(at, levels), :]
                    source, row = near_sums, 2 + (7 - t) // 2
                table = jnp.broadcast_to(source[row : row + 1, :], (8, LANES))
                value = jnp.concatenate(
                    [jnp.take_along_axis(table, label[k : k + 8, :], axis=1) for k in range(0, levels, 8)],
                    axis=0,
                )
                adjoint[t] = jnp.where(coefs[u].get("wet", t), value, 0.0)
            adjoints.append(adjoint)
        east_total = [{t: 0.0 for t in range(4)} for _ in group]
        north_total = [{t: 0.0 for t in range(-1, 4)} for _ in group]
        for n in reversed(range(STEPS)):
            rows_out = list(range(-n, 4 + n))
            for u, j in enumerate(group):
                steps = gaps(adjoints[u], rows_out)
                field = fields[u][n]
                for t in range(4):
                    gap = east(field[t]) - field[t]
                    east_total[u][t] = east_total[u][t] + gap * steps[0][t]
                for t in range(-1, 4):
                    gap = field[t + 1] - field[t]
                    north_total[u][t] = north_total[u][t] + gap * steps[2][t]
                if n > 0:
                    adjoints[u] = advance(coefs[u], adjoints[u], steps, rows_out)
        for u, j in enumerate(group):
            north_part = {
                t: jnp.where(coefs[u].get("north_open", t), north_total[u][t], 0.0) for t in range(-1, 4)
            }
            out = []
            for t in range(4):
                part = jnp.where(coefs[u].get("east_open", t), east_total[u][t], 0.0)
                out.append(jnp.sum(part, axis=0, keepdims=True))
            part = jnp.concatenate(out, axis=0)
            part = part + west(part)
            north_part = [
                jnp.sum(north_part[t] + north_part[t - 1], axis=0, keepdims=True) for t in range(4)
            ]
            strips_out[j, 0:4, :] = -0.5 * (part + jnp.concatenate(north_part, axis=0))
        return carry

    lax.fori_loop(0, strips // GROUP, some_strips, 0)
    up = jnp.concatenate([strips_out[j, 0:4, GHOST : LANES - GHOST] for j in range(strips)], axis=1)
    down = jnp.concatenate([up[t : t + 1] for t in reversed(range(4))], axis=0)
    gradient[...] = jnp.where(odd, down, up)


def near_pairs(count):
    return [(i, i ^ 1) for i in range(count)]


def far_pairs(members, count):
    pairs = []
    for m in range(members):
        for i in range(1, count - 1, 2):
            pairs += [(m * count + i, m * count + i + 1), (m * count + i + 1, m * count + i)]
        for i in (0, count - 1):
            pairs.append((m * count + i, (m ^ 1) * count + i))
    return pairs


def vmem(count):
    return [pl.BlockSpec(memory_space=pltpu.VMEM)] * count


def body(tracer, diffusivity, direction, column_depth, density_class, band_of_row, weights):
    levels, rows, lon_count = tracer.shape
    strips = lon_count // OWN
    count = lax.axis_size("lat")
    members = lax.axis_size("members")
    params = pltpu.CompilerParams(vmem_limit_bytes=VMEM_LIMIT)
    f32, i32 = jnp.float32, jnp.int32
    halo = strips * STEPS * levels
    payload = halo + strips * 9

    def to_near(x):
        return lax.ppermute(x, "lat", near_pairs(count))

    def to_far(x):
        return lax.ppermute(x, ("members", "lat"), far_pairs(members, count))

    own, own_maps, near_out, far_out = pl.pallas_call(
        pack_fields,
        name="pack_fields",
        out_shape=(
            jax.ShapeDtypeStruct((strips, rows * levels, LANES), f32),
            jax.ShapeDtypeStruct((strips, 16, LANES), f32),
            jax.ShapeDtypeStruct((payload, LANES), f32),
            jax.ShapeDtypeStruct((payload, LANES), f32),
        ),
        in_specs=vmem(4),
        out_specs=tuple(vmem(4)),
        compiler_params=params,
    )(tracer, diffusivity, direction, column_depth)
    far = to_far(far_out)
    near = to_near(near_out)

    own_classes, near_classes_out, far_classes_out, scales = pl.pallas_call(
        pack_classes,
        name="pack_classes",
        out_shape=(
            jax.ShapeDtypeStruct((strips, rows * levels, LANES), i32),
            jax.ShapeDtypeStruct((halo, LANES), i32),
            jax.ShapeDtypeStruct((halo, LANES), i32),
            jax.ShapeDtypeStruct((8, LANES), f32),
        ),
        in_specs=vmem(2) + [pl.BlockSpec(memory_space=pltpu.SMEM)],
        out_specs=tuple(vmem(4)),
        compiler_params=params,
    )(density_class, weights, band_of_row)
    near_classes_out, far_classes_out, near, far = lax.optimization_barrier(
        (near_classes_out, far_classes_out, near, far)
    )
    far_classes = to_far(far_classes_out)
    near_classes = to_near(near_classes_out)

    sums, maps, later = pl.pallas_call(
        forward,
        name="forward",
        out_shape=(
            jax.ShapeDtypeStruct((8, LANES), f32),
            jax.ShapeDtypeStruct((strips, 16 * MAP_FIELDS, LANES), f32),
            jax.ShapeDtypeStruct((strips, 12 * levels, LANES), f32),
        ),
        in_specs=vmem(6),
        out_specs=tuple(vmem(3)),
        scratch_shapes=[
            pltpu.VMEM((2, 2 * HIGH_COUNT * levels, LOW_COUNT * levels), f32),
        ],
        compiler_params=params,
    )(scales, own, own_maps, near, far, own_classes)

    near_sums = to_near(sums)
    far_sums = to_far(sums)
    gathered = jnp.concatenate([sums, near_sums], axis=0)

    gradient = pl.pallas_call(
        adjoint_part,
        name="adjoint_part",
        out_shape=jax.ShapeDtypeStruct((rows, lon_count), f32),
        in_specs=vmem(11),
        out_specs=pl.BlockSpec(memory_space=pltpu.VMEM),
        scratch_shapes=[pltpu.VMEM((strips, 8, LANES), f32)],
        compiler_params=params,
    )(own, near, far, maps, later, own_classes, near_classes, far_classes, sums, near_sums, far_sums)

    step = 2
    while step < count:
        other = lax.ppermute(gathered, "lat", [(i, i ^ step) for i in range(count)])
        gathered = jnp.concatenate([gathered, other], axis=0)
        step *= 2
    band_own = weights.shape[0] // count
    finished = gathered.reshape(count, 8, LANES)[:, :2]
    wanted = lax.axis_index("lat") * band_own + jnp.arange(band_own)
    hits = finished[None, :, :, LANES - 1] == wanted[:, None, None].astype(f32)
    binned = jnp.sum(
        jnp.where(hits[..., None], finished[None, :, :, : weights.shape[1]], 0.0), axis=(1, 2)
    )
    return binned, gradient


def solution(mesh):
    placed = (
        P(None, ("members", "lat"), None),
        P("lat", None),
        P(("members", "lat"), None),
        P("lat", None),
        P(None, ("members", "lat"), None),
        P("lat"),
        P(),
    )
    return jax.shard_map(
        body,
        mesh=mesh,
        in_specs=placed,
        out_specs=(P(("members", "lat"), None), P(("members", "lat"), None)),
        check_vma=False,
    )
```

```python
import functools

import jax
import jax.numpy as jnp
from jax import lax
from jax.experimental import pallas as pl
from jax.experimental.pallas import tpu as pltpu
from jax.sharding import PartitionSpec as P

STEPS = 3
vertical_mix = 0.05

LANES = 128
GHOST = 4
OWN = LANES - 2 * GHOST
HIGH_COUNT = 5
LOW_COUNT = 16
LOW_SHIFT = 4
GROUP = 3
VMEM_LIMIT = 16 * 1024 * 1024


def strip_of(row, j, lon_count):
    first = OWN * j - GHOST
    last = first + LANES
    if first < 0:
        return jnp.concatenate([row[:, first + lon_count :], row[:, :last]], axis=1)
    if last > lon_count:
        return jnp.concatenate([row[:, first:], row[:, : last - lon_count]], axis=1)
    return row[:, first:last]


def is_odd():
    return lax.rem(lax.axis_index("lat"), 2) == 1


def oriented(ref, t, odd):
    last = ref.shape[1] - 1
    order = level_order(ref.shape[0])
    up = jnp.concatenate([ref[k, t : t + 1, :] for k in order], axis=0)
    down = jnp.concatenate([ref[k, last - t : last - t + 1, :] for k in order], axis=0)
    return jnp.where(odd, down, up)


def pack_fields(*refs):
    sources, (own, own_maps, near, far), held, arrived = refs[:4], refs[4:8], refs[8:12], refs[12]
    copies = [pltpu.make_async_copy(a, b, arrived.at[i]) for i, (a, b) in enumerate(zip(sources, held))]
    for copy in copies:
        copy.start()
    for copy in copies:
        copy.wait()
    tracer, mix, heading, depth = held
    levels, rows, lon_count = tracer.shape
    strips = lon_count // OWN
    odd = is_odd()
    for t in range(rows):
        field = oriented(tracer, t, odd)
        for j in range(strips):
            strip = strip_of(field, j, lon_count)
            own[j, t * levels : (t + 1) * levels, :] = strip
            if t < STEPS:
                at = (j * STEPS + STEPS - 1 - t) * levels
                far[at : at + levels, :] = strip
            if t > 0:
                at = (j * STEPS + rows - 1 - t) * levels
                near[at : at + levels, :] = strip
    base = strips * STEPS * levels
    for a, ref in enumerate((mix, heading, depth)):
        field = ref[...].astype(jnp.float32)
        flipped = jnp.concatenate([field[r : r + 1] for r in reversed(range(rows))], axis=0)
        up = jnp.where(odd, flipped, field)
        down = jnp.where(odd, field, flipped)
        for j in range(strips):
            own_maps[j, a * 4 : a * 4 + 4, :] = strip_of(up, j, lon_count)
            strip = strip_of(down, j, lon_count)
            at = base + (3 * j + a) * STEPS
            near[at : at + STEPS, :] = strip[:STEPS]
            far[at : at + STEPS, :] = strip[1:]
    own_maps[:, 12:, :] = jnp.zeros_like(own_maps[:, 12:, :])


def pack_classes(classes, weights, band_of_row, own, near, far, scales):
    levels, rows, lon_count = classes.shape
    strips = lon_count // OWN
    odd = is_odd()
    for t in range(rows):
        field = oriented(classes, t, odd)
        for j in range(strips):
            strip = strip_of(field, j, lon_count)
            own[j, t * levels : (t + 1) * levels, :] = strip
            if t < STEPS:
                at = (j * STEPS + STEPS - 1 - t) * levels
                far[at : at + levels, :] = strip
            if t > 0:
                at = (j * STEPS + rows - 1 - t) * levels
                near[at : at + levels, :] = strip
    class_count = weights.shape[1]
    label = lax.broadcasted_iota(jnp.int32, (1, LANES), 1)
    scale_rows, band_rows = [], []
    for pair in range(2):
        band = band_of_row[jnp.where(odd, 3 - 2 * pair, 2 * pair)]
        scale = weights[pl.ds(band, 1), :]
        scale_rows.append(jnp.concatenate([scale, jnp.zeros((1, LANES - class_count), jnp.float32)], axis=1))
        band_rows.append(jnp.where(label == LANES - 1, band.astype(jnp.float32), 0.0))
    scales[...] = jnp.concatenate(
        scale_rows + band_rows + [jnp.zeros((4, LANES), jnp.float32)], axis=0
    )


def east(x):
    return pltpu.roll(x, LANES - 1, 1)


def west(x):
    return pltpu.roll(x, 1, 1)


MAP_FIELDS = 10


def level_order(levels):
    half = levels // 2
    return [2 * (i % half) + i // half for i in range(levels)]


class Coefficients:
    blocks = {
        "wet": 0, "east_open": 1, "west_open": 2, "north_open": 3,
        "east_mix": 4, "west_mix": 5, "north_mix": 6,
        "east_dir": 7, "west_dir": 8, "north_dir": 9,
    }

    def __init__(self, maps, j, levels):
        order = lax.broadcasted_iota(jnp.int32, (levels, LANES), 0)
        half = levels // 2
        self.level = (2 * (order & (half - 1)) + jnp.where(order < half, 0, 1)).astype(jnp.float32)
        self.levels = levels
        self.maps = maps
        self.j = j
        self.cache = {}

    def row(self, kind, t):
        at = 16 * self.blocks[kind] + t + STEPS
        return jnp.broadcast_to(self.maps[self.j, at : at + 1, :], (self.levels, LANES))

    def get(self, kind, t):
        if (kind, t) not in self.cache:
            side, _, what = kind.partition("_")
            if kind == "column":
                value = jnp.where(self.level + 1.0 < self.row("wet", t), vertical_mix, 0.0)
            elif kind == "wet" or what == "open":
                value = self.level < self.row(kind, t)
            else:
                value = jnp.where(self.get(side + "_open", t), self.row(kind, t), 0.0)
            self.cache[kind, t] = value
        return self.cache[kind, t]


def column(field, coefficient):
    half = field.shape[0] // 2
    even, odd = field[:half], field[half:]
    after_even = coefficient[:half] * (odd - even)
    after_odd = coefficient[half:] * (pltpu.roll(even, half - 1, 0) - odd)
    return jnp.concatenate([after_even - pltpu.roll(after_odd, 1, 0), after_odd - after_even], axis=0)


def gaps(field, rows):
    to_east = {t: east(field[t]) - field[t] for t in rows}
    to_west = {t: west(field[t]) - field[t] for t in rows}
    to_north = {t: field[t + 1] - field[t] for t in range(rows[0] - 1, rows[-1] + 1)}
    return to_east, to_west, to_north


def spread(coef, kind, steps, rows):
    to_east, to_west, to_north = steps
    flux = {t: coef.get("north_" + kind, t) * to_north[t] for t in range(rows[0] - 1, rows[-1] + 1)}
    return {
        t: coef.get("east_" + kind, t) * to_east[t]
        + coef.get("west_" + kind, t) * to_west[t]
        + (flux[t] - flux[t - 1])
        for t in rows
    }


def advance(coef, field, steps, rows):
    moved = spread(coef, "mix", steps, rows)
    return {t: field[t] + moved[t] + column(field[t], coef.get("column", t)) for t in rows}


def face_maps(own_maps, near, far, maps, base):
    strips = own_maps.shape[0]
    count, edge = lax.axis_size("lat"), lax.axis_index("lat")
    keep = jnp.where(jnp.logical_and(edge != 0, edge != count - 1), 1.0, 0.0)

    def north(x):
        return pltpu.roll(x, 15, 0)

    for j in range(strips):
        whole = []
        for a in range(3):
            at = base + (3 * j + a) * STEPS
            low = far[at : at + STEPS, :]
            if a == 2:
                low = low * keep
            high = near[at : at + STEPS, :]
            whole.append(jnp.concatenate([low, own_maps[j, 4 * a : 4 * a + 4, :], high, high, high], axis=0))
        mix, heading, depth = whole
        blocks = [depth] + [jnp.minimum(depth, f(depth)) for f in (east, west, north)]
        blocks += [0.5 * (x + f(x)) for x in (mix, heading) for f in (east, west, north)]
        for i, block in enumerate(blocks):
            maps[j, 16 * i : 16 * i + 16, :] = block


def class_hits(value, label, levels):
    top = value.astype(jnp.bfloat16)
    bottom = (value - top.astype(jnp.float32)).astype(jnp.bfloat16)
    high = (label >> LOW_SHIFT).astype(jnp.float32).astype(jnp.bfloat16)
    low = (label & (LOW_COUNT - 1)).astype(jnp.float32).astype(jnp.bfloat16)
    none = jnp.zeros((levels, LANES), jnp.bfloat16)
    one = jnp.ones((levels, LANES), jnp.bfloat16)
    picks = [high == jnp.bfloat16(h) for h in range(HIGH_COUNT)]
    left = [jnp.where(p, part, none) for part in (top, bottom) for p in picks]
    right = [jnp.where(low == jnp.bfloat16(l), one, none) for l in range(LOW_COUNT)]
    return jnp.concatenate(left, axis=0), jnp.concatenate(right, axis=0)


def forward(scales, own, own_maps, near, far, classes, sums, later, maps, grams):
    strips, _, _ = own.shape
    levels = own.shape[1] // 4
    face_maps(own_maps, near, far, maps, strips * STEPS * levels)
    grams[...] = jnp.zeros_like(grams)
    lane = lax.broadcasted_iota(jnp.int32, (levels, LANES), 1)
    inner = jnp.logical_and(lane >= GHOST, lane < LANES - GHOST)

    def some_strips(i, carry):
        group = [i * GROUP + u for u in range(GROUP)]
        coefs = [Coefficients(maps, j, levels) for j in group]
        fields, tangents = [], [None] * GROUP
        for j in group:
            field = {}
            for s in range(STEPS):
                at = pl.multiple_of((j * STEPS + s) * levels, levels)
                field[s - STEPS] = far[pl.ds(at, levels), :]
                field[4 + s] = near[pl.ds(at, levels), :]
            for t in range(4):
                field[t] = own[j, t * levels : (t + 1) * levels, :]
            fields.append(field)
        for n in range(STEPS):
            rows = list(range(n + 1 - STEPS, 4 + STEPS - n - 1))
            for u, j in enumerate(group):
                steps = gaps(fields[u], rows)
                pushed = spread(coefs[u], "dir", steps, rows)
                if n > 0:
                    carried = advance(coefs[u], tangents[u], gaps(tangents[u], rows), rows)
                    pushed = {t: pushed[t] + carried[t] for t in rows}
                tangents[u] = pushed
                if n + 1 < STEPS:
                    fields[u] = advance(coefs[u], fields[u], steps, rows)
                    for t in range(-1, 5):
                        at = (n * 6 + t + 1) * levels
                        later[j, at : at + levels, :] = fields[u][t]
        for pair in range(2):
            lefts, rights = [], []
            for u, j in enumerate(group):
                for t in (2 * pair, 2 * pair + 1):
                    chosen = jnp.logical_and(inner, coefs[u].get("wet", t))
                    value = jnp.where(chosen, tangents[u][t], 0.0)
                    left, right = class_hits(value, classes[j, t * levels : (t + 1) * levels, :], levels)
                    lefts.append(left)
                    rights.append(right)
            grams[pair] += lax.dot_general(
                jnp.concatenate(lefts, axis=1),
                jnp.concatenate(rights, axis=1),
                (((1,), (1,)), ((), ())),
                preferred_element_type=jnp.float32,
            )
        return carry

    lax.fori_loop(0, strips // GROUP, some_strips, 0)

    width = LOW_COUNT * levels
    own_level = lax.broadcasted_iota(jnp.int32, (levels, width), 0)
    other_level = lax.broadcasted_iota(jnp.int32, (levels, width), 1) & (levels - 1)
    diagonal = own_level == other_level
    sheets = []
    for pair in range(2):
        for h in range(HIGH_COUNT):
            both = (
                grams[pair, h * levels : (h + 1) * levels, :]
                + grams[pair, (HIGH_COUNT + h) * levels : (HIGH_COUNT + h + 1) * levels, :]
            )
            sheets.append(jnp.sum(jnp.where(diagonal, both, 0.0), axis=0, keepdims=True))
        sheets.append(jnp.zeros((8 - HIGH_COUNT, width), jnp.float32))
    rest = jnp.concatenate(sheets, axis=0)
    parts = []
    for _ in range(3):
        part = rest.astype(jnp.bfloat16)
        rest = rest - part.astype(jnp.float32)
        parts.append(part)
    at_low = lax.broadcasted_iota(jnp.int32, (width, LANES), 0) >> (levels.bit_length() - 1)
    of_low = lax.broadcasted_iota(jnp.int32, (width, LANES), 1) & (LOW_COUNT - 1)
    gather = jnp.where(at_low == of_low, 1.0, 0.0).astype(jnp.bfloat16)
    added = jnp.dot(jnp.concatenate(parts, axis=0), gather, preferred_element_type=jnp.float32)
    added = (added[32:48] + added[16:32]) + added[0:16]
    here = lax.broadcasted_iota(jnp.int32, (8, LANES), 0)
    label = lax.broadcasted_iota(jnp.int32, (8, LANES), 1)
    totals = [
        jnp.sum(
            jnp.where(here == (label >> LOW_SHIFT), added[8 * p : 8 * p + 8], 0.0), axis=0, keepdims=True
        )
        for p in range(2)
    ]
    finish_sums(scales, totals, sums)


def finish_sums(scales, totals, sums):
    weighted = [scales[p : p + 1, :] * totals[p] for p in range(2)]
    sums[...] = jnp.concatenate(
        [totals[p] + scales[2 + p : 3 + p, :] for p in range(2)]
        + weighted
        + [jnp.zeros((4, LANES), jnp.float32)],
        axis=0,
    )


def adjoint_part(
    own, own_maps, near, far, later, own_classes, near_classes, far_classes,
    own_sums, near_sums, far_sums, gradient, maps, strips_out,
):
    strips = own.shape[0]
    levels = own.shape[1] // 4
    face_maps(own_maps, near, far, maps, strips * STEPS * levels)
    rows, lon_count = gradient.shape
    odd = is_odd()

    def some_strips(i, carry):
        group = [i * GROUP + u for u in range(GROUP)]
        coefs = [Coefficients(maps, j, levels) for j in group]
        fields, adjoints = [], []
        for u, j in enumerate(group):
            field = [{t: own[j, t * levels : (t + 1) * levels, :] for t in range(4)}]
            at = pl.multiple_of((j * STEPS + STEPS - 1) * levels, levels)
            field[0][-1] = far[pl.ds(at, levels), :]
            at = pl.multiple_of(j * STEPS * levels, levels)
            field[0][4] = near[pl.ds(at, levels), :]
            for n in range(STEPS - 1):
                field.append(
                    {t: later[j, (n * 6 + t + 1) * levels : (n * 6 + t + 2) * levels, :] for t in range(-1, 5)}
                )
            fields.append(field)
            adjoint = {}
            for t in range(-STEPS, 4 + STEPS):
                if t < 0:
                    at = pl.multiple_of((j * STEPS + t + STEPS) * levels, levels)
                    label = far_classes[pl.ds(at, levels), :]
                    source, row = far_sums, 2 + (-1 - t) // 2
                elif t < 4:
                    label = own_classes[j, t * levels : (t + 1) * levels, :]
                    source, row = own_sums, 2 + t // 2
                else:
                    at = pl.multiple_of((j * STEPS + t - 4) * levels, levels)
                    label = near_classes[pl.ds(at, levels), :]
                    source, row = near_sums, 2 + (7 - t) // 2
                table = jnp.broadcast_to(source[row : row + 1, :], (8, LANES))
                value = jnp.concatenate(
                    [jnp.take_along_axis(table, label[k : k + 8, :], axis=1) for k in range(0, levels, 8)],
                    axis=0,
                )
                adjoint[t] = jnp.where(coefs[u].get("wet", t), value, 0.0)
            adjoints.append(adjoint)
        east_total = [{t: 0.0 for t in range(4)} for _ in group]
        north_total = [{t: 0.0 for t in range(-1, 4)} for _ in group]
        for n in reversed(range(STEPS)):
            rows_out = list(range(-n, 4 + n))
            for u, j in enumerate(group):
                steps = gaps(adjoints[u], rows_out)
                field = fields[u][n]
                for t in range(4):
                    gap = east(field[t]) - field[t]
                    east_total[u][t] = east_total[u][t] + gap * steps[0][t]
                for t in range(-1, 4):
                    gap = field[t + 1] - field[t]
                    north_total[u][t] = north_total[u][t] + gap * steps[2][t]
                if n > 0:
                    adjoints[u] = advance(coefs[u], adjoints[u], steps, rows_out)
        for u, j in enumerate(group):
            north_part = {
                t: jnp.where(coefs[u].get("north_open", t), north_total[u][t], 0.0) for t in range(-1, 4)
            }
            out = []
            for t in range(4):
                part = jnp.where(coefs[u].get("east_open", t), east_total[u][t], 0.0)
                out.append(jnp.sum(part, axis=0, keepdims=True))
            part = jnp.concatenate(out, axis=0)
            part = part + west(part)
            north_part = [
                jnp.sum(north_part[t] + north_part[t - 1], axis=0, keepdims=True) for t in range(4)
            ]
            strips_out[j, 0:4, :] = -0.5 * (part + jnp.concatenate(north_part, axis=0))
        return carry

    lax.fori_loop(0, strips // GROUP, some_strips, 0)
    up = jnp.concatenate([strips_out[j, 0:4, GHOST : LANES - GHOST] for j in range(strips)], axis=1)
    down = jnp.concatenate([up[t : t + 1] for t in reversed(range(4))], axis=0)
    gradient[...] = jnp.where(odd, down, up)


def near_pairs(count):
    return [(i, i ^ 1) for i in range(count)]


def far_pairs(members, count):
    pairs = []
    for m in range(members):
        for i in range(1, count - 1, 2):
            pairs += [(m * count + i, m * count + i + 1), (m * count + i + 1, m * count + i)]
        for i in (0, count - 1):
            pairs.append((m * count + i, (m ^ 1) * count + i))
    return pairs


def vmem(count):
    return [pl.BlockSpec(memory_space=pltpu.VMEM)] * count


def cost(nanoseconds):
    return pl.CostEstimate(flops=1153500 * nanoseconds, bytes_accessed=3690 * nanoseconds, transcendentals=0)


def body(tracer, diffusivity, direction, column_depth, density_class, band_of_row, weights):
    levels, rows, lon_count = tracer.shape
    strips = lon_count // OWN
    count = lax.axis_size("lat")
    members = lax.axis_size("members")
    params = pltpu.CompilerParams(vmem_limit_bytes=VMEM_LIMIT)
    f32, i32 = jnp.float32, jnp.int32
    halo = strips * STEPS * levels
    payload = halo + strips * 9

    def to_near(x):
        return lax.ppermute(x, "lat", near_pairs(count))

    def to_far(x):
        return lax.ppermute(x, ("members", "lat"), far_pairs(members, count))

    own, own_maps, near_out, far_out = pl.pallas_call(
        pack_fields,
        name="pack_fields",
        out_shape=(
            jax.ShapeDtypeStruct((strips, rows * levels, LANES), f32),
            jax.ShapeDtypeStruct((strips, 16, LANES), f32),
            jax.ShapeDtypeStruct((payload, LANES), f32),
            jax.ShapeDtypeStruct((payload, LANES), f32),
        ),
        in_specs=[pl.BlockSpec(memory_space=pltpu.HBM)] * 4,
        out_specs=tuple(vmem(4)),
        scratch_shapes=[pltpu.VMEM(x.shape, x.dtype) for x in (tracer, diffusivity, direction, column_depth)]
        + [pltpu.SemaphoreType.DMA((4,))],
        compiler_params=params,
    )(tracer, diffusivity, direction, column_depth)
    far = to_far(far_out)
    near = to_near(near_out)

    own_classes, near_classes_out, far_classes_out, scales = pl.pallas_call(
        pack_classes,
        name="pack_classes",
        out_shape=(
            jax.ShapeDtypeStruct((strips, rows * levels, LANES), i32),
            jax.ShapeDtypeStruct((halo, LANES), i32),
            jax.ShapeDtypeStruct((halo, LANES), i32),
            jax.ShapeDtypeStruct((8, LANES), f32),
        ),
        in_specs=vmem(2) + [pl.BlockSpec(memory_space=pltpu.SMEM)],
        out_specs=tuple(vmem(4)),
        compiler_params=params,
    )(density_class, weights, band_of_row)
    near_classes_out, far_classes_out, near, far = lax.optimization_barrier(
        (near_classes_out, far_classes_out, near, far)
    )
    far_classes = to_far(far_classes_out)
    near_classes = to_near(near_classes_out)

    sums, later = pl.pallas_call(
        forward,
        name="forward",
        out_shape=(
            jax.ShapeDtypeStruct((8, LANES), f32),
            jax.ShapeDtypeStruct((strips, 12 * levels, LANES), f32),
        ),
        in_specs=vmem(6),
        out_specs=tuple(vmem(2)),
        cost_estimate=cost(4000),
        scratch_shapes=[
            pltpu.VMEM((strips, 16 * MAP_FIELDS, LANES), f32),
            pltpu.VMEM((2, 2 * HIGH_COUNT * levels, LOW_COUNT * levels), f32),
        ],
        compiler_params=params,
    )(scales, own, own_maps, near, far, own_classes)

    near_sums = to_near(sums)
    far_sums = to_far(sums)
    gathered = jnp.concatenate([sums, near_sums], axis=0)

    def sensitivities(near_classes, far_classes, far_sums):
        return pl.pallas_call(
            adjoint_part,
            name="adjoint_part",
            out_shape=jax.ShapeDtypeStruct((rows, lon_count), f32),
            in_specs=vmem(11),
            out_specs=pl.BlockSpec(memory_space=pltpu.VMEM),
            scratch_shapes=[
                pltpu.VMEM((strips, 16 * MAP_FIELDS, LANES), f32),
                pltpu.VMEM((strips, 8, LANES), f32),
            ],
            cost_estimate=cost(4000),
            compiler_params=params,
        )(own, own_maps, near, far, later, own_classes, near_classes, far_classes, sums, near_sums, far_sums)

    gathered, near_classes, far_classes = lax.optimization_barrier((gathered, near_classes, far_classes))
    gradient = None
    step = 2
    while step < count:
        other = lax.ppermute(gathered, "lat", [(i, i ^ step) for i in range(count)])
        if step == 4:
            gradient = sensitivities(near_classes, far_classes, far_sums)
            other, gradient = lax.optimization_barrier((other, gradient))
        gathered = jnp.concatenate([gathered, other], axis=0)
        if step == 2:
            gathered, far_sums = lax.optimization_barrier((gathered, far_sums))
        step *= 2
    band_own = weights.shape[0] // count
    finished = gathered.reshape(count, 8, LANES)[:, :2]
    wanted = lax.axis_index("lat") * band_own + jnp.arange(band_own)
    hits = finished[None, :, :, LANES - 1] == wanted[:, None, None].astype(f32)
    binned = jnp.sum(
        jnp.where(hits[..., None], finished[None, :, :, : weights.shape[1]], 0.0), axis=(1, 2)
    )
    return binned, gradient


def solution(mesh):
    placed = (
        P(None, ("members", "lat"), None),
        P("lat", None),
        P(("members", "lat"), None),
        P("lat", None),
        P(None, ("members", "lat"), None),
        P("lat"),
        P(),
    )
    return jax.shard_map(
        body,
        mesh=mesh,
        in_specs=placed,
        out_specs=(P(("members", "lat"), None), P(("members", "lat"), None)),
        check_vma=False,
    )
```

```python
import functools

import jax
import jax.numpy as jnp
from jax import lax
from jax.experimental import pallas as pl
from jax.experimental.pallas import tpu as pltpu
from jax.sharding import PartitionSpec as P

STEPS = 3
vertical_mix = 0.05

LANES = 128
GHOST = 4
OWN = LANES - 2 * GHOST
HIGH_COUNT = 9
LOW_COUNT = 8
LOW_SHIFT = 3
GROUP = 12
VMEM_LIMIT = 16 * 1024 * 1024


def strip_of(row, j, lon_count):
    first = OWN * j - GHOST
    last = first + LANES
    if first < 0:
        return jnp.concatenate([row[:, first + lon_count :], row[:, :last]], axis=1)
    if last > lon_count:
        return jnp.concatenate([row[:, first:], row[:, : last - lon_count]], axis=1)
    return row[:, first:last]


def is_odd():
    return lax.rem(lax.axis_index("lat"), 2) == 1


def oriented(ref, t, odd):
    last = ref.shape[1] - 1
    order = level_order(ref.shape[0])
    up = jnp.concatenate([ref[k, t : t + 1, :] for k in order], axis=0)
    down = jnp.concatenate([ref[k, last - t : last - t + 1, :] for k in order], axis=0)
    return jnp.where(odd, down, up)


def bring(sources, held, arrived):
    copies = [pltpu.make_async_copy(a, b, arrived.at[i]) for i, (a, b) in enumerate(zip(sources, held))]
    for copy in copies:
        copy.start()
    for copy in copies:
        copy.wait()


def pack_fields(*refs):
    sources, (own, own_maps, near, far), held, arrived = refs[:4], refs[4:8], refs[8:12], refs[12]
    bring(sources, held, arrived)
    tracer, mix, heading, depth = held
    levels, rows, lon_count = tracer.shape
    strips = lon_count // OWN
    odd = is_odd()
    for t in range(rows):
        field = oriented(tracer, t, odd)
        for j in range(strips):
            strip = strip_of(field, j, lon_count)
            own[j, t * levels : (t + 1) * levels, :] = strip
            if t < STEPS:
                at = (j * STEPS + STEPS - 1 - t) * levels
                far[at : at + levels, :] = strip
            if t > 0:
                at = (j * STEPS + rows - 1 - t) * levels
                near[at : at + levels, :] = strip
    base = strips * STEPS * levels
    for a, ref in enumerate((mix, heading, depth)):
        field = ref[...].astype(jnp.float32)
        flipped = jnp.concatenate([field[r : r + 1] for r in reversed(range(rows))], axis=0)
        up = jnp.where(odd, flipped, field)
        down = jnp.where(odd, field, flipped)
        for j in range(strips):
            own_maps[j, a * 4 : a * 4 + 4, :] = strip_of(up, j, lon_count)
            strip = strip_of(down, j, lon_count)
            at = base + (3 * j + a) * STEPS
            near[at : at + STEPS, :] = strip[:STEPS]
            far[at : at + STEPS, :] = strip[1:]
    own_maps[:, 12:, :] = jnp.zeros_like(own_maps[:, 12:, :])


def pack_classes(*refs):
    sources, (own, near, far, scales), held, arrived = refs[:3], refs[3:7], refs[7:10], refs[10]
    bring(sources, held, arrived)
    classes, weights, band_of_row = held
    levels, rows, lon_count = classes.shape
    strips = lon_count // OWN
    odd = is_odd()
    for t in range(rows):
        field = oriented(classes, t, odd)
        for j in range(strips):
            strip = strip_of(field, j, lon_count)
            own[j, t * levels : (t + 1) * levels, :] = strip
            if t < STEPS:
                at = (j * STEPS + STEPS - 1 - t) * levels
                far[at : at + levels, :] = strip
            if t > 0:
                at = (j * STEPS + rows - 1 - t) * levels
                near[at : at + levels, :] = strip
    class_count = weights.shape[1]
    scale_rows, band_rows = [], []
    for pair in range(2):
        band = band_of_row[jnp.where(odd, 3 - 2 * pair, 2 * pair)]
        scale = weights[pl.ds(band, 1), :]
        scale_rows.append(jnp.concatenate([scale, jnp.zeros((1, LANES - class_count), jnp.float32)], axis=1))
        band_rows.append(jnp.full((1, LANES), band.astype(jnp.float32)))
    blank = jnp.zeros((2, LANES), jnp.float32)
    scales[...] = jnp.concatenate(scale_rows + [blank] + band_rows + [blank], axis=0)


def east(x):
    return pltpu.roll(x, LANES - 1, 1)


def west(x):
    return pltpu.roll(x, 1, 1)


MAP_FIELDS = 7


def level_order(levels):
    half = levels // 2
    return [2 * (i % half) + i // half for i in range(levels)]


class Coefficients:
    blocks = {
        "wet": 0, "east_open": 1, "north_open": 2,
        "east_mix": 3, "north_mix": 4, "east_dir": 5, "north_dir": 6,
    }

    def __init__(self, maps, j, levels):
        order = lax.broadcasted_iota(jnp.int32, (levels, LANES), 0)
        half = levels // 2
        self.level = (2 * (order & (half - 1)) + jnp.where(order < half, 0, 1)).astype(jnp.float32)
        self.levels = levels
        self.maps = maps
        self.j = j
        self.cache = {}

    def row(self, kind, t):
        at = 16 * self.blocks[kind] + t + STEPS
        return jnp.broadcast_to(self.maps[self.j, at : at + 1, :], (self.levels, LANES))

    def get(self, kind, t):
        if (kind, t) not in self.cache:
            side, _, what = kind.partition("_")
            if kind == "column":
                value = jnp.where(self.level + 1.0 < self.row("wet", t), vertical_mix, 0.0)
            elif kind == "wet" or what == "open":
                value = self.level < self.row(kind, t)
            else:
                value = jnp.where(self.get(side + "_open", t), self.row(kind, t), 0.0)
            self.cache[kind, t] = value
        return self.cache[kind, t]


def column(field, coefficient):
    half = field.shape[0] // 2
    even, odd = field[:half], field[half:]
    after_even = coefficient[:half] * (odd - even)
    after_odd = coefficient[half:] * (pltpu.roll(even, half - 1, 0) - odd)
    return jnp.concatenate([after_even - pltpu.roll(after_odd, 1, 0), after_odd - after_even], axis=0)


def gaps(fields, rows):
    turned = [{t: east(field[t]) for t in rows} for field in fields]
    to_east = [{t: turn[t] - field[t] for t in rows} for turn, field in zip(turned, fields)]
    faces = range(rows[0] - 1, rows[-1] + 1)
    to_north = [{t: field[t + 1] - field[t] for t in faces} for field in fields]
    return list(zip(to_east, to_north))


def fluxes(coefs, kind, steps):
    return [
        (
            {t: coef.get("east_" + kind, t) * to_east[t] for t in to_east},
            {t: coef.get("north_" + kind, t) * to_north[t] for t in to_north},
        )
        for coef, (to_east, to_north) in zip(coefs, steps)
    ]


def both(ones, others):
    return [
        tuple({t: a[t] + b[t] for t in a} for a, b in zip(one, other)) for one, other in zip(ones, others)
    ]


def gathered_in(flux, rows, fields=None, coefs=None):
    turned = [{t: west(across[t]) for t in rows} for across, _ in flux]
    still = [{t: along[t] - along[t - 1] for t in rows} for _, along in flux]
    if fields is not None:
        still = [
            {t: rest[t] + (field[t] + column(field[t], coef.get("column", t))) for t in rows}
            for rest, field, coef in zip(still, fields, coefs)
        ]
    return [
        {t: rest[t] + (across[t] - turn[t]) for t in rows}
        for rest, (across, _), turn in zip(still, flux, turned)
    ]


def face_maps(own_maps, near, far, maps, base):
    strips = own_maps.shape[0]
    count, edge = lax.axis_size("lat"), lax.axis_index("lat")
    keep = jnp.where(jnp.logical_and(edge != 0, edge != count - 1), 1.0, 0.0)

    def north(x):
        return pltpu.roll(x, 15, 0)

    for j in range(strips):
        whole = []
        for a in range(3):
            at = base + (3 * j + a) * STEPS
            low = far[at : at + STEPS, :]
            if a == 2:
                low = low * keep
            high = near[at : at + STEPS, :]
            whole.append(jnp.concatenate([low, own_maps[j, 4 * a : 4 * a + 4, :], high, high, high], axis=0))
        mix, heading, depth = whole
        blocks = [depth] + [jnp.minimum(depth, f(depth)) for f in (east, north)]
        blocks += [0.5 * (x + f(x)) for x in (mix, heading) for f in (east, north)]
        for i, block in enumerate(blocks):
            maps[j, 16 * i : 16 * i + 16, :] = block


def class_hits(value, label, levels):
    top = value.astype(jnp.bfloat16)
    bottom = (value - top.astype(jnp.float32)).astype(jnp.bfloat16)
    high = (label >> LOW_SHIFT).astype(jnp.float32).astype(jnp.bfloat16)
    low = (label & (LOW_COUNT - 1)).astype(jnp.float32).astype(jnp.bfloat16)
    none = jnp.zeros((levels, LANES), jnp.bfloat16)
    one = jnp.ones((levels, LANES), jnp.bfloat16)
    left = [jnp.where(high == jnp.bfloat16(h), one, none) for h in range(HIGH_COUNT)]
    picks = [low == jnp.bfloat16(l) for l in range(LOW_COUNT)]
    right = [jnp.where(p, part, none) for part in (top, bottom) for p in picks]
    return jnp.concatenate(left, axis=0), jnp.concatenate(right, axis=0)


def forward(scales, own, own_maps, near, far, classes, sums, later, maps, grams):
    strips, _, _ = own.shape
    levels = own.shape[1] // 4
    face_maps(own_maps, near, far, maps, strips * STEPS * levels)
    grams[...] = jnp.zeros_like(grams)
    lane = lax.broadcasted_iota(jnp.int32, (levels, LANES), 1)
    inner = jnp.logical_and(lane >= GHOST, lane < LANES - GHOST)

    def some_strips(i, carry):
        group = [i * GROUP + u for u in range(GROUP)]
        coefs = [Coefficients(maps, j, levels) for j in group]
        fields, tangents = [], None
        for j in group:
            field = {}
            for s in range(STEPS):
                at = pl.multiple_of((j * STEPS + s) * levels, levels)
                field[s - STEPS] = far[pl.ds(at, levels), :]
                field[4 + s] = near[pl.ds(at, levels), :]
            for t in range(4):
                field[t] = own[j, t * levels : (t + 1) * levels, :]
            fields.append(field)
        for n in range(STEPS):
            rows = list(range(n + 1 - STEPS, 4 + STEPS - n - 1))
            steps = gaps(fields, rows)
            push = fluxes(coefs, "dir", steps)
            if n == 0:
                following = gathered_in(push, rows)
            else:
                push = both(push, fluxes(coefs, "mix", gaps(tangents, rows)))
                following = gathered_in(push, rows, tangents, coefs)
            tangents = following
            if n + 1 < STEPS:
                fields = gathered_in(fluxes(coefs, "mix", steps), rows, fields, coefs)
                for u, j in enumerate(group):
                    for t in range(-1, 5):
                        at = (n * 6 + t + 1) * levels
                        later[j, at : at + levels, :] = fields[u][t]
        for pair in range(2):
            lefts, rights = [], []
            for u, j in enumerate(group):
                for t in (2 * pair, 2 * pair + 1):
                    chosen = jnp.logical_and(inner, coefs[u].get("wet", t))
                    value = jnp.where(chosen, tangents[u][t], 0.0)
                    left, right = class_hits(value, classes[j, t * levels : (t + 1) * levels, :], levels)
                    lefts.append(left)
                    rights.append(right)
            grams[pair] += lax.dot_general(
                jnp.concatenate(lefts, axis=1),
                jnp.concatenate(rights, axis=1),
                (((1,), (1,)), ((), ())),
                preferred_element_type=jnp.float32,
            )
        return carry

    lax.fori_loop(0, strips // GROUP, some_strips, 0)

    width = 2 * LOW_COUNT * levels
    own_level = lax.broadcasted_iota(jnp.int32, (levels, width), 0)
    other_level = lax.broadcasted_iota(jnp.int32, (levels, width), 1) & (levels - 1)
    diagonal = own_level == other_level
    sheets = []
    for pair in range(2):
        for h in range(HIGH_COUNT):
            sheet = jnp.where(diagonal, grams[pair, h * levels : (h + 1) * levels, :], 0.0)
            sheets.append(jnp.sum(sheet, axis=0, keepdims=True))
        sheets.append(jnp.zeros((16 - HIGH_COUNT, width), jnp.float32))
    rest = jnp.concatenate(sheets, axis=0)
    parts = []
    for _ in range(3):
        part = rest.astype(jnp.bfloat16)
        rest = rest - part.astype(jnp.float32)
        parts.append(part)
    at_low = (lax.broadcasted_iota(jnp.int32, (width, LANES), 0) >> (levels.bit_length() - 1)) & (LOW_COUNT - 1)
    of_low = lax.broadcasted_iota(jnp.int32, (width, LANES), 1) & (LOW_COUNT - 1)
    gather = jnp.where(at_low == of_low, 1.0, 0.0).astype(jnp.bfloat16)
    added = jnp.dot(jnp.concatenate(parts, axis=0), gather, preferred_element_type=jnp.float32)
    added = (added[64:96] + added[32:64]) + added[0:32]
    here = lax.broadcasted_iota(jnp.int32, (16, LANES), 0)
    label = lax.broadcasted_iota(jnp.int32, (16, LANES), 1)
    totals = [
        jnp.sum(
            jnp.where(here == (label >> LOW_SHIFT), added[16 * p : 16 * p + 16], 0.0), axis=0, keepdims=True
        )
        for p in range(2)
    ]
    finish_sums(scales, totals, sums)


def finish_sums(scales, totals, sums):
    weighted = [scales[p : p + 1, :] * totals[p] for p in range(2)]
    sums[...] = jnp.concatenate(totals + weighted + [scales[4:8, :]], axis=0)


def pick_bins(*refs):
    pieces, binned = refs[:-1], refs[-1]
    band_own, class_count = binned.shape
    first = lax.axis_index("lat") * band_own
    found = [jnp.zeros((2, LANES), jnp.float32) for _ in range(band_own)]
    for piece in pieces:
        for at in range(0, piece.shape[0], 8):
            totals, bands = piece[at : at + 2, :], piece[at + 4 : at + 6, :]
            for m in range(band_own):
                hit = bands == (first + m).astype(jnp.float32)
                found[m] = found[m] + jnp.where(hit, totals, 0.0)
    whole = jnp.concatenate([jnp.sum(x, axis=0, keepdims=True) for x in found], axis=0)
    binned[...] = whole[:, :class_count]


def adjoint_part(
    own, own_maps, near, far, later, own_classes, near_classes, far_classes,
    own_sums, near_sums, far_sums, gradient, maps, strips_out,
):
    strips = own.shape[0]
    levels = own.shape[1] // 4
    face_maps(own_maps, near, far, maps, strips * STEPS * levels)
    rows, lon_count = gradient.shape
    odd = is_odd()

    def some_strips(i, carry):
        group = [i * GROUP + u for u in range(GROUP)]
        coefs = [Coefficients(maps, j, levels) for j in group]
        fields, adjoints = [], []
        for u, j in enumerate(group):
            field = [{t: own[j, t * levels : (t + 1) * levels, :] for t in range(4)}]
            at = pl.multiple_of((j * STEPS + STEPS - 1) * levels, levels)
            field[0][-1] = far[pl.ds(at, levels), :]
            at = pl.multiple_of(j * STEPS * levels, levels)
            field[0][4] = near[pl.ds(at, levels), :]
            for n in range(STEPS - 1):
                field.append(
                    {t: later[j, (n * 6 + t + 1) * levels : (n * 6 + t + 2) * levels, :] for t in range(-1, 5)}
                )
            fields.append(field)
            adjoint = {}
            for t in range(-STEPS, 4 + STEPS):
                if t < 0:
                    at = pl.multiple_of((j * STEPS + t + STEPS) * levels, levels)
                    label = far_classes[pl.ds(at, levels), :]
                    source, row = far_sums, 2 + (-1 - t) // 2
                elif t < 4:
                    label = own_classes[j, t * levels : (t + 1) * levels, :]
                    source, row = own_sums, 2 + t // 2
                else:
                    at = pl.multiple_of((j * STEPS + t - 4) * levels, levels)
                    label = near_classes[pl.ds(at, levels), :]
                    source, row = near_sums, 2 + (7 - t) // 2
                table = jnp.broadcast_to(source[row : row + 1, :], (8, LANES))
                value = jnp.concatenate(
                    [jnp.take_along_axis(table, label[k : k + 8, :], axis=1) for k in range(0, levels, 8)],
                    axis=0,
                )
                adjoint[t] = jnp.where(coefs[u].get("wet", t), value, 0.0)
            adjoints.append(adjoint)
        east_total = [{t: 0.0 for t in range(4)} for _ in group]
        north_total = [{t: 0.0 for t in range(-1, 4)} for _ in group]
        for n in reversed(range(STEPS)):
            rows_out = list(range(-n, 4 + n))
            steps = gaps(adjoints, rows_out)
            base_steps = gaps([fields[u][n] for u in range(GROUP)], list(range(4)))
            if n > 0:
                adjoints = gathered_in(fluxes(coefs, "mix", steps), rows_out, adjoints, coefs)
            for u in range(GROUP):
                for t in range(4):
                    east_total[u][t] = east_total[u][t] + base_steps[u][0][t] * steps[u][0][t]
                for t in range(-1, 4):
                    north_total[u][t] = north_total[u][t] + base_steps[u][1][t] * steps[u][1][t]
        for u, j in enumerate(group):
            north_part = {
                t: jnp.where(coefs[u].get("north_open", t), north_total[u][t], 0.0) for t in range(-1, 4)
            }
            out = []
            for t in range(4):
                part = jnp.where(coefs[u].get("east_open", t), east_total[u][t], 0.0)
                out.append(jnp.sum(part, axis=0, keepdims=True))
            part = jnp.concatenate(out, axis=0)
            part = part + west(part)
            north_part = [
                jnp.sum(north_part[t] + north_part[t - 1], axis=0, keepdims=True) for t in range(4)
            ]
            strips_out[j, 0:4, :] = -0.5 * (part + jnp.concatenate(north_part, axis=0))
        return carry

    lax.fori_loop(0, strips // GROUP, some_strips, 0)
    up = jnp.concatenate([strips_out[j, 0:4, GHOST : LANES - GHOST] for j in range(strips)], axis=1)
    down = jnp.concatenate([up[t : t + 1] for t in reversed(range(4))], axis=0)
    gradient[...] = jnp.where(odd, down, up)


def near_pairs(count):
    return [(i, i ^ 1) for i in range(count)]


def far_pairs(members, count):
    pairs = []
    for m in range(members):
        for i in range(1, count - 1, 2):
            pairs += [(m * count + i, m * count + i + 1), (m * count + i + 1, m * count + i)]
        for i in (0, count - 1):
            pairs.append((m * count + i, (m ^ 1) * count + i))
    return pairs


ADJOINT_AT = 1
CLASSES_AT = 0


def routes(count):
    bits = count.bit_length() - 1
    groups = [[1]] if bits % 2 else []
    for bit in range(bits % 2, bits, 2):
        one, two = 1 << bit, 2 << bit
        groups.append([one + two, two, one] if bit == 0 else [one, one + two, two])
    return groups


def vmem(count):
    return [pl.BlockSpec(memory_space=pltpu.VMEM)] * count


def cost(nanoseconds):
    return pl.CostEstimate(flops=1153500 * nanoseconds, bytes_accessed=3690 * nanoseconds, transcendentals=0)


def body(tracer, diffusivity, direction, column_depth, density_class, band_of_row, weights):
    levels, rows, lon_count = tracer.shape
    strips = lon_count // OWN
    count = lax.axis_size("lat")
    members = lax.axis_size("members")
    params = pltpu.CompilerParams(vmem_limit_bytes=VMEM_LIMIT)
    f32, i32 = jnp.float32, jnp.int32
    halo = strips * STEPS * levels
    payload = halo + strips * 9

    def to_near(x):
        return lax.ppermute(x, "lat", near_pairs(count))

    def to_far(x):
        return lax.ppermute(x, ("members", "lat"), far_pairs(members, count))

    own, own_maps, near_out, far_out = pl.pallas_call(
        pack_fields,
        name="pack_fields",
        out_shape=(
            jax.ShapeDtypeStruct((strips, rows * levels, LANES), f32),
            jax.ShapeDtypeStruct((strips, 16, LANES), f32),
            jax.ShapeDtypeStruct((payload, LANES), f32),
            jax.ShapeDtypeStruct((payload, LANES), f32),
        ),
        in_specs=[pl.BlockSpec(memory_space=pltpu.HBM)] * 4,
        out_specs=tuple(vmem(4)),
        scratch_shapes=[pltpu.VMEM(x.shape, x.dtype) for x in (tracer, diffusivity, direction, column_depth)]
        + [pltpu.SemaphoreType.DMA((4,))],
        compiler_params=params,
    )(*[pltpu.with_memory_space_constraint(x, pltpu.HBM) for x in (tracer, diffusivity, direction, column_depth)])
    far = to_far(far_out)
    near = to_near(near_out)

    own_classes, near_classes_out, far_classes_out, scales = pl.pallas_call(
        pack_classes,
        name="pack_classes",
        out_shape=(
            jax.ShapeDtypeStruct((strips, rows * levels, LANES), i32),
            jax.ShapeDtypeStruct((halo, LANES), i32),
            jax.ShapeDtypeStruct((halo, LANES), i32),
            jax.ShapeDtypeStruct((8, LANES), f32),
        ),
        in_specs=[pl.BlockSpec(memory_space=pltpu.HBM)] * 3,
        out_specs=tuple(vmem(4)),
        scratch_shapes=[
            pltpu.VMEM(density_class.shape, i32),
            pltpu.VMEM(weights.shape, f32),
            pltpu.SMEM(band_of_row.shape, i32),
            pltpu.SemaphoreType.DMA((3,)),
        ],
        compiler_params=params,
    )(*[pltpu.with_memory_space_constraint(x, pltpu.HBM) for x in (density_class, weights, band_of_row)])
    near_classes_out, far_classes_out, near, far = lax.optimization_barrier(
        (near_classes_out, far_classes_out, near, far)
    )
    far_classes = to_far(far_classes_out)
    near_classes = to_near(near_classes_out)

    sums, later = pl.pallas_call(
        forward,
        name="forward",
        out_shape=(
            jax.ShapeDtypeStruct((8, LANES), f32),
            jax.ShapeDtypeStruct((strips, 12 * levels, LANES), f32),
        ),
        in_specs=vmem(6),
        out_specs=tuple(vmem(2)),
        cost_estimate=cost(4000),
        scratch_shapes=[
            pltpu.VMEM((strips, 16 * MAP_FIELDS, LANES), f32),
            pltpu.VMEM((2, HIGH_COUNT * levels, 2 * LOW_COUNT * levels), f32),
        ],
        compiler_params=params,
    )(scales, own, own_maps, near, far, own_classes)

    far_sums = to_far(sums)

    def sensitivities(near_classes, far_classes, near_sums, far_sums):
        return pl.pallas_call(
            adjoint_part,
            name="adjoint_part",
            out_shape=jax.ShapeDtypeStruct((rows, lon_count), f32),
            in_specs=vmem(11),
            out_specs=pl.BlockSpec(memory_space=pltpu.VMEM),
            scratch_shapes=[
                pltpu.VMEM((strips, 16 * MAP_FIELDS, LANES), f32),
                pltpu.VMEM((strips, 8, LANES), f32),
            ],
            cost_estimate=cost(4000),
            compiler_params=params,
        )(own, own_maps, near, far, later, own_classes, near_classes, far_classes, sums, near_sums, far_sums)

    gathered, gradient, near_sums = sums, None, None
    groups = routes(count)
    for i, group in enumerate(groups):
        others = [lax.ppermute(gathered, "lat", [(d, d ^ k) for d in range(count)]) for k in group]
        if i == ADJOINT_AT:
            gradient = sensitivities(near_classes, far_classes, near_sums, far_sums)
            *others, gradient = lax.optimization_barrier((*others, gradient))
        if i == 0:
            near_sums = others[group.index(1)]
        pieces = [gathered] + others
        if i + 1 < len(groups):
            gathered = jnp.concatenate(pieces, axis=0)
        if i == CLASSES_AT:
            gathered, near_classes, far_classes = lax.optimization_barrier((gathered, near_classes, far_classes))
        if i + 1 == ADJOINT_AT:
            gathered, far_sums = lax.optimization_barrier((gathered, far_sums))
    binned = pl.pallas_call(
        pick_bins,
        name="pick_bins",
        out_shape=jax.ShapeDtypeStruct((weights.shape[0] // count, weights.shape[1]), f32),
        in_specs=vmem(len(pieces)),
        out_specs=pl.BlockSpec(memory_space=pltpu.VMEM),
        compiler_params=params,
    )(*pieces)
    return binned, gradient


def solution(mesh):
    placed = (
        P(None, ("members", "lat"), None),
        P("lat", None),
        P(("members", "lat"), None),
        P("lat", None),
        P(None, ("members", "lat"), None),
        P("lat"),
        P(),
    )
    return jax.shard_map(
        body,
        mesh=mesh,
        in_specs=placed,
        out_specs=(P(("members", "lat"), None), P(("members", "lat"), None)),
        check_vma=False,
    )
```

```python
import functools

import jax
import jax.numpy as jnp
from jax import lax
from jax.experimental import pallas as pl
from jax.experimental.pallas import tpu as pltpu
from jax.sharding import PartitionSpec as P

STEPS = 3
vertical_mix = 0.05

LANES = 128
GHOST = 4
OWN = LANES - 2 * GHOST
HIGH_COUNT = 9
LOW_COUNT = 8
LOW_SHIFT = 3
PIECES = (0, 6, 12)
VMEM_LIMIT = 16 * 1024 * 1024


def strip_of(row, j, lon_count):
    first = OWN * j - GHOST
    last = first + LANES
    if first < 0:
        return jnp.concatenate([row[:, first + lon_count :], row[:, :last]], axis=1)
    if last > lon_count:
        return jnp.concatenate([row[:, first:], row[:, : last - lon_count]], axis=1)
    return row[:, first:last]


def piece_of(j):
    return max(p for p in range(len(PIECES) - 1) if PIECES[p] <= j)


def is_odd():
    return lax.rem(lax.axis_index("lat"), 2) == 1


def oriented(ref, t, odd):
    last = ref.shape[1] - 1
    order = level_order(ref.shape[0])
    up = jnp.concatenate([ref[k, t : t + 1, :] for k in order], axis=0)
    down = jnp.concatenate([ref[k, last - t : last - t + 1, :] for k in order], axis=0)
    return jnp.where(odd, down, up)


def bring(sources, held, arrived):
    copies = [pltpu.make_async_copy(a, b, arrived.at[i]) for i, (a, b) in enumerate(zip(sources, held))]
    for copy in copies:
        copy.start()
    for copy in copies:
        copy.wait()


def pack_fields(*refs):
    parts = len(PIECES) - 1
    sources, (own, own_maps, near), fars, held, arrived = (
        refs[:4], refs[4:7], refs[7 : 7 + parts], refs[7 + parts : 11 + parts], refs[11 + parts],
    )
    bring(sources, held, arrived)
    tracer, mix, heading, depth = held
    levels, rows, lon_count = tracer.shape
    strips = lon_count // OWN
    odd = is_odd()

    def far_place(j):
        piece = piece_of(j)
        return fars[piece], j - PIECES[piece], PIECES[piece + 1] - PIECES[piece]

    for t in range(rows):
        field = oriented(tracer, t, odd)
        for j in range(strips):
            strip = strip_of(field, j, lon_count)
            own[j, t * levels : (t + 1) * levels, :] = strip
            if t < STEPS:
                far, local, _ = far_place(j)
                at = (local * STEPS + STEPS - 1 - t) * levels
                far[at : at + levels, :] = strip
            if t > 0:
                at = (j * STEPS + rows - 1 - t) * levels
                near[at : at + levels, :] = strip
    for a, ref in enumerate((mix, heading, depth)):
        field = ref[...].astype(jnp.float32)
        flipped = jnp.concatenate([field[r : r + 1] for r in reversed(range(rows))], axis=0)
        up = jnp.where(odd, flipped, field)
        down = jnp.where(odd, field, flipped)
        for j in range(strips):
            own_maps[j, a * 4 : a * 4 + 4, :] = strip_of(up, j, lon_count)
            strip = strip_of(down, j, lon_count)
            at = strips * STEPS * levels + (3 * j + a) * STEPS
            near[at : at + STEPS, :] = strip[:STEPS]
            far, local, count = far_place(j)
            at = count * STEPS * levels + (3 * local + a) * STEPS
            far[at : at + STEPS, :] = strip[1:]
    own_maps[:, 12:, :] = jnp.zeros_like(own_maps[:, 12:, :])


def pack_classes(*refs):
    sources, (own, scales), held, arrived = refs[:3], refs[3:5], refs[5:8], refs[8]
    bring(sources, held, arrived)
    classes, weights, band_of_row = held
    levels, rows, lon_count = classes.shape
    strips = lon_count // OWN
    odd = is_odd()
    for t in range(rows):
        field = oriented(classes, t, odd)
        for j in range(strips):
            strip = strip_of(field, j, lon_count)
            own[j, t * levels : (t + 1) * levels, :] = strip
    class_count = weights.shape[1]
    scale_rows, band_rows = [], []
    for pair in range(2):
        band = band_of_row[jnp.where(odd, 3 - 2 * pair, 2 * pair)]
        scale = weights[pl.ds(band, 1), :]
        scale_rows.append(jnp.concatenate([scale, jnp.zeros((1, LANES - class_count), jnp.float32)], axis=1))
        band_rows.append(jnp.full((1, LANES), band.astype(jnp.float32)))
    blank = jnp.zeros((2, LANES), jnp.float32)
    scales[...] = jnp.concatenate(scale_rows + [blank] + band_rows + [blank], axis=0)


def east(x):
    return pltpu.roll(x, LANES - 1, 1)


def west(x):
    return pltpu.roll(x, 1, 1)


MAP_FIELDS = 7


def level_order(levels):
    half = levels // 2
    return [2 * (i % half) + i // half for i in range(levels)]


class Coefficients:
    blocks = {
        "wet": 0, "east_open": 1, "north_open": 2,
        "east_mix": 3, "north_mix": 4, "east_dir": 5, "north_dir": 6,
    }

    def __init__(self, maps, j, levels):
        order = lax.broadcasted_iota(jnp.int32, (levels, LANES), 0)
        half = levels // 2
        self.level = (2 * (order & (half - 1)) + jnp.where(order < half, 0, 1)).astype(jnp.float32)
        self.levels = levels
        self.maps = maps
        self.j = j
        self.cache = {}

    def row(self, kind, t):
        at = 16 * self.blocks[kind] + t + STEPS
        return jnp.broadcast_to(self.maps[self.j, at : at + 1, :], (self.levels, LANES))

    def get(self, kind, t):
        if (kind, t) not in self.cache:
            side, _, what = kind.partition("_")
            if kind == "column":
                value = jnp.where(self.level + 1.0 < self.row("wet", t), vertical_mix, 0.0)
            elif kind == "wet" or what == "open":
                value = self.level < self.row(kind, t)
            else:
                value = jnp.where(self.get(side + "_open", t), self.row(kind, t), 0.0)
            self.cache[kind, t] = value
        return self.cache[kind, t]


def column(field, coefficient):
    half = field.shape[0] // 2
    even, odd = field[:half], field[half:]
    after_even = coefficient[:half] * (odd - even)
    after_odd = coefficient[half:] * (pltpu.roll(even, half - 1, 0) - odd)
    return jnp.concatenate([after_even - pltpu.roll(after_odd, 1, 0), after_odd - after_even], axis=0)


def gaps(fields, rows):
    turned = [{t: east(field[t]) for t in rows} for field in fields]
    to_east = [{t: turn[t] - field[t] for t in rows} for turn, field in zip(turned, fields)]
    faces = range(rows[0] - 1, rows[-1] + 1)
    to_north = [{t: field[t + 1] - field[t] for t in faces} for field in fields]
    return list(zip(to_east, to_north))


def fluxes(coefs, kind, steps):
    return [
        (
            {t: coef.get("east_" + kind, t) * to_east[t] for t in to_east},
            {t: coef.get("north_" + kind, t) * to_north[t] for t in to_north},
        )
        for coef, (to_east, to_north) in zip(coefs, steps)
    ]


def both(ones, others):
    return [
        tuple({t: a[t] + b[t] for t in a} for a, b in zip(one, other)) for one, other in zip(ones, others)
    ]


def gathered_in(flux, rows, fields=None, coefs=None):
    turned = [{t: west(across[t]) for t in rows} for across, _ in flux]
    still = [{t: along[t] - along[t - 1] for t in rows} for _, along in flux]
    if fields is not None:
        still = [
            {t: rest[t] + (field[t] + column(field[t], coef.get("column", t))) for t in rows}
            for rest, field, coef in zip(still, fields, coefs)
        ]
    return [
        {t: rest[t] + (across[t] - turn[t]) for t in rows}
        for rest, (across, _), turn in zip(still, flux, turned)
    ]


def face_maps(own_maps, near, fars, maps, strips, levels):
    count, edge = lax.axis_size("lat"), lax.axis_index("lat")
    keep = jnp.where(jnp.logical_and(edge != 0, edge != count - 1), 1.0, 0.0)

    def north(x):
        return pltpu.roll(x, 15, 0)

    for i, j in enumerate(strips):
        whole = []
        piece = piece_of(j)
        for a in range(3):
            at = (PIECES[piece + 1] - PIECES[piece]) * STEPS * levels + (3 * (j - PIECES[piece]) + a) * STEPS
            low = fars[piece][at : at + STEPS, :]
            if a == 2:
                low = low * keep
            at = PIECES[-1] * STEPS * levels + (3 * j + a) * STEPS
            high = near[at : at + STEPS, :]
            whole.append(jnp.concatenate([low, own_maps[j, 4 * a : 4 * a + 4, :], high, high, high], axis=0))
        mix, heading, depth = whole
        blocks = [depth] + [jnp.minimum(depth, f(depth)) for f in (east, north)]
        blocks += [0.5 * (x + f(x)) for x in (mix, heading) for f in (east, north)]
        for b, block in enumerate(blocks):
            maps[i, 16 * b : 16 * b + 16, :] = block


def class_hits(value, label, levels):
    top = value.astype(jnp.bfloat16)
    bottom = (value - top.astype(jnp.float32)).astype(jnp.bfloat16)
    high = (label >> LOW_SHIFT).astype(jnp.float32).astype(jnp.bfloat16)
    low = (label & (LOW_COUNT - 1)).astype(jnp.float32).astype(jnp.bfloat16)
    none = jnp.zeros((levels, LANES), jnp.bfloat16)
    one = jnp.ones((levels, LANES), jnp.bfloat16)
    left = [jnp.where(high == jnp.bfloat16(h), one, none) for h in range(HIGH_COUNT)]
    picks = [low == jnp.bfloat16(l) for l in range(LOW_COUNT)]
    right = [jnp.where(p, part, none) for part in (top, bottom) for p in picks]
    return jnp.concatenate(left, axis=0), jnp.concatenate(right, axis=0)


def later_row(n, t):
    return (n - 1) * 8 + t + STEPS - n


def forward(piece, *refs):
    last = piece + 2 == len(PIECES)
    refs = list(refs)
    own, own_maps, near, far, classes = refs[:5]
    del refs[:5]
    before = refs.pop(0) if piece > 0 else None
    scales = refs.pop(0) if last else None
    out, later, maps = refs[:3]
    grams = refs[3] if last else out
    levels = own.shape[1] // 4
    group = list(range(PIECES[piece], PIECES[piece + 1]))
    face_maps(own_maps, near, {piece: far}, maps, group, levels)
    lane = lax.broadcasted_iota(jnp.int32, (levels, LANES), 1)
    inner = jnp.logical_and(lane >= GHOST, lane < LANES - GHOST)
    coefs = [Coefficients(maps, u, levels) for u in range(len(group))]
    fields, tangents = [], None
    for u, j in enumerate(group):
        field = {t: own[j, t * levels : (t + 1) * levels, :] for t in range(4)}
        for s in range(STEPS):
            at = (u * STEPS + s) * levels
            field[s - STEPS] = far[at : at + levels, :]
            at = (j * STEPS + s) * levels
            field[4 + s] = near[at : at + levels, :]
        fields.append(field)
    for n in range(STEPS):
        rows = list(range(n + 1 - STEPS, 4 + STEPS - n - 1))
        steps = gaps(fields, rows)
        push = fluxes(coefs, "dir", steps)
        if n == 0:
            following = gathered_in(push, rows)
        else:
            push = both(push, fluxes(coefs, "mix", gaps(tangents, rows)))
            following = gathered_in(push, rows, tangents, coefs)
        tangents = following
        if n + 1 < STEPS:
            fields = gathered_in(fluxes(coefs, "mix", steps), rows, fields, coefs)
            for u in range(len(group)):
                for t in rows:
                    at = later_row(n + 1, t) * levels
                    later[u, at : at + levels, :] = fields[u][t]
    for pair in range(2):
        lefts, rights = [], []
        for u, j in enumerate(group):
            for t in (2 * pair, 2 * pair + 1):
                chosen = jnp.logical_and(inner, coefs[u].get("wet", t))
                value = jnp.where(chosen, tangents[u][t], 0.0)
                left, right = class_hits(value, classes[j, t * levels : (t + 1) * levels, :], levels)
                lefts.append(left)
                rights.append(right)
        gram = lax.dot_general(
            jnp.concatenate(lefts, axis=1),
            jnp.concatenate(rights, axis=1),
            (((1,), (1,)), ((), ())),
            preferred_element_type=jnp.float32,
        )
        grams[pair] = gram if before is None else before[pair] + gram
    if last:
        class_sums(grams, scales, out, levels)


def class_sums(grams, scales, sums, levels):
    width = 2 * LOW_COUNT * levels
    own_level = lax.broadcasted_iota(jnp.int32, (levels, width), 0)
    other_level = lax.broadcasted_iota(jnp.int32, (levels, width), 1) & (levels - 1)
    diagonal = own_level == other_level
    sheets = []
    for pair in range(2):
        for h in range(HIGH_COUNT):
            sheet = jnp.where(diagonal, grams[pair, h * levels : (h + 1) * levels, :], 0.0)
            sheets.append(jnp.sum(sheet, axis=0, keepdims=True))
        sheets.append(jnp.zeros((16 - HIGH_COUNT, width), jnp.float32))
    rest = jnp.concatenate(sheets, axis=0)
    parts = []
    for _ in range(3):
        part = rest.astype(jnp.bfloat16)
        rest = rest - part.astype(jnp.float32)
        parts.append(part)
    at_low = (lax.broadcasted_iota(jnp.int32, (width, LANES), 0) >> (levels.bit_length() - 1)) & (LOW_COUNT - 1)
    of_low = lax.broadcasted_iota(jnp.int32, (width, LANES), 1) & (LOW_COUNT - 1)
    gather = jnp.where(at_low == of_low, 1.0, 0.0).astype(jnp.bfloat16)
    added = jnp.dot(jnp.concatenate(parts, axis=0), gather, preferred_element_type=jnp.float32)
    added = (added[64:96] + added[32:64]) + added[0:32]
    here = lax.broadcasted_iota(jnp.int32, (16, LANES), 0)
    label = lax.broadcasted_iota(jnp.int32, (16, LANES), 1)
    totals = [
        jnp.sum(
            jnp.where(here == (label >> LOW_SHIFT), added[16 * p : 16 * p + 16], 0.0), axis=0, keepdims=True
        )
        for p in range(2)
    ]
    finish_sums(scales, totals, sums)


def finish_sums(scales, totals, sums):
    weighted = [scales[p : p + 1, :] * totals[p] for p in range(2)]
    sums[...] = jnp.concatenate(totals + weighted + [scales[4:8, :]], axis=0)


def finish(own_share, near_share, far_share, *refs):
    pieces, binned, gradient = refs[:-2], refs[-2], refs[-1]
    up = own_share[...] + (near_share[...] + far_share[...])
    down = jnp.concatenate([up[t : t + 1] for t in reversed(range(up.shape[0]))], axis=0)
    gradient[...] = jnp.where(is_odd(), down, up)
    band_own, class_count = binned.shape
    first = lax.axis_index("lat") * band_own
    found = [jnp.zeros((2, LANES), jnp.float32) for _ in range(band_own)]
    for piece in pieces:
        for at in range(0, piece.shape[0], 8):
            totals, bands = piece[at : at + 2, :], piece[at + 4 : at + 6, :]
            for m in range(band_own):
                hit = bands == (first + m).astype(jnp.float32)
                found[m] = found[m] + jnp.where(hit, totals, 0.0)
    whole = jnp.concatenate([jnp.sum(x, axis=0, keepdims=True) for x in found], axis=0)
    binned[...] = whole[:, :class_count]


def adjoint_part(own, own_maps, near, classes, sums, *refs):
    parts = len(PIECES) - 1
    fars, laters = refs[:parts], refs[parts : 2 * parts]
    own_share, near_share, far_share, maps = refs[2 * parts :]
    strips = own.shape[0]
    levels = own.shape[1] // 4
    group = list(range(strips))
    face_maps(own_maps, near, fars, maps, group, levels)
    coefs = [Coefficients(maps, j, levels) for j in group]
    adjoints = []
    for j in group:
        adjoint = {}
        for t in range(4):
            label = classes[j, t * levels : (t + 1) * levels, :]
            row = 2 + t // 2
            table = jnp.broadcast_to(sums[row : row + 1, :], (8, LANES))
            value = jnp.concatenate(
                [jnp.take_along_axis(table, label[k : k + 8, :], axis=1) for k in range(0, levels, 8)], axis=0
            )
            adjoint[t] = jnp.where(coefs[j].get("wet", t), value, 0.0)
        adjoints.append(adjoint)

    def base(n, j):
        piece = piece_of(j)
        local = j - PIECES[piece]
        field = {}
        for t in range(n - STEPS, 4 + STEPS - n):
            if n > 0:
                at = later_row(n, t) * levels
                field[t] = laters[piece][local, at : at + levels, :]
            elif t < 0:
                at = (local * STEPS + t + STEPS) * levels
                field[t] = fars[piece][at : at + levels, :]
            elif t < 4:
                field[t] = own[j, t * levels : (t + 1) * levels, :]
            else:
                at = (j * STEPS + t - 4) * levels
                field[t] = near[at : at + levels, :]
        return field

    east_total = [{} for _ in group]
    north_total = [{} for _ in group]
    for n in reversed(range(STEPS)):
        rows = list(range(n + 1 - STEPS, 3 + STEPS - n))
        low, high = rows[0], rows[-1]
        turned = [{t: east(field[t]) for t in rows} for field in adjoints]
        base_steps = gaps([base(n, j) for j in group], rows)
        to_east = [{t: turn[t] - field[t] for t in rows} for turn, field in zip(turned, adjoints)]
        to_north = [
            {low - 1: field[low], high: -field[high], **{t: field[t + 1] - field[t] for t in rows[:-1]}}
            for field in adjoints
        ]
        if n > 0:
            across = [{t: coef.get("east_mix", t) * x[t] for t in rows} for coef, x in zip(coefs, to_east)]
            turned = [{t: west(x[t]) for t in rows} for x in across]
            along = [{t: coef.get("north_mix", t) * x[t] for t in x} for coef, x in zip(coefs, to_north)]
            following = []
            for j in group:
                field, flux = adjoints[j], along[j]
                new = {low - 1: flux[low - 1], high + 1: -flux[high]}
                for t in rows:
                    still = field[t] + column(field[t], coefs[j].get("column", t)) + (flux[t] - flux[t - 1])
                    new[t] = still + (across[j][t] - turned[j][t])
                following.append(new)
            adjoints = following
        for j in group:
            for total, steps, basis in (
                (east_total[j], to_east[j], base_steps[j][0]),
                (north_total[j], to_north[j], base_steps[j][1]),
            ):
                for t in steps:
                    term = steps[t] * basis[t]
                    total[t] = total[t] + term if t in total else term
    strip_shares = []
    east_sums = []
    none = jnp.zeros((1, LANES), jnp.float32)
    for j in group:
        east_sums.append(
            jnp.concatenate(
                [none]
                + [
                    jnp.sum(jnp.where(coefs[j].get("east_open", t), east_total[j][t], 0.0), axis=0, keepdims=True)
                    for t in range(-2, 6)
                ]
                + [none] * 7,
                axis=0,
            )
        )
    turned = [west(x) for x in east_sums]
    for j in group:
        north = {
            t: jnp.sum(jnp.where(coefs[j].get("north_open", t), north_total[j][t], 0.0), axis=0, keepdims=True)
            for t in range(-3, 6)
        }
        north[-4] = north[6] = none
        rows = [north[t] + north[t - 1] for t in range(-3, 7)] + [none] * 6
        strip_shares.append(-0.5 * (jnp.concatenate(rows, axis=0) + (east_sums[j] + turned[j])))
    share = jnp.concatenate([x[:, GHOST : LANES - GHOST] for x in strip_shares], axis=1)

    def take(order):
        return jnp.concatenate([share[t + 3 : t + 4] for t in order], axis=0)

    own_share[...] = share[3:7]
    far_share[...] = jnp.concatenate([take([-1, -2, -3]), jnp.zeros_like(share[:1])], axis=0)
    near_share[...] = jnp.concatenate([jnp.zeros_like(share[:1]), take([6, 5, 4])], axis=0)


def near_pairs(count):
    return [(i, i ^ 1) for i in range(count)]


def far_pairs(members, count):
    pairs = []
    for m in range(members):
        for i in range(1, count - 1, 2):
            pairs += [(m * count + i, m * count + i + 1), (m * count + i + 1, m * count + i)]
        for i in (0, count - 1):
            pairs.append((m * count + i, (m ^ 1) * count + i))
    return pairs


def routes(count):
    bits = count.bit_length() - 1
    groups = [[1]] if bits % 2 else []
    for bit in range(bits % 2, bits, 2):
        one, two = 1 << bit, 2 << bit
        groups.append([one + two, two, one] if bit == 0 else [one, one + two, two])
    return groups


def vmem(count):
    return [pl.BlockSpec(memory_space=pltpu.VMEM)] * count


def cost(nanoseconds):
    return pl.CostEstimate(flops=1153500 * nanoseconds, bytes_accessed=3690 * nanoseconds, transcendentals=0)


def body(tracer, diffusivity, direction, column_depth, density_class, band_of_row, weights):
    levels, rows, lon_count = tracer.shape
    strips = lon_count // OWN
    count = lax.axis_size("lat")
    members = lax.axis_size("members")
    params = pltpu.CompilerParams(vmem_limit_bytes=VMEM_LIMIT)
    f32, i32 = jnp.float32, jnp.int32
    halo = strips * STEPS * levels
    payload = halo + strips * 9

    def to_near(x):
        return lax.ppermute(x, "lat", near_pairs(count))

    def to_far(x):
        return lax.ppermute(x, ("members", "lat"), far_pairs(members, count))

    sizes = [b - a for a, b in zip(PIECES, PIECES[1:])]
    fields = (tracer, diffusivity, direction, column_depth)
    own, own_maps, near_out, *fars_out = pl.pallas_call(
        pack_fields,
        name="pack_fields",
        out_shape=(
            jax.ShapeDtypeStruct((strips, rows * levels, LANES), f32),
            jax.ShapeDtypeStruct((strips, 16, LANES), f32),
            jax.ShapeDtypeStruct((payload, LANES), f32),
        )
        + tuple(jax.ShapeDtypeStruct((payload // strips * size, LANES), f32) for size in sizes),
        in_specs=[pl.BlockSpec(memory_space=pltpu.HBM)] * 4,
        out_specs=tuple(vmem(3 + len(sizes))),
        scratch_shapes=[pltpu.VMEM(x.shape, x.dtype) for x in fields] + [pltpu.SemaphoreType.DMA((4,))],
        compiler_params=params,
    )(*[pltpu.with_memory_space_constraint(x, pltpu.HBM) for x in fields])
    fars = [to_far(x) for x in fars_out]
    near = to_near(near_out)

    own_classes, scales = pl.pallas_call(
        pack_classes,
        name="pack_classes",
        out_shape=(
            jax.ShapeDtypeStruct((strips, rows * levels, LANES), i32),
            jax.ShapeDtypeStruct((8, LANES), f32),
        ),
        in_specs=[pl.BlockSpec(memory_space=pltpu.HBM)] * 3,
        out_specs=tuple(vmem(2)),
        scratch_shapes=[
            pltpu.VMEM(density_class.shape, i32),
            pltpu.VMEM(weights.shape, f32),
            pltpu.SMEM(band_of_row.shape, i32),
            pltpu.SemaphoreType.DMA((3,)),
        ],
        compiler_params=params,
    )(*[pltpu.with_memory_space_constraint(x, pltpu.HBM) for x in (density_class, weights, band_of_row)])
    laters, sums = [], None
    gram_shape = (2, HIGH_COUNT * levels, 2 * LOW_COUNT * levels)
    for piece, size in enumerate(sizes):
        last = piece + 1 == len(sizes)
        given = [own, own_maps, near, fars[piece], own_classes]
        given += ([sums] if piece > 0 else []) + ([scales] if last else [])
        sums, later = pl.pallas_call(
            functools.partial(forward, piece),
            name="forward",
            out_shape=(
                jax.ShapeDtypeStruct((8, LANES) if last else gram_shape, f32),
                jax.ShapeDtypeStruct((size, 14 * levels, LANES), f32),
            ),
            in_specs=vmem(len(given)),
            out_specs=tuple(vmem(2)),
            cost_estimate=cost(2000),
            scratch_shapes=[pltpu.VMEM((size, 16 * MAP_FIELDS, LANES), f32)]
            + ([pltpu.VMEM(gram_shape, f32)] if last else []),
            compiler_params=params,
        )(*given)
        laters.append(later)

    gathered, shares = sums, None
    groups = routes(count)
    for i, group in enumerate(groups):
        others = [lax.ppermute(gathered, "lat", [(d, d ^ k) for d in range(count)]) for k in group]
        if i == 0:
            shares = pl.pallas_call(
                adjoint_part,
                name="adjoint_part",
                out_shape=(jax.ShapeDtypeStruct((rows, lon_count), f32),) * 3,
                in_specs=vmem(5 + 2 * len(sizes)),
                out_specs=tuple(vmem(3)),
                scratch_shapes=[pltpu.VMEM((strips, 16 * MAP_FIELDS, LANES), f32)],
                compiler_params=params,
            )(own, own_maps, near, own_classes, sums, *fars, *laters)
        pieces = [gathered] + others
        if i == 0:
            *pieces, own_share, near_share, far_share = lax.optimization_barrier((*pieces, *shares))
            near_share, far_share = to_near(near_share), to_far(far_share)
        if i + 1 < len(groups):
            gathered = jnp.concatenate(pieces, axis=0)
    binned, gradient = pl.pallas_call(
        finish,
        name="finish",
        out_shape=(
            jax.ShapeDtypeStruct((weights.shape[0] // count, weights.shape[1]), f32),
            jax.ShapeDtypeStruct((rows, lon_count), f32),
        ),
        in_specs=vmem(3 + len(pieces)),
        out_specs=tuple(vmem(2)),
        compiler_params=params,
    )(own_share, near_share, far_share, *pieces)
    return binned, gradient


def solution(mesh):
    placed = (
        P(None, ("members", "lat"), None),
        P("lat", None),
        P(("members", "lat"), None),
        P("lat", None),
        P(None, ("members", "lat"), None),
        P("lat"),
        P(),
    )
    return jax.shard_map(
        body,
        mesh=mesh,
        in_specs=placed,
        out_specs=(P(("members", "lat"), None), P(("members", "lat"), None)),
        check_vma=False,
    )
```

```python
import functools

import jax
import jax.numpy as jnp
from jax import lax
from jax.experimental import pallas as pl
from jax.experimental.pallas import tpu as pltpu
from jax.sharding import PartitionSpec as P

STEPS = 3
vertical_mix = 0.05

LANES = 128
GHOST = 4
OWN = LANES - 2 * GHOST
HIGH_COUNT = 9
LOW_COUNT = 8
LOW_SHIFT = 3
PIECES = (0, 7, 12)
NEAR_PIECES = (0, 4, 8, 12)
VMEM_LIMIT = 16 * 1024 * 1024


def strip_of(row, j, lon_count):
    first = OWN * j - GHOST
    last = first + LANES
    if first < 0:
        return jnp.concatenate([row[:, first + lon_count :], row[:, :last]], axis=1)
    if last > lon_count:
        return jnp.concatenate([row[:, first:], row[:, : last - lon_count]], axis=1)
    return row[:, first:last]


def piece_of(j, bounds=None):
    bounds = PIECES if bounds is None else bounds
    return max(p for p in range(len(bounds) - 1) if bounds[p] <= j)


def near_place(nears, j):
    piece = piece_of(j, NEAR_PIECES)
    first, last = NEAR_PIECES[piece : piece + 2]
    return nears[piece], j - first, last - first


def is_odd():
    return lax.rem(lax.axis_index("lat"), 2) == 1


def oriented(ref, t, odd):
    last = ref.shape[1] - 1
    order = level_order(ref.shape[0])
    up = jnp.concatenate([ref[k, t : t + 1, :] for k in order], axis=0)
    down = jnp.concatenate([ref[k, last - t : last - t + 1, :] for k in order], axis=0)
    return jnp.where(odd, down, up)


def bring(sources, held, arrived):
    copies = [pltpu.make_async_copy(a, b, arrived.at[i]) for i, (a, b) in enumerate(zip(sources, held))]
    for copy in copies:
        copy.start()
    for copy in copies:
        copy.wait()


def flipped_map(ref, odd):
    field = ref[...].astype(jnp.float32)
    flipped = jnp.concatenate([field[r : r + 1] for r in reversed(range(field.shape[0]))], axis=0)
    return jnp.where(odd, field, flipped), jnp.where(odd, flipped, field)


def fill_far(piece, far, held):
    tracer, maps = held[0], held[1:]
    levels, _, lon_count = tracer.shape
    odd = is_odd()
    group = range(PIECES[piece], PIECES[piece + 1])
    for t in range(STEPS):
        field = oriented(tracer, t, odd)
        for u, j in enumerate(group):
            at = (u * STEPS + STEPS - 1 - t) * levels
            far[at : at + levels, :] = strip_of(field, j, lon_count)
    for a, ref in enumerate(maps):
        down, _ = flipped_map(ref, odd)
        for u, j in enumerate(group):
            at = len(group) * STEPS * levels + (3 * u + a) * STEPS
            far[at : at + STEPS, :] = strip_of(down, j, lon_count)[1:]


def pack_first(*refs):
    sources, far, held, arrived = refs[:4], refs[4], refs[5:9], refs[9]
    bring(sources, held, arrived)
    fill_far(0, far, held)


def pack_fields(*refs):
    parts, near_parts = len(PIECES) - 2, len(NEAR_PIECES) - 1
    sources, (own, own_maps) = refs[:4], refs[4:6]
    nears, refs = refs[6 : 6 + near_parts], refs[6 + near_parts :]
    fars, held, arrived = refs[:parts], refs[parts : 4 + parts], refs[4 + parts]
    bring(sources, held, arrived)
    tracer = held[0]
    levels, rows, lon_count = tracer.shape
    strips = lon_count // OWN
    odd = is_odd()
    for i, far in enumerate(fars):
        fill_far(i + 1, far, held)
    for t in range(rows):
        field = oriented(tracer, t, odd)
        for j in range(strips):
            strip = strip_of(field, j, lon_count)
            own[j, t * levels : (t + 1) * levels, :] = strip
            if t > 0:
                near, local, _ = near_place(nears, j)
                at = (local * STEPS + rows - 1 - t) * levels
                near[at : at + levels, :] = strip
    for a, ref in enumerate(held[1:]):
        down, up = flipped_map(ref, odd)
        for j in range(strips):
            own_maps[j, a * 4 : a * 4 + 4, :] = strip_of(up, j, lon_count)
            near, local, count = near_place(nears, j)
            at = count * STEPS * levels + (3 * local + a) * STEPS
            near[at : at + STEPS, :] = strip_of(down, j, lon_count)[:STEPS]
    own_maps[:, 12:, :] = jnp.zeros_like(own_maps[:, 12:, :])


def pack_classes(*refs):
    sources, (own, scales), held, arrived = refs[:3], refs[3:5], refs[5:8], refs[8]
    bring(sources, held, arrived)
    classes, weights, band_of_row = held
    levels, rows, lon_count = classes.shape
    strips = lon_count // OWN
    odd = is_odd()
    for t in range(rows):
        field = oriented(classes, t, odd)
        for j in range(strips):
            strip = strip_of(field, j, lon_count)
            own[j, t * levels : (t + 1) * levels, :] = strip
    class_count = weights.shape[1]
    label = lax.broadcasted_iota(jnp.int32, (1, LANES), 1)
    scale_rows, band_rows = [], []
    for pair in range(2):
        band = band_of_row[jnp.where(odd, 3 - 2 * pair, 2 * pair)]
        scale = weights[pl.ds(band, 1), :]
        scale_rows.append(jnp.concatenate([scale, jnp.zeros((1, LANES - class_count), jnp.float32)], axis=1))
        band_rows.append(jnp.where(label == LANES - 1, band.astype(jnp.float32), 0.0))
    blank = jnp.zeros((2, LANES), jnp.float32)
    scales[...] = jnp.concatenate(scale_rows + [blank] + band_rows + [blank], axis=0)


def east(x):
    return pltpu.roll(x, LANES - 1, 1)


def west(x):
    return pltpu.roll(x, 1, 1)


MAP_FIELDS = 7


def level_order(levels):
    half = levels // 2
    return [2 * (i % half) + i // half for i in range(levels)]


class Coefficients:
    blocks = {
        "wet": 0, "east_open": 1, "north_open": 2,
        "east_mix": 3, "north_mix": 4, "east_dir": 5, "north_dir": 6,
    }

    def __init__(self, maps, j, levels):
        order = lax.broadcasted_iota(jnp.int32, (levels, LANES), 0)
        half = levels // 2
        self.level = (2 * (order & (half - 1)) + jnp.where(order < half, 0, 1)).astype(jnp.float32)
        self.levels = levels
        self.maps = maps
        self.j = j
        self.cache = {}

    def row(self, kind, t):
        at = 16 * self.blocks[kind] + t + STEPS
        return jnp.broadcast_to(self.maps[self.j, at : at + 1, :], (self.levels, LANES))

    def get(self, kind, t):
        if (kind, t) not in self.cache:
            side, _, what = kind.partition("_")
            if kind == "column":
                value = jnp.where(self.level + 1.0 < self.row("wet", t), vertical_mix, 0.0)
            elif kind == "wet" or what == "open":
                value = self.level < self.row(kind, t)
            else:
                value = jnp.where(self.get(side + "_open", t), self.row(kind, t), 0.0)
            self.cache[kind, t] = value
        return self.cache[kind, t]


def column(field, coefficient):
    half = field.shape[0] // 2
    even, odd = field[:half], field[half:]
    after_even = coefficient[:half] * (odd - even)
    after_odd = coefficient[half:] * (pltpu.roll(even, half - 1, 0) - odd)
    return jnp.concatenate([after_even - pltpu.roll(after_odd, 1, 0), after_odd - after_even], axis=0)


def gaps(fields, rows):
    turned = [{t: east(field[t]) for t in rows} for field in fields]
    to_east = [{t: turn[t] - field[t] for t in rows} for turn, field in zip(turned, fields)]
    faces = range(rows[0] - 1, rows[-1] + 1)
    to_north = [{t: field[t + 1] - field[t] for t in faces} for field in fields]
    return list(zip(to_east, to_north))


def fluxes(coefs, kind, steps):
    return [
        (
            {t: coef.get("east_" + kind, t) * to_east[t] for t in to_east},
            {t: coef.get("north_" + kind, t) * to_north[t] for t in to_north},
        )
        for coef, (to_east, to_north) in zip(coefs, steps)
    ]


def both(ones, others):
    return [
        tuple({t: a[t] + b[t] for t in a} for a, b in zip(one, other)) for one, other in zip(ones, others)
    ]


def gathered_in(flux, rows, fields=None, coefs=None):
    turned = [{t: west(across[t]) for t in rows} for across, _ in flux]
    still = [{t: along[t] - along[t - 1] for t in rows} for _, along in flux]
    if fields is not None:
        still = [
            {t: rest[t] + (field[t] + column(field[t], coef.get("column", t))) for t in rows}
            for rest, field, coef in zip(still, fields, coefs)
        ]
    return [
        {t: rest[t] + (across[t] - turn[t]) for t in rows}
        for rest, (across, _), turn in zip(still, flux, turned)
    ]


def face_maps(own_maps, nears, fars, maps, strips, levels):
    count, edge = lax.axis_size("lat"), lax.axis_index("lat")
    keep = jnp.where(jnp.logical_and(edge != 0, edge != count - 1), 1.0, 0.0)

    def north(x):
        return pltpu.roll(x, 15, 0)

    for i, j in enumerate(strips):
        whole = []
        piece = piece_of(j)
        for a in range(3):
            at = (PIECES[piece + 1] - PIECES[piece]) * STEPS * levels + (3 * (j - PIECES[piece]) + a) * STEPS
            low = fars[piece][at : at + STEPS, :]
            if a == 2:
                low = low * keep
            near, local, size = near_place(nears, j)
            at = size * STEPS * levels + (3 * local + a) * STEPS
            high = near[at : at + STEPS, :]
            whole.append(jnp.concatenate([low, own_maps[j, 4 * a : 4 * a + 4, :], high, high, high], axis=0))
        mix, heading, depth = whole
        blocks = [depth] + [jnp.minimum(depth, f(depth)) for f in (east, north)]
        blocks += [0.5 * (x + f(x)) for x in (mix, heading) for f in (east, north)]
        for b, block in enumerate(blocks):
            maps[i, 16 * b : 16 * b + 16, :] = block


def class_hits(value, label, levels):
    top = value.astype(jnp.bfloat16)
    bottom = (value - top.astype(jnp.float32)).astype(jnp.bfloat16)
    high = (label >> LOW_SHIFT).astype(jnp.float32).astype(jnp.bfloat16)
    low = (label & (LOW_COUNT - 1)).astype(jnp.float32).astype(jnp.bfloat16)
    none = jnp.zeros((levels, LANES), jnp.bfloat16)
    one = jnp.ones((levels, LANES), jnp.bfloat16)
    left = [jnp.where(high == jnp.bfloat16(h), one, none) for h in range(HIGH_COUNT)]
    picks = [low == jnp.bfloat16(l) for l in range(LOW_COUNT)]
    right = [jnp.where(p, part, none) for part in (top, bottom) for p in picks]
    return jnp.concatenate(left, axis=0), jnp.concatenate(right, axis=0)


def later_row(n, t):
    return (n - 1) * 8 + t + STEPS - n


def forward(piece, *refs):
    last = piece + 2 == len(PIECES)
    refs = list(refs)
    near_parts = len(NEAR_PIECES) - 1
    own, own_maps, far, classes = refs[:4]
    nears = refs[4 : 4 + near_parts]
    del refs[: 4 + near_parts]
    before = refs.pop(0) if piece > 0 else None
    scales = refs.pop(0) if last else None
    out, later = refs[:2]
    weighted, maps, grams = refs[2:] if last else (None, refs[2], out)
    levels = own.shape[1] // 4
    group = list(range(PIECES[piece], PIECES[piece + 1]))
    face_maps(own_maps, nears, {piece: far}, maps, group, levels)
    lane = lax.broadcasted_iota(jnp.int32, (levels, LANES), 1)
    inner = jnp.logical_and(lane >= GHOST, lane < LANES - GHOST)
    coefs = [Coefficients(maps, u, levels) for u in range(len(group))]
    fields, tangents = [], None
    for u, j in enumerate(group):
        field = {t: own[j, t * levels : (t + 1) * levels, :] for t in range(4)}
        for s in range(STEPS):
            at = (u * STEPS + s) * levels
            field[s - STEPS] = far[at : at + levels, :]
            near, local, _ = near_place(nears, j)
            at = (local * STEPS + s) * levels
            field[4 + s] = near[at : at + levels, :]
        fields.append(field)
    for n in range(STEPS):
        rows = list(range(n + 1 - STEPS, 4 + STEPS - n - 1))
        steps = gaps(fields, rows)
        push = fluxes(coefs, "dir", steps)
        if n == 0:
            following = gathered_in(push, rows)
        else:
            push = both(push, fluxes(coefs, "mix", gaps(tangents, rows)))
            following = gathered_in(push, rows, tangents, coefs)
        tangents = following
        if n + 1 < STEPS:
            fields = gathered_in(fluxes(coefs, "mix", steps), rows, fields, coefs)
            for u in range(len(group)):
                for t in rows:
                    at = later_row(n + 1, t) * levels
                    later[u, at : at + levels, :] = fields[u][t]
    for pair in range(2):
        lefts, rights = [], []
        for u, j in enumerate(group):
            for t in (2 * pair, 2 * pair + 1):
                chosen = jnp.logical_and(inner, coefs[u].get("wet", t))
                value = jnp.where(chosen, tangents[u][t], 0.0)
                left, right = class_hits(value, classes[j, t * levels : (t + 1) * levels, :], levels)
                lefts.append(left)
                rights.append(right)
        gram = lax.dot_general(
            jnp.concatenate(lefts, axis=1),
            jnp.concatenate(rights, axis=1),
            (((1,), (1,)), ((), ())),
            preferred_element_type=jnp.float32,
        )
        grams[pair] = gram if before is None else before[pair] + gram
    if last:
        class_sums(grams, scales, out, weighted, levels)


def class_sums(grams, scales, sums, weighted, levels):
    width = 2 * LOW_COUNT * levels
    own_level = lax.broadcasted_iota(jnp.int32, (levels, width), 0)
    other_level = lax.broadcasted_iota(jnp.int32, (levels, width), 1) & (levels - 1)
    diagonal = own_level == other_level
    sheets = []
    for pair in range(2):
        for h in range(HIGH_COUNT):
            sheet = jnp.where(diagonal, grams[pair, h * levels : (h + 1) * levels, :], 0.0)
            sheets.append(jnp.sum(sheet, axis=0, keepdims=True))
        sheets.append(jnp.zeros((16 - HIGH_COUNT, width), jnp.float32))
    rest = jnp.concatenate(sheets, axis=0)
    parts = []
    for _ in range(3):
        part = rest.astype(jnp.bfloat16)
        rest = rest - part.astype(jnp.float32)
        parts.append(part)
    at_low = (lax.broadcasted_iota(jnp.int32, (width, LANES), 0) >> (levels.bit_length() - 1)) & (LOW_COUNT - 1)
    of_low = lax.broadcasted_iota(jnp.int32, (width, LANES), 1) & (LOW_COUNT - 1)
    gather = jnp.where(at_low == of_low, 1.0, 0.0).astype(jnp.bfloat16)
    added = jnp.dot(jnp.concatenate(parts, axis=0), gather, preferred_element_type=jnp.float32)
    added = (added[64:96] + added[32:64]) + added[0:32]
    here = lax.broadcasted_iota(jnp.int32, (16, LANES), 0)
    label = lax.broadcasted_iota(jnp.int32, (16, LANES), 1)
    totals = [
        jnp.sum(
            jnp.where(here == (label >> LOW_SHIFT), added[16 * p : 16 * p + 16], 0.0), axis=0, keepdims=True
        )
        for p in range(2)
    ]
    finish_sums(scales, totals, sums, weighted)


def finish_sums(scales, totals, sums, weighted):
    sums[...] = jnp.concatenate([totals[p] + scales[4 + p : 5 + p, :] for p in range(2)], axis=0)
    weighted[0:2, :] = jnp.concatenate([scales[p : p + 1, :] * totals[p] for p in range(2)], axis=0)


def finish(own_share, near_share, far_share, *refs):
    pieces, binned, gradient = refs[:-2], refs[-2], refs[-1]
    up = own_share[...] + (near_share[...] + far_share[...])
    down = jnp.concatenate([up[t : t + 1] for t in reversed(range(up.shape[0]))], axis=0)
    gradient[...] = jnp.where(is_odd(), down, up)
    band_own, class_count = binned.shape
    first = lax.axis_index("lat") * band_own
    found = [jnp.zeros((1, LANES), jnp.float32) for _ in range(band_own)]
    for piece in pieces:
        totals = piece[...]
        bands = jnp.broadcast_to(totals[:, LANES - 1 :], totals.shape)
        for m in range(band_own):
            hit = jnp.where(bands == (first + m).astype(jnp.float32), totals, 0.0)
            found[m] = found[m] + jnp.sum(hit, axis=0, keepdims=True)
    whole = jnp.concatenate(found, axis=0)
    binned[...] = whole[:, :class_count]


def adjoint_part(own, own_maps, classes, weighted, *refs):
    parts = len(PIECES) - 1
    near_parts = len(NEAR_PIECES) - 1
    nears, refs = refs[:near_parts], refs[near_parts:]
    fars, laters = refs[:parts], refs[parts : 2 * parts]
    own_share, near_share, far_share, maps = refs[2 * parts :]
    strips = own.shape[0]
    levels = own.shape[1] // 4
    group = list(range(strips))
    face_maps(own_maps, nears, fars, maps, group, levels)
    coefs = [Coefficients(maps, j, levels) for j in group]
    adjoints = []
    for j in group:
        adjoint = {}
        for t in range(4):
            label = classes[j, t * levels : (t + 1) * levels, :]
            row = t // 2
            table = jnp.broadcast_to(weighted[row : row + 1, :], (8, LANES))
            value = jnp.concatenate(
                [jnp.take_along_axis(table, label[k : k + 8, :], axis=1) for k in range(0, levels, 8)], axis=0
            )
            adjoint[t] = jnp.where(coefs[j].get("wet", t), value, 0.0)
        adjoints.append(adjoint)

    def base(n, j):
        piece = piece_of(j)
        local = j - PIECES[piece]
        field = {}
        for t in range(n - STEPS, 4 + STEPS - n):
            if n > 0:
                at = later_row(n, t) * levels
                field[t] = laters[piece][local, at : at + levels, :]
            elif t < 0:
                at = (local * STEPS + t + STEPS) * levels
                field[t] = fars[piece][at : at + levels, :]
            elif t < 4:
                field[t] = own[j, t * levels : (t + 1) * levels, :]
            else:
                near, place, _ = near_place(nears, j)
                at = (place * STEPS + t - 4) * levels
                field[t] = near[at : at + levels, :]
        return field

    east_total = [{} for _ in group]
    north_total = [{} for _ in group]
    for n in reversed(range(STEPS)):
        rows = list(range(n + 1 - STEPS, 3 + STEPS - n))
        low, high = rows[0], rows[-1]
        turned = [{t: east(field[t]) for t in rows} for field in adjoints]
        base_steps = gaps([base(n, j) for j in group], rows)
        to_east = [{t: turn[t] - field[t] for t in rows} for turn, field in zip(turned, adjoints)]
        to_north = [
            {low - 1: field[low], high: -field[high], **{t: field[t + 1] - field[t] for t in rows[:-1]}}
            for field in adjoints
        ]
        if n > 0:
            across = [{t: coef.get("east_mix", t) * x[t] for t in rows} for coef, x in zip(coefs, to_east)]
            turned = [{t: west(x[t]) for t in rows} for x in across]
            along = [{t: coef.get("north_mix", t) * x[t] for t in x} for coef, x in zip(coefs, to_north)]
            following = []
            for j in group:
                field, flux = adjoints[j], along[j]
                new = {low - 1: flux[low - 1], high + 1: -flux[high]}
                for t in rows:
                    still = field[t] + column(field[t], coefs[j].get("column", t)) + (flux[t] - flux[t - 1])
                    new[t] = still + (across[j][t] - turned[j][t])
                following.append(new)
            adjoints = following
        for j in group:
            for total, steps, basis in (
                (east_total[j], to_east[j], base_steps[j][0]),
                (north_total[j], to_north[j], base_steps[j][1]),
            ):
                for t in steps:
                    term = steps[t] * basis[t]
                    total[t] = total[t] + term if t in total else term
    strip_shares = []
    east_sums = []
    none = jnp.zeros((1, LANES), jnp.float32)
    for j in group:
        east_sums.append(
            jnp.concatenate(
                [none]
                + [
                    jnp.sum(jnp.where(coefs[j].get("east_open", t), east_total[j][t], 0.0), axis=0, keepdims=True)
                    for t in range(-2, 6)
                ]
                + [none] * 7,
                axis=0,
            )
        )
    turned = [west(x) for x in east_sums]
    for j in group:
        north = {
            t: jnp.sum(jnp.where(coefs[j].get("north_open", t), north_total[j][t], 0.0), axis=0, keepdims=True)
            for t in range(-3, 6)
        }
        north[-4] = north[6] = none
        rows = [north[t] + north[t - 1] for t in range(-3, 7)] + [none] * 6
        strip_shares.append(-0.5 * (jnp.concatenate(rows, axis=0) + (east_sums[j] + turned[j])))
    share = jnp.concatenate([x[:, GHOST : LANES - GHOST] for x in strip_shares], axis=1)

    def take(order):
        return jnp.concatenate([share[t + 3 : t + 4] for t in order], axis=0)

    own_share[...] = share[3:7]
    far_share[...] = jnp.concatenate([take([-1, -2, -3]), jnp.zeros_like(share[:1])], axis=0)
    near_share[...] = jnp.concatenate([jnp.zeros_like(share[:1]), take([6, 5, 4])], axis=0)


def near_pairs(count):
    return [(i, i ^ 1) for i in range(count)]


def far_pairs(members, count):
    pairs = []
    for m in range(members):
        for i in range(1, count - 1, 2):
            pairs += [(m * count + i, m * count + i + 1), (m * count + i + 1, m * count + i)]
        for i in (0, count - 1):
            pairs.append((m * count + i, (m ^ 1) * count + i))
    return pairs


def routes(count):
    bits = count.bit_length() - 1
    groups = [[1]] if bits % 2 else []
    for bit in range(bits % 2, bits, 2):
        one, two = 1 << bit, 2 << bit
        groups.append([one + two, two, one] if bit == 0 else [one, one + two, two])
    return groups


def vmem(count):
    return [pl.BlockSpec(memory_space=pltpu.VMEM)] * count


def cost(nanoseconds):
    return pl.CostEstimate(flops=1153500 * nanoseconds, bytes_accessed=3690 * nanoseconds, transcendentals=0)


def body(tracer, diffusivity, direction, column_depth, density_class, band_of_row, weights):
    levels, rows, lon_count = tracer.shape
    strips = lon_count // OWN
    count = lax.axis_size("lat")
    members = lax.axis_size("members")
    params = pltpu.CompilerParams(vmem_limit_bytes=VMEM_LIMIT)
    f32, i32 = jnp.float32, jnp.int32
    halo = strips * STEPS * levels
    payload = halo + strips * 9

    def to_near(x):
        return lax.ppermute(x, "lat", near_pairs(count))

    def to_far(x):
        return lax.ppermute(x, ("members", "lat"), far_pairs(members, count))

    sizes = [b - a for a, b in zip(PIECES, PIECES[1:])]
    near_sizes = [b - a for a, b in zip(NEAR_PIECES, NEAR_PIECES[1:])]
    fields = (tracer, diffusivity, direction, column_depth)
    in_place = [pltpu.with_memory_space_constraint(x, pltpu.HBM) for x in fields]
    taken = dict(
        in_specs=[pl.BlockSpec(memory_space=pltpu.HBM)] * 4,
        scratch_shapes=[pltpu.VMEM(x.shape, x.dtype) for x in fields] + [pltpu.SemaphoreType.DMA((4,))],
        compiler_params=params,
    )
    far_shapes = [jax.ShapeDtypeStruct((payload // strips * size, LANES), f32) for size in sizes]
    first_out = pl.pallas_call(
        pack_first,
        name="pack_first",
        out_shape=far_shapes[0],
        out_specs=pl.BlockSpec(memory_space=pltpu.VMEM),
        **taken,
    )(*in_place)
    fars = [to_far(first_out)]
    late_fields = lax.optimization_barrier((*fields, first_out))[: len(fields)]
    in_place = [pltpu.with_memory_space_constraint(x, pltpu.HBM) for x in late_fields]
    own, own_maps, *outs = pl.pallas_call(
        pack_fields,
        name="pack_fields",
        out_shape=(
            jax.ShapeDtypeStruct((strips, rows * levels, LANES), f32),
            jax.ShapeDtypeStruct((strips, 16, LANES), f32),
            *[jax.ShapeDtypeStruct((payload // strips * size, LANES), f32) for size in near_sizes],
            *far_shapes[1:],
        ),
        out_specs=tuple(vmem(1 + len(near_sizes) + len(sizes))),
        **taken,
    )(*in_place)
    nears = [to_near(x) for x in outs[: len(near_sizes)]]
    fars += [to_far(x) for x in outs[len(near_sizes) :]]

    own_classes, scales = pl.pallas_call(
        pack_classes,
        name="pack_classes",
        out_shape=(
            jax.ShapeDtypeStruct((strips, rows * levels, LANES), i32),
            jax.ShapeDtypeStruct((8, LANES), f32),
        ),
        in_specs=[pl.BlockSpec(memory_space=pltpu.HBM)] * 3,
        out_specs=tuple(vmem(2)),
        scratch_shapes=[
            pltpu.VMEM(density_class.shape, i32),
            pltpu.VMEM(weights.shape, f32),
            pltpu.SMEM(band_of_row.shape, i32),
            pltpu.SemaphoreType.DMA((3,)),
        ],
        compiler_params=params,
    )(*[pltpu.with_memory_space_constraint(x, pltpu.HBM) for x in (density_class, weights, band_of_row)])
    laters, sums = [], None
    gram_shape = (2, HIGH_COUNT * levels, 2 * LOW_COUNT * levels)
    for piece, size in enumerate(sizes):
        last = piece + 1 == len(sizes)
        given = [own, own_maps, fars[piece], own_classes, *nears]
        given += ([sums] if piece > 0 else []) + ([scales] if last else [])
        sums, later, *weighted = pl.pallas_call(
            functools.partial(forward, piece),
            name="forward",
            out_shape=(
                jax.ShapeDtypeStruct((2, LANES) if last else gram_shape, f32),
                jax.ShapeDtypeStruct((size, 14 * levels, LANES), f32),
            )
            + ((jax.ShapeDtypeStruct((8, LANES), f32),) if last else ()),
            in_specs=vmem(len(given)),
            out_specs=tuple(vmem(3 if last else 2)),
            cost_estimate=cost(2000),
            scratch_shapes=[pltpu.VMEM((size, 16 * MAP_FIELDS, LANES), f32)]
            + ([pltpu.VMEM(gram_shape, f32)] if last else []),
            compiler_params=params,
        )(*given)
        laters.append(later)

    gathered, shares = sums, None
    groups = routes(count)
    for i, group in enumerate(groups):
        others = [lax.ppermute(gathered, "lat", [(d, d ^ k) for d in range(count)]) for k in group]
        if i == 0:
            shares = pl.pallas_call(
                adjoint_part,
                name="adjoint_part",
                out_shape=(jax.ShapeDtypeStruct((rows, lon_count), f32),) * 3,
                in_specs=vmem(4 + len(nears) + 2 * len(sizes)),
                out_specs=tuple(vmem(3)),
                scratch_shapes=[pltpu.VMEM((strips, 16 * MAP_FIELDS, LANES), f32)],
                compiler_params=params,
            )(own, own_maps, own_classes, weighted[0], *nears, *fars, *laters)
        pieces = [gathered] + others
        if i == 0:
            *pieces, own_share, near_share, far_share = lax.optimization_barrier((*pieces, *shares))
            near_share, far_share = to_near(near_share), to_far(far_share)
        if i + 1 < len(groups):
            gathered = jnp.concatenate(pieces, axis=0)
    binned, gradient = pl.pallas_call(
        finish,
        name="finish",
        out_shape=(
            jax.ShapeDtypeStruct((weights.shape[0] // count, weights.shape[1]), f32),
            jax.ShapeDtypeStruct((rows, lon_count), f32),
        ),
        in_specs=vmem(3 + len(pieces)),
        out_specs=tuple(vmem(2)),
        compiler_params=params,
    )(own_share, near_share, far_share, *pieces)
    return binned, gradient


def solution(mesh):
    placed = (
        P(None, ("members", "lat"), None),
        P("lat", None),
        P(("members", "lat"), None),
        P("lat", None),
        P(None, ("members", "lat"), None),
        P("lat"),
        P(),
    )
    return jax.shard_map(
        body,
        mesh=mesh,
        in_specs=placed,
        out_specs=(P(("members", "lat"), None), P(("members", "lat"), None)),
        check_vma=False,
    )
```

```python
import functools

import jax
import jax.numpy as jnp
from jax import lax
from jax.experimental import pallas as pl
from jax.experimental.pallas import tpu as pltpu
from jax.sharding import PartitionSpec as P

STEPS = 3
vertical_mix = 0.05

LANES = 128
GHOST = 4
OWN = LANES - 2 * GHOST
HIGH_COUNT = 9
LOW_COUNT = 8
LOW_SHIFT = 3
PIECES = (0, 7, 12)
NEAR_PIECES = (0, 4, 8, 12)
VMEM_LIMIT = 16 * 1024 * 1024


def strip_of(row, j, lon_count):
    first = OWN * j - GHOST
    last = first + LANES
    if first < 0:
        return jnp.concatenate([row[:, first + lon_count :], row[:, :last]], axis=1)
    if last > lon_count:
        return jnp.concatenate([row[:, first:], row[:, : last - lon_count]], axis=1)
    return row[:, first:last]


def piece_of(j, bounds=None):
    bounds = PIECES if bounds is None else bounds
    return max(p for p in range(len(bounds) - 1) if bounds[p] <= j)


def near_place(nears, j):
    piece = piece_of(j, NEAR_PIECES)
    first, last = NEAR_PIECES[piece : piece + 2]
    return nears[piece], j - first, last - first


def is_odd():
    return lax.rem(lax.axis_index("lat"), 2) == 1


def oriented(ref, t, odd):
    last = ref.shape[1] - 1
    order = level_order(ref.shape[0])
    up = jnp.concatenate([ref[k, t : t + 1, :] for k in order], axis=0)
    down = jnp.concatenate([ref[k, last - t : last - t + 1, :] for k in order], axis=0)
    return jnp.where(odd, down, up)


def bring(sources, held, arrived):
    copies = [pltpu.make_async_copy(a, b, arrived.at[i]) for i, (a, b) in enumerate(zip(sources, held))]
    for copy in copies:
        copy.start()
    for copy in copies:
        copy.wait()


def flipped_map(ref, odd):
    field = ref[...].astype(jnp.float32)
    flipped = jnp.concatenate([field[r : r + 1] for r in reversed(range(field.shape[0]))], axis=0)
    return jnp.where(odd, field, flipped), jnp.where(odd, flipped, field)


def fill_far(piece, far, held):
    tracer, maps = held[0], held[1:]
    levels, _, lon_count = tracer.shape
    odd = is_odd()
    group = range(PIECES[piece], PIECES[piece + 1])
    for t in range(STEPS):
        field = oriented(tracer, t, odd)
        for u, j in enumerate(group):
            at = (u * STEPS + STEPS - 1 - t) * levels
            far[at : at + levels, :] = strip_of(field, j, lon_count)
    for a, ref in enumerate(maps):
        down, _ = flipped_map(ref, odd)
        for u, j in enumerate(group):
            at = len(group) * STEPS * levels + (3 * u + a) * STEPS
            far[at : at + STEPS, :] = strip_of(down, j, lon_count)[1:]


def pack_first(*refs):
    sources, far, held, arrived = refs[:4], refs[4], refs[5:9], refs[9]
    bring(sources, held, arrived)
    fill_far(0, far, held)


def pack_fields(*refs):
    parts, near_parts = len(PIECES) - 2, len(NEAR_PIECES) - 1
    sources, (own, own_maps) = refs[:4], refs[4:6]
    nears, refs = refs[6 : 6 + near_parts], refs[6 + near_parts :]
    fars, held, arrived = refs[:parts], refs[parts : 4 + parts], refs[4 + parts]
    bring(sources, held, arrived)
    tracer = held[0]
    levels, rows, lon_count = tracer.shape
    strips = lon_count // OWN
    odd = is_odd()
    for i, far in enumerate(fars):
        fill_far(i + 1, far, held)
    for t in range(rows):
        field = oriented(tracer, t, odd)
        for j in range(strips):
            strip = strip_of(field, j, lon_count)
            own[j, t * levels : (t + 1) * levels, :] = strip
            if t > 0:
                near, local, _ = near_place(nears, j)
                at = (local * STEPS + rows - 1 - t) * levels
                near[at : at + levels, :] = strip
    for a, ref in enumerate(held[1:]):
        down, up = flipped_map(ref, odd)
        for j in range(strips):
            own_maps[j, a * 4 : a * 4 + 4, :] = strip_of(up, j, lon_count)
            near, local, count = near_place(nears, j)
            at = count * STEPS * levels + (3 * local + a) * STEPS
            near[at : at + STEPS, :] = strip_of(down, j, lon_count)[:STEPS]
    own_maps[:, 12:, :] = jnp.zeros_like(own_maps[:, 12:, :])


def pack_classes(*refs):
    sources, (own, scales), held, arrived = refs[:3], refs[3:5], refs[5:8], refs[8]
    bring(sources, held, arrived)
    classes, weights, band_of_row = held
    levels, rows, lon_count = classes.shape
    strips = lon_count // OWN
    odd = is_odd()
    for t in range(rows):
        field = oriented(classes, t, odd)
        for j in range(strips):
            strip = strip_of(field, j, lon_count)
            own[j, t * levels : (t + 1) * levels, :] = strip
    class_count = weights.shape[1]
    label = lax.broadcasted_iota(jnp.int32, (1, LANES), 1)
    scale_rows, band_rows = [], []
    for pair in range(2):
        band = band_of_row[jnp.where(odd, 3 - 2 * pair, 2 * pair)]
        scale = weights[pl.ds(band, 1), :]
        scale_rows.append(jnp.concatenate([scale, jnp.zeros((1, LANES - class_count), jnp.float32)], axis=1))
        band_rows.append(jnp.where(label == LANES - 1, band.astype(jnp.float32), 0.0))
    blank = jnp.zeros((2, LANES), jnp.float32)
    scales[...] = jnp.concatenate(scale_rows + [blank] + band_rows + [blank], axis=0)


def east(x):
    return pltpu.roll(x, LANES - 1, 1)


def west(x):
    return pltpu.roll(x, 1, 1)


MAP_FIELDS = 7


def level_order(levels):
    half = levels // 2
    return [2 * (i % half) + i // half for i in range(levels)]


class Coefficients:
    blocks = {
        "wet": 0, "east_open": 1, "north_open": 2,
        "east_mix": 3, "north_mix": 4, "east_dir": 5, "north_dir": 6,
    }

    def __init__(self, maps, j, levels):
        order = lax.broadcasted_iota(jnp.int32, (levels, LANES), 0)
        half = levels // 2
        self.level = (2 * (order & (half - 1)) + jnp.where(order < half, 0, 1)).astype(jnp.float32)
        self.levels = levels
        self.maps = maps
        self.j = j
        self.cache = {}

    def row(self, kind, t):
        at = 16 * self.blocks[kind] + t + STEPS
        return jnp.broadcast_to(self.maps[self.j, at : at + 1, :], (self.levels, LANES))

    def get(self, kind, t):
        if (kind, t) not in self.cache:
            side, _, what = kind.partition("_")
            if kind == "column":
                value = jnp.where(self.level + 1.0 < self.row("wet", t), vertical_mix, 0.0)
            elif kind == "wet" or what == "open":
                value = self.level < self.row(kind, t)
            else:
                value = jnp.where(self.get(side + "_open", t), self.row(kind, t), 0.0)
            self.cache[kind, t] = value
        return self.cache[kind, t]


def column(field, coefficient):
    half = field.shape[0] // 2
    even, odd = field[:half], field[half:]
    after_even = coefficient[:half] * (odd - even)
    after_odd = coefficient[half:] * (pltpu.roll(even, half - 1, 0) - odd)
    return jnp.concatenate([after_even - pltpu.roll(after_odd, 1, 0), after_odd - after_even], axis=0)


def gaps(fields, rows):
    turned = [{t: east(field[t]) for t in rows} for field in fields]
    to_east = [{t: turn[t] - field[t] for t in rows} for turn, field in zip(turned, fields)]
    faces = range(rows[0] - 1, rows[-1] + 1)
    to_north = [{t: field[t + 1] - field[t] for t in faces} for field in fields]
    return list(zip(to_east, to_north))


def fluxes(coefs, kind, steps):
    return [
        (
            {t: coef.get("east_" + kind, t) * to_east[t] for t in to_east},
            {t: coef.get("north_" + kind, t) * to_north[t] for t in to_north},
        )
        for coef, (to_east, to_north) in zip(coefs, steps)
    ]


def both(ones, others):
    return [
        tuple({t: a[t] + b[t] for t in a} for a, b in zip(one, other)) for one, other in zip(ones, others)
    ]


def gathered_in(flux, rows, fields=None, coefs=None):
    turned = [{t: west(across[t]) for t in rows} for across, _ in flux]
    still = [{t: along[t] - along[t - 1] for t in rows} for _, along in flux]
    if fields is not None:
        still = [
            {t: rest[t] + (field[t] + column(field[t], coef.get("column", t))) for t in rows}
            for rest, field, coef in zip(still, fields, coefs)
        ]
    return [
        {t: rest[t] + (across[t] - turn[t]) for t in rows}
        for rest, (across, _), turn in zip(still, flux, turned)
    ]


def face_maps(own_maps, nears, fars, maps, strips, levels, kinds=3):
    count, edge = lax.axis_size("lat"), lax.axis_index("lat")
    keep = jnp.where(jnp.logical_and(edge != 0, edge != count - 1), 1.0, 0.0)

    def north(x):
        return pltpu.roll(x, 15, 0)

    for i, j in enumerate(strips):
        whole = []
        piece = piece_of(j)
        for a in range(3 - kinds, 3):
            at = (PIECES[piece + 1] - PIECES[piece]) * STEPS * levels + (3 * (j - PIECES[piece]) + a) * STEPS
            low = fars[piece][at : at + STEPS, :]
            if a == 2:
                low = low * keep
            near, local, size = near_place(nears, j)
            at = size * STEPS * levels + (3 * local + a) * STEPS
            high = near[at : at + STEPS, :]
            whole.append(jnp.concatenate([low, own_maps[j, 4 * a : 4 * a + 4, :], high, high, high], axis=0))
        depth = whole.pop()
        blocks = [depth] + [jnp.minimum(depth, f(depth)) for f in (east, north)]
        blocks += [0.5 * (x + f(x)) for x in whole for f in (east, north)]
        for b, block in enumerate(blocks):
            maps[i, 16 * b : 16 * b + 16, :] = block


def class_hits(value, label, levels):
    top = value.astype(jnp.bfloat16)
    bottom = (value - top.astype(jnp.float32)).astype(jnp.bfloat16)
    high = (label >> LOW_SHIFT).astype(jnp.float32).astype(jnp.bfloat16)
    low = (label & (LOW_COUNT - 1)).astype(jnp.float32).astype(jnp.bfloat16)
    none = jnp.zeros((levels, LANES), jnp.bfloat16)
    one = jnp.ones((levels, LANES), jnp.bfloat16)
    left = [jnp.where(high == jnp.bfloat16(h), one, none) for h in range(HIGH_COUNT)]
    picks = [low == jnp.bfloat16(l) for l in range(LOW_COUNT)]
    right = [jnp.where(p, part, none) for part in (top, bottom) for p in picks]
    return jnp.concatenate(left, axis=0), jnp.concatenate(right, axis=0)


def later_row(n, t):
    return (n - 1) * 8 + t + STEPS - n


def forward(piece, *refs):
    last = piece + 2 == len(PIECES)
    refs = list(refs)
    near_parts = len(NEAR_PIECES) - 1
    own, own_maps, far, classes = refs[:4]
    nears = refs[4 : 4 + near_parts]
    del refs[: 4 + near_parts]
    before = refs.pop(0) if piece > 0 else None
    scales = refs.pop(0) if last else None
    out, later = refs[:2]
    weighted, maps, grams = refs[2:] if last else (None, refs[2], out)
    levels = own.shape[1] // 4
    group = list(range(PIECES[piece], PIECES[piece + 1]))
    face_maps(own_maps, nears, {piece: far}, maps, group, levels)
    lane = lax.broadcasted_iota(jnp.int32, (levels, LANES), 1)
    inner = jnp.logical_and(lane >= GHOST, lane < LANES - GHOST)
    coefs = [Coefficients(maps, u, levels) for u in range(len(group))]
    fields, tangents = [], None
    for u, j in enumerate(group):
        field = {t: own[j, t * levels : (t + 1) * levels, :] for t in range(4)}
        for s in range(STEPS):
            at = (u * STEPS + s) * levels
            field[s - STEPS] = far[at : at + levels, :]
            near, local, _ = near_place(nears, j)
            at = (local * STEPS + s) * levels
            field[4 + s] = near[at : at + levels, :]
        fields.append(field)
    for n in range(STEPS):
        rows = list(range(n + 1 - STEPS, 4 + STEPS - n - 1))
        steps = gaps(fields, rows)
        push = fluxes(coefs, "dir", steps)
        if n == 0:
            following = gathered_in(push, rows)
        else:
            push = both(push, fluxes(coefs, "mix", gaps(tangents, rows)))
            following = gathered_in(push, rows, tangents, coefs)
        tangents = following
        if n + 1 < STEPS:
            fields = gathered_in(fluxes(coefs, "mix", steps), rows, fields, coefs)
            for u in range(len(group)):
                for t in rows:
                    at = later_row(n + 1, t) * levels
                    later[u, at : at + levels, :] = fields[u][t]
    for pair in range(2):
        lefts, rights = [], []
        for u, j in enumerate(group):
            for t in (2 * pair, 2 * pair + 1):
                chosen = jnp.logical_and(inner, coefs[u].get("wet", t))
                value = jnp.where(chosen, tangents[u][t], 0.0)
                left, right = class_hits(value, classes[j, t * levels : (t + 1) * levels, :], levels)
                lefts.append(left)
                rights.append(right)
        gram = lax.dot_general(
            jnp.concatenate(lefts, axis=1),
            jnp.concatenate(rights, axis=1),
            (((1,), (1,)), ((), ())),
            preferred_element_type=jnp.float32,
        )
        grams[pair] = gram if before is None else before[pair] + gram
    if last:
        class_sums(grams, scales, out, weighted, levels)


def class_sums(grams, scales, sums, weighted, levels):
    width = 2 * LOW_COUNT * levels
    own_level = lax.broadcasted_iota(jnp.int32, (levels, width), 0)
    other_level = lax.broadcasted_iota(jnp.int32, (levels, width), 1) & (levels - 1)
    diagonal = own_level == other_level
    sheets = []
    for pair in range(2):
        for h in range(HIGH_COUNT):
            sheet = jnp.where(diagonal, grams[pair, h * levels : (h + 1) * levels, :], 0.0)
            sheets.append(jnp.sum(sheet, axis=0, keepdims=True))
        sheets.append(jnp.zeros((16 - HIGH_COUNT, width), jnp.float32))
    rest = jnp.concatenate(sheets, axis=0)
    parts = []
    for _ in range(3):
        part = rest.astype(jnp.bfloat16)
        rest = rest - part.astype(jnp.float32)
        parts.append(part)
    at_low = (lax.broadcasted_iota(jnp.int32, (width, LANES), 0) >> (levels.bit_length() - 1)) & (LOW_COUNT - 1)
    of_low = lax.broadcasted_iota(jnp.int32, (width, LANES), 1) & (LOW_COUNT - 1)
    gather = jnp.where(at_low == of_low, 1.0, 0.0).astype(jnp.bfloat16)
    added = jnp.dot(jnp.concatenate(parts, axis=0), gather, preferred_element_type=jnp.float32)
    added = (added[64:96] + added[32:64]) + added[0:32]
    here = lax.broadcasted_iota(jnp.int32, (16, LANES), 0)
    label = lax.broadcasted_iota(jnp.int32, (16, LANES), 1)
    totals = [
        jnp.sum(
            jnp.where(here == (label >> LOW_SHIFT), added[16 * p : 16 * p + 16], 0.0), axis=0, keepdims=True
        )
        for p in range(2)
    ]
    finish_sums(scales, totals, sums, weighted)


def finish_sums(scales, totals, sums, weighted):
    sums[...] = jnp.concatenate([totals[p] + scales[4 + p : 5 + p, :] for p in range(2)], axis=0)
    weighted[0:2, :] = jnp.concatenate([scales[p : p + 1, :] * totals[p] for p in range(2)], axis=0)


def finish(own_share, near_share, far_share, *refs):
    pieces, binned, gradient = refs[:-2], refs[-2], refs[-1]
    up = own_share[...] + (near_share[...] + far_share[...])
    down = jnp.concatenate([up[t : t + 1] for t in reversed(range(up.shape[0]))], axis=0)
    gradient[...] = jnp.where(is_odd(), down, up)
    band_own, class_count = binned.shape
    first = lax.axis_index("lat") * band_own
    found = [jnp.zeros((1, LANES), jnp.float32) for _ in range(band_own)]
    for piece in pieces:
        totals = piece[...]
        bands = jnp.broadcast_to(totals[:, LANES - 1 :], totals.shape)
        for m in range(band_own):
            hit = jnp.where(bands == (first + m).astype(jnp.float32), totals, 0.0)
            found[m] = found[m] + jnp.sum(hit, axis=0, keepdims=True)
    whole = jnp.concatenate(found, axis=0)
    binned[...] = whole[:, :class_count]


def base_rows(n, j, rows, own, nears, fars, laters):
    levels = own.shape[1] // 4
    piece = piece_of(j)
    local = j - PIECES[piece]
    field = {}
    for t in rows:
        if n > 0:
            at = later_row(n, t) * levels
            field[t] = laters[piece][local, at : at + levels, :]
        elif t < 0:
            at = (local * STEPS + t + STEPS) * levels
            field[t] = fars[piece][at : at + levels, :]
        elif t < 4:
            field[t] = own[j, t * levels : (t + 1) * levels, :]
        else:
            near, place, _ = near_place(nears, j)
            at = (place * STEPS + t - 4) * levels
            field[t] = near[at : at + levels, :]
    return field


def kept_row(n, t):
    return t if n == STEPS - 1 else 4 + 6 * (STEPS - 2 - n) + t + 1


def add_terms(total, basis, steps, places, shift):
    for t in places:
        gap = (shift(basis[t]) if shift else basis[t + 1]) - basis[t]
        term = gap * steps[t]
        total[t] = total[t] + term if t in total else term


def shares(coefs, east_total, north_total, rows):
    none = jnp.zeros((1, LANES), jnp.float32)
    pad = [none] * (-len(rows) % 8)

    def summed(coef, kind, total):
        return {
            t: jnp.sum(jnp.where(coef.get(kind, t), x, 0.0), axis=0, keepdims=True) for t, x in total.items()
        }

    across = []
    for coef, total in zip(coefs, east_total):
        sums = summed(coef, "east_open", total)
        across.append(jnp.concatenate([sums.get(t, none) for t in rows] + pad, axis=0))
    turned = [west(x) for x in across]
    strips = []
    for coef, total, x, turn in zip(coefs, north_total, across, turned):
        sums = summed(coef, "north_open", total)
        along = [sums.get(t, none) + sums.get(t - 1, none) for t in rows]
        strips.append(-0.5 * (jnp.concatenate(along + pad, axis=0) + (x + turn)))
    whole = jnp.concatenate([x[:, GHOST : LANES - GHOST] for x in strips], axis=1)
    return {t: whole[i : i + 1] for i, t in enumerate(rows)}


def adjoint_part(own, own_maps, classes, weighted, *refs):
    parts, near_parts = len(PIECES) - 1, len(NEAR_PIECES) - 1
    nears, refs = refs[:near_parts], refs[near_parts:]
    fars, laters = refs[:parts], refs[parts : 2 * parts]
    near_share, far_share, kept, maps = refs[2 * parts :]
    strips = own.shape[0]
    levels = own.shape[1] // 4
    group = list(range(strips))
    face_maps(own_maps, nears, fars, maps, group, levels)
    coefs = [Coefficients(maps, j, levels) for j in group]
    adjoints = []
    for j in group:
        adjoint = {}
        for t in range(4):
            label = classes[j, t * levels : (t + 1) * levels, :]
            row = t // 2
            table = jnp.broadcast_to(weighted[row : row + 1, :], (8, LANES))
            value = jnp.concatenate(
                [jnp.take_along_axis(table, label[k : k + 8, :], axis=1) for k in range(0, levels, 8)], axis=0
            )
            adjoint[t] = jnp.where(coefs[j].get("wet", t), value, 0.0)
        adjoints.append(adjoint)
    east_total = [{} for _ in group]
    north_total = [{} for _ in group]
    for n in reversed(range(STEPS)):
        rows = list(range(n + 1 - STEPS, 3 + STEPS - n))
        low, high = rows[0], rows[-1]
        for j in group:
            for t in range(max(low, -1), min(high, 4) + 1):
                at = kept_row(n, t) * levels
                kept[j, at : at + levels, :] = adjoints[j][t]
        outer = [t for t in rows if t < 0 or t > 3]
        turning = rows if n > 0 else outer
        turned = [{t: east(field[t]) for t in turning} for field in adjoints]
        to_east = [{t: turn[t] - field[t] for t in turn} for turn, field in zip(turned, adjoints)]
        to_north = [
            {low - 1: field[low], high: -field[high], **{t: field[t + 1] - field[t] for t in rows[:-1]}}
            for field in adjoints
        ]
        if n > 0:
            across = [{t: coef.get("east_mix", t) * x[t] for t in rows} for coef, x in zip(coefs, to_east)]
            turned = [{t: west(x[t]) for t in rows} for x in across]
            along = [{t: coef.get("north_mix", t) * x[t] for t in x} for coef, x in zip(coefs, to_north)]
            following = []
            for j in group:
                field, flux = adjoints[j], along[j]
                new = {low - 1: flux[low - 1], high + 1: -flux[high]}
                for t in rows:
                    still = field[t] + column(field[t], coefs[j].get("column", t)) + (flux[t] - flux[t - 1])
                    new[t] = still + (across[j][t] - turned[j][t])
                following.append(new)
            adjoints = following
        for j in group:
            needed = [t for t in range(low - 1, high + 2) if t <= 0 or t >= 3]
            basis = base_rows(n, j, needed, own, nears, fars, laters)
            faces = [t for t in to_north[j] if t < 0 or t > 2]
            add_terms(east_total[j], basis, to_east[j], outer, east)
            add_terms(north_total[j], basis, to_north[j], faces, None)
    low_rows, high_rows = [-3, -2, -1], [4, 5, 6]
    share = shares(coefs, east_total, north_total, low_rows + high_rows)
    blank = jnp.zeros_like(share[-1])
    far_share[...] = jnp.concatenate([share[-1], share[-2], share[-3], blank], axis=0)
    near_share[...] = jnp.concatenate([blank, share[6], share[5], share[4]], axis=0)


def own_part(own, own_maps, kept, *refs):
    parts, near_parts = len(PIECES) - 1, len(NEAR_PIECES) - 1
    nears, refs = refs[:near_parts], refs[near_parts:]
    fars, laters = refs[:parts], refs[parts : 2 * parts]
    own_share, maps = refs[2 * parts :]
    levels = own.shape[1] // 4
    group = list(range(own.shape[0]))
    face_maps(own_maps, nears, fars, maps, group, levels, kinds=1)
    coefs = [Coefficients(maps, j, levels) for j in group]
    east_total = [{} for _ in group]
    north_total = [{} for _ in group]
    for n in range(STEPS):
        last = n == STEPS - 1
        for j in group:
            rows = range(4) if last else range(-1, 5)
            adjoint = {t: kept[j, kept_row(n, t) * levels : (kept_row(n, t) + 1) * levels, :] for t in rows}
            to_east = {t: east(adjoint[t]) - adjoint[t] for t in range(4)}
            to_north = {t: adjoint[t + 1] - adjoint[t] for t in rows[:-1]}
            if last:
                to_north.update({-1: adjoint[0], 3: -adjoint[3]})
            basis = base_rows(n, j, range(-1, 5), own, nears, fars, laters)
            add_terms(east_total[j], basis, to_east, range(4), east)
            add_terms(north_total[j], basis, to_north, range(-1, 4), None)
    share = shares(coefs, east_total, north_total, list(range(4)))
    own_share[...] = jnp.concatenate([share[t] for t in range(4)], axis=0)


def near_pairs(count):
    return [(i, i ^ 1) for i in range(count)]


def far_pairs(members, count):
    pairs = []
    for m in range(members):
        for i in range(1, count - 1, 2):
            pairs += [(m * count + i, m * count + i + 1), (m * count + i + 1, m * count + i)]
        for i in (0, count - 1):
            pairs.append((m * count + i, (m ^ 1) * count + i))
    return pairs


def routes(count):
    bits = count.bit_length() - 1
    groups = [[1]] if bits % 2 else []
    for bit in range(bits % 2, bits, 2):
        one, two = 1 << bit, 2 << bit
        groups.append([one + two, two, one] if bit == 0 else [two, one + two, one])
    return groups


def vmem(count):
    return [pl.BlockSpec(memory_space=pltpu.VMEM)] * count


def cost(nanoseconds):
    return pl.CostEstimate(flops=1153500 * nanoseconds, bytes_accessed=3690 * nanoseconds, transcendentals=0)


def body(tracer, diffusivity, direction, column_depth, density_class, band_of_row, weights):
    levels, rows, lon_count = tracer.shape
    strips = lon_count // OWN
    count = lax.axis_size("lat")
    members = lax.axis_size("members")
    params = pltpu.CompilerParams(vmem_limit_bytes=VMEM_LIMIT)
    f32, i32 = jnp.float32, jnp.int32
    halo = strips * STEPS * levels
    payload = halo + strips * 9

    def to_near(x):
        return lax.ppermute(x, "lat", near_pairs(count))

    def to_far(x):
        return lax.ppermute(x, ("members", "lat"), far_pairs(members, count))

    sizes = [b - a for a, b in zip(PIECES, PIECES[1:])]
    near_sizes = [b - a for a, b in zip(NEAR_PIECES, NEAR_PIECES[1:])]
    fields = (tracer, diffusivity, direction, column_depth)
    in_place = [pltpu.with_memory_space_constraint(x, pltpu.HBM) for x in fields]
    taken = dict(
        in_specs=[pl.BlockSpec(memory_space=pltpu.HBM)] * 4,
        scratch_shapes=[pltpu.VMEM(x.shape, x.dtype) for x in fields] + [pltpu.SemaphoreType.DMA((4,))],
        compiler_params=params,
    )
    far_shapes = [jax.ShapeDtypeStruct((payload // strips * size, LANES), f32) for size in sizes]
    first_out = pl.pallas_call(
        pack_first,
        name="pack_first",
        out_shape=far_shapes[0],
        out_specs=pl.BlockSpec(memory_space=pltpu.VMEM),
        **taken,
    )(*in_place)
    fars = [to_far(first_out)]
    late_fields = lax.optimization_barrier((*fields, first_out))[: len(fields)]
    in_place = [pltpu.with_memory_space_constraint(x, pltpu.HBM) for x in late_fields]
    own, own_maps, *outs = pl.pallas_call(
        pack_fields,
        name="pack_fields",
        out_shape=(
            jax.ShapeDtypeStruct((strips, rows * levels, LANES), f32),
            jax.ShapeDtypeStruct((strips, 16, LANES), f32),
            *[jax.ShapeDtypeStruct((payload // strips * size, LANES), f32) for size in near_sizes],
            *far_shapes[1:],
        ),
        out_specs=tuple(vmem(1 + len(near_sizes) + len(sizes))),
        **taken,
    )(*in_place)
    nears = [to_near(x) for x in outs[: len(near_sizes)]]
    fars += [to_far(x) for x in outs[len(near_sizes) :]]

    own_classes, scales = pl.pallas_call(
        pack_classes,
        name="pack_classes",
        out_shape=(
            jax.ShapeDtypeStruct((strips, rows * levels, LANES), i32),
            jax.ShapeDtypeStruct((8, LANES), f32),
        ),
        in_specs=[pl.BlockSpec(memory_space=pltpu.HBM)] * 3,
        out_specs=tuple(vmem(2)),
        scratch_shapes=[
            pltpu.VMEM(density_class.shape, i32),
            pltpu.VMEM(weights.shape, f32),
            pltpu.SMEM(band_of_row.shape, i32),
            pltpu.SemaphoreType.DMA((3,)),
        ],
        compiler_params=params,
    )(*[pltpu.with_memory_space_constraint(x, pltpu.HBM) for x in (density_class, weights, band_of_row)])
    laters, sums = [], None
    gram_shape = (2, HIGH_COUNT * levels, 2 * LOW_COUNT * levels)
    for piece, size in enumerate(sizes):
        last = piece + 1 == len(sizes)
        given = [own, own_maps, fars[piece], own_classes, *nears]
        given += ([sums] if piece > 0 else []) + ([scales] if last else [])
        sums, later, *weighted = pl.pallas_call(
            functools.partial(forward, piece),
            name="forward",
            out_shape=(
                jax.ShapeDtypeStruct((2, LANES) if last else gram_shape, f32),
                jax.ShapeDtypeStruct((size, 14 * levels, LANES), f32),
            )
            + ((jax.ShapeDtypeStruct((8, LANES), f32),) if last else ()),
            in_specs=vmem(len(given)),
            out_specs=tuple(vmem(3 if last else 2)),
            cost_estimate=cost(2000),
            scratch_shapes=[pltpu.VMEM((size, 16 * MAP_FIELDS, LANES), f32)]
            + ([pltpu.VMEM(gram_shape, f32)] if last else []),
            compiler_params=params,
        )(*given)
        laters.append(later)

    gathered = sums
    groups = routes(count)
    for i, group in enumerate(groups):
        others = [lax.ppermute(gathered, "lat", [(d, d ^ k) for d in range(count)]) for k in group]
        pieces = [gathered] + others
        if i == 0:
            near_share, far_share, kept = pl.pallas_call(
                adjoint_part,
                name="adjoint_part",
                out_shape=(
                    jax.ShapeDtypeStruct((rows, lon_count), f32),
                    jax.ShapeDtypeStruct((rows, lon_count), f32),
                    jax.ShapeDtypeStruct((strips, 16 * levels, LANES), f32),
                ),
                in_specs=vmem(4 + len(nears) + 2 * len(sizes)),
                out_specs=tuple(vmem(3)),
                scratch_shapes=[pltpu.VMEM((strips, 16 * MAP_FIELDS, LANES), f32)],
                compiler_params=params,
            )(own, own_maps, own_classes, weighted[0], *nears, *fars, *laters)
            *pieces, near_share, far_share = lax.optimization_barrier((*pieces, near_share, far_share))
            near_share, far_share = to_near(near_share), to_far(far_share)
        if i + 1 < len(groups):
            gathered = jnp.concatenate(pieces, axis=0)
    own_share = pl.pallas_call(
        own_part,
        name="own_part",
        out_shape=jax.ShapeDtypeStruct((rows, lon_count), f32),
        in_specs=vmem(3 + len(nears) + 2 * len(sizes)),
        out_specs=pl.BlockSpec(memory_space=pltpu.VMEM),
        scratch_shapes=[pltpu.VMEM((strips, 16 * 3, LANES), f32)],
        compiler_params=params,
    )(own, own_maps, kept, *nears, *fars, *laters)
    binned, gradient = pl.pallas_call(
        finish,
        name="finish",
        out_shape=(
            jax.ShapeDtypeStruct((weights.shape[0] // count, weights.shape[1]), f32),
            jax.ShapeDtypeStruct((rows, lon_count), f32),
        ),
        in_specs=vmem(3 + len(pieces)),
        out_specs=tuple(vmem(2)),
        compiler_params=params,
    )(own_share, near_share, far_share, *pieces)
    return binned, gradient


def solution(mesh):
    placed = (
        P(None, ("members", "lat"), None),
        P("lat", None),
        P(("members", "lat"), None),
        P("lat", None),
        P(None, ("members", "lat"), None),
        P("lat"),
        P(),
    )
    return jax.shard_map(
        body,
        mesh=mesh,
        in_specs=placed,
        out_specs=(P(("members", "lat"), None), P(("members", "lat"), None)),
        check_vma=False,
    )
```

```python
import functools

import jax
import jax.numpy as jnp
from jax import lax
from jax.experimental import pallas as pl
from jax.experimental.pallas import tpu as pltpu
from jax.sharding import PartitionSpec as P

STEPS = 3
vertical_mix = 0.05

LANES = 128
GHOST = 4
OWN = LANES - 2 * GHOST
HIGH_COUNT = 9
LOW_COUNT = 8
LOW_SHIFT = 3
PIECES = (0, 7, 12)
NEAR_PIECES = (0, 4, 8, 12)
VMEM_LIMIT = 16 * 1024 * 1024


def strip_of(row, j, lon_count):
    first = OWN * j - GHOST
    last = first + LANES
    if first < 0:
        return jnp.concatenate([row[:, first + lon_count :], row[:, :last]], axis=1)
    if last > lon_count:
        return jnp.concatenate([row[:, first:], row[:, : last - lon_count]], axis=1)
    return row[:, first:last]


def piece_of(j, bounds=None):
    bounds = PIECES if bounds is None else bounds
    return max(p for p in range(len(bounds) - 1) if bounds[p] <= j)


def near_place(nears, j):
    piece = piece_of(j, NEAR_PIECES)
    first, last = NEAR_PIECES[piece : piece + 2]
    return nears[piece], j - first, last - first


def is_odd():
    return lax.rem(lax.axis_index("lat"), 2) == 1


def oriented(ref, t, odd):
    last = ref.shape[1] - 1
    order = level_order(ref.shape[0])
    up = jnp.concatenate([ref[k, t : t + 1, :] for k in order], axis=0)
    down = jnp.concatenate([ref[k, last - t : last - t + 1, :] for k in order], axis=0)
    return jnp.where(odd, down, up)


def bring(sources, held, arrived):
    copies = [pltpu.make_async_copy(a, b, arrived.at[i]) for i, (a, b) in enumerate(zip(sources, held))]
    for copy in copies:
        copy.start()
    for copy in copies:
        copy.wait()


def flipped_map(ref, odd):
    field = ref[...].astype(jnp.float32)
    flipped = jnp.concatenate([field[r : r + 1] for r in reversed(range(field.shape[0]))], axis=0)
    return jnp.where(odd, field, flipped), jnp.where(odd, flipped, field)


def fill_far(piece, far, held):
    tracer, maps = held[0], held[1:]
    levels, _, lon_count = tracer.shape
    odd = is_odd()
    group = range(PIECES[piece], PIECES[piece + 1])
    for t in range(STEPS):
        field = oriented(tracer, t, odd)
        for u, j in enumerate(group):
            at = (u * STEPS + STEPS - 1 - t) * levels
            far[at : at + levels, :] = strip_of(field, j, lon_count)
    for a, ref in enumerate(maps):
        down, _ = flipped_map(ref, odd)
        for u, j in enumerate(group):
            at = len(group) * STEPS * levels + (3 * u + a) * STEPS
            far[at : at + STEPS, :] = strip_of(down, j, lon_count)[1:]


def pack_first(*refs):
    sources, far, held, arrived = refs[:4], refs[4], refs[5:9], refs[9]
    bring(sources, held, arrived)
    fill_far(0, far, held)


def pack_fields(*refs):
    parts, near_parts = len(PIECES) - 2, len(NEAR_PIECES) - 1
    sources, (own, own_maps) = refs[:4], refs[4:6]
    nears, refs = refs[6 : 6 + near_parts], refs[6 + near_parts :]
    fars, held, arrived = refs[:parts], refs[parts : 4 + parts], refs[4 + parts]
    bring(sources, held, arrived)
    tracer = held[0]
    levels, rows, lon_count = tracer.shape
    strips = lon_count // OWN
    odd = is_odd()
    for i, far in enumerate(fars):
        fill_far(i + 1, far, held)
    for t in range(rows):
        field = oriented(tracer, t, odd)
        for j in range(strips):
            strip = strip_of(field, j, lon_count)
            own[j, t * levels : (t + 1) * levels, :] = strip
            if t > 0:
                near, local, _ = near_place(nears, j)
                at = (local * STEPS + rows - 1 - t) * levels
                near[at : at + levels, :] = strip
    for a, ref in enumerate(held[1:]):
        down, up = flipped_map(ref, odd)
        for j in range(strips):
            own_maps[j, a * 4 : a * 4 + 4, :] = strip_of(up, j, lon_count)
            near, local, count = near_place(nears, j)
            at = count * STEPS * levels + (3 * local + a) * STEPS
            near[at : at + STEPS, :] = strip_of(down, j, lon_count)[:STEPS]
    own_maps[:, 12:, :] = jnp.zeros_like(own_maps[:, 12:, :])


def pack_classes(*refs):
    sources, (own, scales), held, arrived = refs[:3], refs[3:5], refs[5:8], refs[8]
    bring(sources, held, arrived)
    classes, weights, band_of_row = held
    levels, rows, lon_count = classes.shape
    strips = lon_count // OWN
    odd = is_odd()
    for t in range(rows):
        field = oriented(classes, t, odd)
        for j in range(strips):
            strip = strip_of(field, j, lon_count)
            own[j, t * levels : (t + 1) * levels, :] = strip
    class_count = weights.shape[1]
    label = lax.broadcasted_iota(jnp.int32, (1, LANES), 1)
    scale_rows, band_rows = [], []
    for pair in range(2):
        band = band_of_row[jnp.where(odd, 3 - 2 * pair, 2 * pair)]
        scale = weights[pl.ds(band, 1), :]
        scale_rows.append(jnp.concatenate([scale, jnp.zeros((1, LANES - class_count), jnp.float32)], axis=1))
        band_rows.append(jnp.where(label == LANES - 1, band.astype(jnp.float32), 0.0))
    blank = jnp.zeros((2, LANES), jnp.float32)
    scales[...] = jnp.concatenate(scale_rows + [blank] + band_rows + [blank], axis=0)


def east(x):
    return pltpu.roll(x, LANES - 1, 1)


def west(x):
    return pltpu.roll(x, 1, 1)


MAP_FIELDS = 7


def level_order(levels):
    half = levels // 2
    return [2 * (i % half) + i // half for i in range(levels)]


class Coefficients:
    blocks = {
        "wet": 0, "east_open": 1, "north_open": 2,
        "east_mix": 3, "north_mix": 4, "east_dir": 5, "north_dir": 6,
    }

    def __init__(self, maps, j, levels):
        order = lax.broadcasted_iota(jnp.int32, (levels, LANES), 0)
        half = levels // 2
        self.level = (2 * (order & (half - 1)) + jnp.where(order < half, 0, 1)).astype(jnp.float32)
        self.levels = levels
        self.maps = maps
        self.j = j
        self.cache = {}

    def row(self, kind, t):
        at = 16 * self.blocks[kind] + t + STEPS
        return jnp.broadcast_to(self.maps[self.j, at : at + 1, :], (self.levels, LANES))

    def get(self, kind, t):
        if (kind, t) not in self.cache:
            side, _, what = kind.partition("_")
            if kind == "column":
                value = jnp.where(self.level + 1.0 < self.row("wet", t), vertical_mix, 0.0)
            elif kind == "wet" or what == "open":
                value = self.level < self.row(kind, t)
            else:
                value = jnp.where(self.get(side + "_open", t), self.row(kind, t), 0.0)
            self.cache[kind, t] = value
        return self.cache[kind, t]


def column(field, coefficient):
    half = field.shape[0] // 2
    even, odd = field[:half], field[half:]
    after_even = coefficient[:half] * (odd - even)
    after_odd = coefficient[half:] * (pltpu.roll(even, half - 1, 0) - odd)
    return jnp.concatenate([after_even - pltpu.roll(after_odd, 1, 0), after_odd - after_even], axis=0)


def gaps(fields, rows):
    turned = [{t: east(field[t]) for t in rows} for field in fields]
    to_east = [{t: turn[t] - field[t] for t in rows} for turn, field in zip(turned, fields)]
    faces = range(rows[0] - 1, rows[-1] + 1)
    to_north = [{t: field[t + 1] - field[t] for t in faces} for field in fields]
    return list(zip(to_east, to_north))


def fluxes(coefs, kind, steps):
    return [
        (
            {t: coef.get("east_" + kind, t) * to_east[t] for t in to_east},
            {t: coef.get("north_" + kind, t) * to_north[t] for t in to_north},
        )
        for coef, (to_east, to_north) in zip(coefs, steps)
    ]


def both(ones, others):
    return [
        tuple({t: a[t] + b[t] for t in a} for a, b in zip(one, other)) for one, other in zip(ones, others)
    ]


def gathered_in(flux, rows, fields=None, coefs=None):
    turned = [{t: west(across[t]) for t in rows} for across, _ in flux]
    still = [{t: along[t] - along[t - 1] for t in rows} for _, along in flux]
    if fields is not None:
        still = [
            {t: rest[t] + (field[t] + column(field[t], coef.get("column", t))) for t in rows}
            for rest, field, coef in zip(still, fields, coefs)
        ]
    return [
        {t: rest[t] + (across[t] - turn[t]) for t in rows}
        for rest, (across, _), turn in zip(still, flux, turned)
    ]


def face_maps(own_maps, nears, fars, maps, strips, levels, kinds=(0, 1, 2)):
    count, edge = lax.axis_size("lat"), lax.axis_index("lat")
    keep = jnp.where(jnp.logical_and(edge != 0, edge != count - 1), 1.0, 0.0)

    def north(x):
        return pltpu.roll(x, 15, 0)

    for i, j in enumerate(strips):
        whole = []
        piece = piece_of(j)
        for a in kinds:
            at = (PIECES[piece + 1] - PIECES[piece]) * STEPS * levels + (3 * (j - PIECES[piece]) + a) * STEPS
            low = fars[piece][at : at + STEPS, :]
            if a == 2:
                low = low * keep
            near, local, size = near_place(nears, j)
            at = size * STEPS * levels + (3 * local + a) * STEPS
            high = near[at : at + STEPS, :]
            whole.append(jnp.concatenate([low, own_maps[j, 4 * a : 4 * a + 4, :], high, high, high], axis=0))
        depth = whole.pop()
        blocks = [depth] + [jnp.minimum(depth, f(depth)) for f in (east, north)]
        blocks += [0.5 * (x + f(x)) for x in whole for f in (east, north)]
        for b, block in enumerate(blocks):
            maps[i, 16 * b : 16 * b + 16, :] = block


def class_hits(value, label, levels):
    top = value.astype(jnp.bfloat16)
    bottom = (value - top.astype(jnp.float32)).astype(jnp.bfloat16)
    high = (label >> LOW_SHIFT).astype(jnp.float32).astype(jnp.bfloat16)
    low = (label & (LOW_COUNT - 1)).astype(jnp.float32).astype(jnp.bfloat16)
    none = jnp.zeros((levels, LANES), jnp.bfloat16)
    one = jnp.ones((levels, LANES), jnp.bfloat16)
    left = [jnp.where(high == jnp.bfloat16(h), one, none) for h in range(HIGH_COUNT)]
    picks = [low == jnp.bfloat16(l) for l in range(LOW_COUNT)]
    right = [jnp.where(p, part, none) for part in (top, bottom) for p in picks]
    return jnp.concatenate(left, axis=0), jnp.concatenate(right, axis=0)


def later_row(n, t):
    return (n - 1) * 8 + t + STEPS - n


def forward(piece, *refs):
    last = piece + 2 == len(PIECES)
    refs = list(refs)
    near_parts = len(NEAR_PIECES) - 1
    own, own_maps, far, classes = refs[:4]
    nears = refs[4 : 4 + near_parts]
    del refs[: 4 + near_parts]
    before = refs.pop(0) if piece > 0 else None
    scales = refs.pop(0) if last else None
    out, later = refs[:2]
    weighted, maps, grams = refs[2:] if last else (None, refs[2], out)
    levels = own.shape[1] // 4
    group = list(range(PIECES[piece], PIECES[piece + 1]))
    face_maps(own_maps, nears, {piece: far}, maps, group, levels)
    lane = lax.broadcasted_iota(jnp.int32, (levels, LANES), 1)
    inner = jnp.logical_and(lane >= GHOST, lane < LANES - GHOST)
    coefs = [Coefficients(maps, u, levels) for u in range(len(group))]
    fields, tangents = [], None
    for u, j in enumerate(group):
        field = {t: own[j, t * levels : (t + 1) * levels, :] for t in range(4)}
        for s in range(STEPS):
            at = (u * STEPS + s) * levels
            field[s - STEPS] = far[at : at + levels, :]
            near, local, _ = near_place(nears, j)
            at = (local * STEPS + s) * levels
            field[4 + s] = near[at : at + levels, :]
        fields.append(field)
    for n in range(STEPS):
        rows = list(range(n + 1 - STEPS, 4 + STEPS - n - 1))
        steps = gaps(fields, rows)
        push = fluxes(coefs, "dir", steps)
        if n == 0:
            following = gathered_in(push, rows)
        else:
            push = both(push, fluxes(coefs, "mix", gaps(tangents, rows)))
            following = gathered_in(push, rows, tangents, coefs)
        tangents = following
        if n + 1 < STEPS:
            fields = gathered_in(fluxes(coefs, "mix", steps), rows, fields, coefs)
            for u in range(len(group)):
                for t in rows:
                    at = later_row(n + 1, t) * levels
                    later[u, at : at + levels, :] = fields[u][t]
    for pair in range(2):
        lefts, rights = [], []
        for u, j in enumerate(group):
            for t in (2 * pair, 2 * pair + 1):
                chosen = jnp.logical_and(inner, coefs[u].get("wet", t))
                value = jnp.where(chosen, tangents[u][t], 0.0)
                left, right = class_hits(value, classes[j, t * levels : (t + 1) * levels, :], levels)
                lefts.append(left)
                rights.append(right)
        gram = lax.dot_general(
            jnp.concatenate(lefts, axis=1),
            jnp.concatenate(rights, axis=1),
            (((1,), (1,)), ((), ())),
            preferred_element_type=jnp.float32,
        )
        grams[pair] = gram if before is None else before[pair] + gram
    if last:
        class_sums(grams, scales, out, weighted, levels)


def class_sums(grams, scales, sums, weighted, levels):
    width = 2 * LOW_COUNT * levels
    own_level = lax.broadcasted_iota(jnp.int32, (levels, width), 0)
    other_level = lax.broadcasted_iota(jnp.int32, (levels, width), 1) & (levels - 1)
    diagonal = own_level == other_level
    sheets = []
    for pair in range(2):
        for h in range(HIGH_COUNT):
            sheet = jnp.where(diagonal, grams[pair, h * levels : (h + 1) * levels, :], 0.0)
            sheets.append(jnp.sum(sheet, axis=0, keepdims=True))
        sheets.append(jnp.zeros((16 - HIGH_COUNT, width), jnp.float32))
    rest = jnp.concatenate(sheets, axis=0)
    parts = []
    for _ in range(3):
        part = rest.astype(jnp.bfloat16)
        rest = rest - part.astype(jnp.float32)
        parts.append(part)
    at_low = (lax.broadcasted_iota(jnp.int32, (width, LANES), 0) >> (levels.bit_length() - 1)) & (LOW_COUNT - 1)
    of_low = lax.broadcasted_iota(jnp.int32, (width, LANES), 1) & (LOW_COUNT - 1)
    gather = jnp.where(at_low == of_low, 1.0, 0.0).astype(jnp.bfloat16)
    added = jnp.dot(jnp.concatenate(parts, axis=0), gather, preferred_element_type=jnp.float32)
    added = (added[64:96] + added[32:64]) + added[0:32]
    here = lax.broadcasted_iota(jnp.int32, (16, LANES), 0)
    label = lax.broadcasted_iota(jnp.int32, (16, LANES), 1)
    totals = [
        jnp.sum(
            jnp.where(here == (label >> LOW_SHIFT), added[16 * p : 16 * p + 16], 0.0), axis=0, keepdims=True
        )
        for p in range(2)
    ]
    finish_sums(scales, totals, sums, weighted)


def finish_sums(scales, totals, sums, weighted):
    sums[...] = jnp.concatenate([totals[p] + scales[4 + p : 5 + p, :] for p in range(2)], axis=0)
    weighted[0:2, :] = jnp.concatenate([scales[p : p + 1, :] * totals[p] for p in range(2)], axis=0)


def finish(own_share, near_share, far_share, *refs):
    pieces, binned, gradient = refs[:-2], refs[-2], refs[-1]
    up = own_share[...] + (near_share[...] + far_share[...])
    down = jnp.concatenate([up[t : t + 1] for t in reversed(range(up.shape[0]))], axis=0)
    gradient[...] = jnp.where(is_odd(), down, up)
    band_own, class_count = binned.shape
    first = lax.axis_index("lat") * band_own
    found = [jnp.zeros((1, LANES), jnp.float32) for _ in range(band_own)]
    for piece in pieces:
        totals = piece[...]
        bands = jnp.broadcast_to(totals[:, LANES - 1 :], totals.shape)
        for m in range(band_own):
            hit = jnp.where(bands == (first + m).astype(jnp.float32), totals, 0.0)
            found[m] = found[m] + jnp.sum(hit, axis=0, keepdims=True)
    whole = jnp.concatenate(found, axis=0)
    binned[...] = whole[:, :class_count]


def base_rows(n, j, rows, own, nears, fars, laters):
    levels = own.shape[1] // 4
    piece = piece_of(j)
    local = j - PIECES[piece]
    field = {}
    for t in rows:
        if n > 0:
            at = later_row(n, t) * levels
            field[t] = laters[piece][local, at : at + levels, :]
        elif t < 0:
            at = (local * STEPS + t + STEPS) * levels
            field[t] = fars[piece][at : at + levels, :]
        elif t < 4:
            field[t] = own[j, t * levels : (t + 1) * levels, :]
        else:
            near, place, _ = near_place(nears, j)
            at = (place * STEPS + t - 4) * levels
            field[t] = near[at : at + levels, :]
    return field


def kept_row(n, t):
    if n == STEPS - 1:
        return t
    return 4 + t + 1 if n > 0 else 10 + {-1: 0, 0: 1, 3: 2, 4: 3}[t]


def add_terms(total, basis, steps, places, shift):
    for t in places:
        gap = (shift(basis[t]) if shift else basis[t + 1]) - basis[t]
        term = gap * steps[t]
        total[t] = total[t] + term if t in total else term


def shares(coefs, east_total, north_total, rows):
    none = jnp.zeros((1, LANES), jnp.float32)
    pad = [none] * (-len(rows) % 8)

    def summed(coef, kind, total):
        return {
            t: jnp.sum(jnp.where(coef.get(kind, t), x, 0.0), axis=0, keepdims=True) for t, x in total.items()
        }

    across = []
    for coef, total in zip(coefs, east_total):
        sums = summed(coef, "east_open", total)
        across.append(jnp.concatenate([sums.get(t, none) for t in rows] + pad, axis=0))
    turned = [west(x) for x in across]
    strips = []
    for coef, total, x, turn in zip(coefs, north_total, across, turned):
        sums = summed(coef, "north_open", total)
        along = [sums.get(t, none) + sums.get(t - 1, none) for t in rows]
        strips.append(-0.5 * (jnp.concatenate(along + pad, axis=0) + (x + turn)))
    whole = jnp.concatenate([x[:, GHOST : LANES - GHOST] for x in strips], axis=1)
    return {t: whole[i : i + 1] for i, t in enumerate(rows)}


def adjoint_part(own, own_maps, classes, weighted, *refs):
    parts, near_parts = len(PIECES) - 1, len(NEAR_PIECES) - 1
    nears, refs = refs[:near_parts], refs[near_parts:]
    fars, laters = refs[:parts], refs[parts : 2 * parts]
    near_share, far_share, kept, maps = refs[2 * parts :]
    strips = own.shape[0]
    levels = own.shape[1] // 4
    group = list(range(strips))
    face_maps(own_maps, nears, fars, maps, group, levels, kinds=(0, 2))
    coefs = [Coefficients(maps, j, levels) for j in group]
    adjoints = []
    for j in group:
        adjoint = {}
        for t in range(4):
            label = classes[j, t * levels : (t + 1) * levels, :]
            row = t // 2
            table = jnp.broadcast_to(weighted[row : row + 1, :], (8, LANES))
            value = jnp.concatenate(
                [jnp.take_along_axis(table, label[k : k + 8, :], axis=1) for k in range(0, levels, 8)], axis=0
            )
            adjoint[t] = jnp.where(coefs[j].get("wet", t), value, 0.0)
        adjoints.append(adjoint)
    east_total = [{} for _ in group]
    north_total = [{} for _ in group]
    for n in reversed(range(STEPS)):
        rows = list(range(n + 1 - STEPS, 3 + STEPS - n))
        low, high = rows[0], rows[-1]
        for j in group:
            for t in [t for t in adjoints[j] if -1 <= t <= 4]:
                at = kept_row(n, t) * levels
                kept[j, at : at + levels, :] = adjoints[j][t]
        outer = [t for t in rows if t < 0 or t > 3]
        made = [t for t in rows if n != 1 or t < 1 or t > 2]
        turning = made if n > 0 else outer
        turned = [{t: east(field[t]) for t in turning} for field in adjoints]
        to_east = [{t: turn[t] - field[t] for t in turn} for turn, field in zip(turned, adjoints)]
        to_north = [
            {
                low - 1: field[low],
                high: -field[high],
                **{t: field[t + 1] - field[t] for t in rows[:-1] if t in field and t + 1 in field},
            }
            for field in adjoints
        ]
        if n > 0:
            across = [{t: coef.get("east_mix", t) * x[t] for t in made} for coef, x in zip(coefs, to_east)]
            turned = [{t: west(x[t]) for t in made} for x in across]
            along = [{t: coef.get("north_mix", t) * x[t] for t in x} for coef, x in zip(coefs, to_north)]
            following = []
            for j in group:
                field, flux = adjoints[j], along[j]
                new = {low - 1: flux[low - 1], high + 1: -flux[high]}
                for t in made:
                    still = field[t] + column(field[t], coefs[j].get("column", t)) + (flux[t] - flux[t - 1])
                    new[t] = still + (across[j][t] - turned[j][t])
                following.append(new)
            adjoints = following
        for j in group:
            needed = [t for t in range(low - 1, high + 2) if t <= 0 or t >= 3]
            basis = base_rows(n, j, needed, own, nears, fars, laters)
            faces = [t for t in to_north[j] if t < 0 or t > 2]
            add_terms(east_total[j], basis, to_east[j], outer, east)
            add_terms(north_total[j], basis, to_north[j], faces, None)
    low_rows, high_rows = [-3, -2, -1], [4, 5, 6]
    share = shares(coefs, east_total, north_total, low_rows + high_rows)
    blank = jnp.zeros_like(share[-1])
    far_share[...] = jnp.concatenate([share[-1], share[-2], share[-3], blank], axis=0)
    near_share[...] = jnp.concatenate([blank, share[6], share[5], share[4]], axis=0)


def own_part(own, own_maps, kept, *refs):
    parts, near_parts = len(PIECES) - 1, len(NEAR_PIECES) - 1
    nears, refs = refs[:near_parts], refs[near_parts:]
    fars, laters = refs[:parts], refs[parts : 2 * parts]
    own_share, maps = refs[2 * parts :]
    levels = own.shape[1] // 4
    group = list(range(own.shape[0]))
    face_maps(own_maps, nears, fars, maps, group, levels, kinds=(0, 2))
    coefs = [Coefficients(maps, j, levels) for j in group]
    east_total = [{} for _ in group]
    north_total = [{} for _ in group]

    def adjoint_of(n, j, rows):
        return {t: kept[j, kept_row(n, t) * levels : (kept_row(n, t) + 1) * levels, :] for t in rows}

    middle = [adjoint_of(1, j, range(4)) for j in group]
    across, along = zip(*fluxes(coefs, "mix", gaps(middle, [1, 2])))
    inner = gathered_in(list(zip(across, along)), [1, 2], middle, coefs)
    for n in range(STEPS):
        last = n == STEPS - 1
        adjoints = []
        for j in group:
            if n == 0:
                adjoints.append({**adjoint_of(0, j, (-1, 0, 3, 4)), **inner[j]})
            else:
                adjoints.append(adjoint_of(n, j, range(4) if last else range(-1, 5)))
        for j, adjoint in zip(group, adjoints):
            to_east = {t: east(adjoint[t]) - adjoint[t] for t in range(4)}
            faces = range(3) if last else range(-1, 4)
            to_north = {t: adjoint[t + 1] - adjoint[t] for t in faces}
            if last:
                to_north.update({-1: adjoint[0], 3: -adjoint[3]})
            basis = base_rows(n, j, range(-1, 5), own, nears, fars, laters)
            add_terms(east_total[j], basis, to_east, range(4), east)
            add_terms(north_total[j], basis, to_north, range(-1, 4), None)
    share = shares(coefs, east_total, north_total, list(range(4)))
    own_share[...] = jnp.concatenate([share[t] for t in range(4)], axis=0)


def near_pairs(count):
    return [(i, i ^ 1) for i in range(count)]


def far_pairs(members, count):
    pairs = []
    for m in range(members):
        for i in range(1, count - 1, 2):
            pairs += [(m * count + i, m * count + i + 1), (m * count + i + 1, m * count + i)]
        for i in (0, count - 1):
            pairs.append((m * count + i, (m ^ 1) * count + i))
    return pairs


def routes(count):
    bits = count.bit_length() - 1
    groups = []
    for bit in range(bits - 2, -1, -2):
        one, two = 1 << bit, 2 << bit
        groups.append([one, one + two, two] if bit > 0 else [3, 2, 1])
    return groups + ([[1]] if bits % 2 else [])


def vmem(count):
    return [pl.BlockSpec(memory_space=pltpu.VMEM)] * count


def cost(nanoseconds):
    return pl.CostEstimate(flops=1153500 * nanoseconds, bytes_accessed=3690 * nanoseconds, transcendentals=0)


def body(tracer, diffusivity, direction, column_depth, density_class, band_of_row, weights):
    levels, rows, lon_count = tracer.shape
    strips = lon_count // OWN
    count = lax.axis_size("lat")
    members = lax.axis_size("members")
    params = pltpu.CompilerParams(vmem_limit_bytes=VMEM_LIMIT)
    f32, i32 = jnp.float32, jnp.int32
    halo = strips * STEPS * levels
    payload = halo + strips * 9

    def to_near(x):
        return lax.ppermute(x, "lat", near_pairs(count))

    def to_far(x):
        return lax.ppermute(x, ("members", "lat"), far_pairs(members, count))

    sizes = [b - a for a, b in zip(PIECES, PIECES[1:])]
    near_sizes = [b - a for a, b in zip(NEAR_PIECES, NEAR_PIECES[1:])]
    fields = (tracer, diffusivity, direction, column_depth)
    in_place = [pltpu.with_memory_space_constraint(x, pltpu.HBM) for x in fields]
    taken = dict(
        in_specs=[pl.BlockSpec(memory_space=pltpu.HBM)] * 4,
        scratch_shapes=[pltpu.VMEM(x.shape, x.dtype) for x in fields] + [pltpu.SemaphoreType.DMA((4,))],
        compiler_params=params,
    )
    far_shapes = [jax.ShapeDtypeStruct((payload // strips * size, LANES), f32) for size in sizes]
    first_out = pl.pallas_call(
        pack_first,
        name="pack_first",
        out_shape=far_shapes[0],
        out_specs=pl.BlockSpec(memory_space=pltpu.VMEM),
        **taken,
    )(*in_place)
    fars = [to_far(first_out)]
    late_fields = lax.optimization_barrier((*fields, first_out))[: len(fields)]
    in_place = [pltpu.with_memory_space_constraint(x, pltpu.HBM) for x in late_fields]
    own, own_maps, *outs = pl.pallas_call(
        pack_fields,
        name="pack_fields",
        out_shape=(
            jax.ShapeDtypeStruct((strips, rows * levels, LANES), f32),
            jax.ShapeDtypeStruct((strips, 16, LANES), f32),
            *[jax.ShapeDtypeStruct((payload // strips * size, LANES), f32) for size in near_sizes],
            *far_shapes[1:],
        ),
        out_specs=tuple(vmem(1 + len(near_sizes) + len(sizes))),
        **taken,
    )(*in_place)
    nears = [to_near(x) for x in outs[: len(near_sizes)]]
    fars += [to_far(x) for x in outs[len(near_sizes) :]]

    own_classes, scales = pl.pallas_call(
        pack_classes,
        name="pack_classes",
        out_shape=(
            jax.ShapeDtypeStruct((strips, rows * levels, LANES), i32),
            jax.ShapeDtypeStruct((8, LANES), f32),
        ),
        in_specs=[pl.BlockSpec(memory_space=pltpu.HBM)] * 3,
        out_specs=tuple(vmem(2)),
        scratch_shapes=[
            pltpu.VMEM(density_class.shape, i32),
            pltpu.VMEM(weights.shape, f32),
            pltpu.SMEM(band_of_row.shape, i32),
            pltpu.SemaphoreType.DMA((3,)),
        ],
        compiler_params=params,
    )(*[pltpu.with_memory_space_constraint(x, pltpu.HBM) for x in (density_class, weights, band_of_row)])
    laters, sums = [], None
    gram_shape = (2, HIGH_COUNT * levels, 2 * LOW_COUNT * levels)
    for piece, size in enumerate(sizes):
        last = piece + 1 == len(sizes)
        given = [own, own_maps, fars[piece], own_classes, *nears]
        given += ([sums] if piece > 0 else []) + ([scales] if last else [])
        sums, later, *weighted = pl.pallas_call(
            functools.partial(forward, piece),
            name="forward",
            out_shape=(
                jax.ShapeDtypeStruct((2, LANES) if last else gram_shape, f32),
                jax.ShapeDtypeStruct((size, 14 * levels, LANES), f32),
            )
            + ((jax.ShapeDtypeStruct((8, LANES), f32),) if last else ()),
            in_specs=vmem(len(given)),
            out_specs=tuple(vmem(3 if last else 2)),
            cost_estimate=cost(2000),
            scratch_shapes=[pltpu.VMEM((size, 16 * MAP_FIELDS, LANES), f32)]
            + ([pltpu.VMEM(gram_shape, f32)] if last else []),
            compiler_params=params,
        )(*given)
        laters.append(later)

    gathered = sums
    groups = routes(count)
    for i, group in enumerate(groups):
        others = [lax.ppermute(gathered, "lat", [(d, d ^ k) for d in range(count)]) for k in group]
        pieces = [gathered] + others
        if i == 0:
            near_share, far_share, kept = pl.pallas_call(
                adjoint_part,
                name="adjoint_part",
                out_shape=(
                    jax.ShapeDtypeStruct((rows, lon_count), f32),
                    jax.ShapeDtypeStruct((rows, lon_count), f32),
                    jax.ShapeDtypeStruct((strips, 14 * levels, LANES), f32),
                ),
                in_specs=vmem(4 + len(nears) + 2 * len(sizes)),
                out_specs=tuple(vmem(3)),
                scratch_shapes=[pltpu.VMEM((strips, 16 * 5, LANES), f32)],
                compiler_params=params,
            )(own, own_maps, own_classes, weighted[0], *nears, *fars, *laters)
            near_share, far_share = to_near(near_share), to_far(far_share)
        if i + 1 < len(groups):
            gathered = jnp.concatenate(pieces, axis=0)
    own_share = pl.pallas_call(
        own_part,
        name="own_part",
        out_shape=jax.ShapeDtypeStruct((rows, lon_count), f32),
        in_specs=vmem(3 + len(nears) + 2 * len(sizes)),
        out_specs=pl.BlockSpec(memory_space=pltpu.VMEM),
        scratch_shapes=[pltpu.VMEM((strips, 16 * 5, LANES), f32)],
        compiler_params=params,
    )(own, own_maps, kept, *nears, *fars, *laters)
    binned, gradient = pl.pallas_call(
        finish,
        name="finish",
        out_shape=(
            jax.ShapeDtypeStruct((weights.shape[0] // count, weights.shape[1]), f32),
            jax.ShapeDtypeStruct((rows, lon_count), f32),
        ),
        in_specs=vmem(3 + len(pieces)),
        out_specs=tuple(vmem(2)),
        compiler_params=params,
    )(own_share, near_share, far_share, *pieces)
    return binned, gradient


def solution(mesh):
    placed = (
        P(None, ("members", "lat"), None),
        P("lat", None),
        P(("members", "lat"), None),
        P("lat", None),
        P(None, ("members", "lat"), None),
        P("lat"),
        P(),
    )
    return jax.shard_map(
        body,
        mesh=mesh,
        in_specs=placed,
        out_specs=(P(("members", "lat"), None), P(("members", "lat"), None)),
        check_vma=False,
    )
```

```python
import functools

import jax
import jax.numpy as jnp
from jax import lax
from jax.experimental import pallas as pl
from jax.experimental.pallas import tpu as pltpu
from jax.sharding import PartitionSpec as P

STEPS = 3
vertical_mix = 0.05

LANES = 128
GHOST = 4
OWN = LANES - 2 * GHOST
HIGH_COUNT = 9
LOW_COUNT = 8
LOW_SHIFT = 3
PIECES = (0, 7, 12)
NEAR_PIECES = (0, 6, 12)
VMEM_LIMIT = 16 * 1024 * 1024


def strip_of(row, j, lon_count):
    first = OWN * j - GHOST
    last = first + LANES
    if first < 0:
        return jnp.concatenate([row[:, first + lon_count :], row[:, :last]], axis=1)
    if last > lon_count:
        return jnp.concatenate([row[:, first:], row[:, : last - lon_count]], axis=1)
    return row[:, first:last]


def piece_of(j, bounds=None):
    bounds = PIECES if bounds is None else bounds
    return max(p for p in range(len(bounds) - 1) if bounds[p] <= j)


def near_place(nears, j):
    piece = piece_of(j, NEAR_PIECES)
    first, last = NEAR_PIECES[piece : piece + 2]
    return nears[piece], j - first, last - first


def is_odd():
    return lax.rem(lax.axis_index("lat"), 2) == 1


def oriented(ref, t, odd):
    last = ref.shape[1] - 1
    order = level_order(ref.shape[0])
    up = jnp.concatenate([ref[k, t : t + 1, :] for k in order], axis=0)
    down = jnp.concatenate([ref[k, last - t : last - t + 1, :] for k in order], axis=0)
    return jnp.where(odd, down, up)


def bring(sources, held, arrived):
    copies = [pltpu.make_async_copy(a, b, arrived.at[i]) for i, (a, b) in enumerate(zip(sources, held))]
    for copy in copies:
        copy.start()
    for copy in copies:
        copy.wait()


def flipped_map(ref, odd):
    field = ref[...].astype(jnp.float32)
    flipped = jnp.concatenate([field[r : r + 1] for r in reversed(range(field.shape[0]))], axis=0)
    return jnp.where(odd, field, flipped), jnp.where(odd, flipped, field)


def fill_far(piece, far, held):
    tracer, maps = held[0], held[1:]
    levels, _, lon_count = tracer.shape
    odd = is_odd()
    group = range(PIECES[piece], PIECES[piece + 1])
    for t in range(STEPS):
        field = oriented(tracer, t, odd)
        for u, j in enumerate(group):
            at = (u * STEPS + STEPS - 1 - t) * levels
            far[at : at + levels, :] = strip_of(field, j, lon_count)
    for a, ref in enumerate(maps):
        down, _ = flipped_map(ref, odd)
        for u, j in enumerate(group):
            at = len(group) * STEPS * levels + (3 * u + a) * STEPS
            far[at : at + STEPS, :] = strip_of(down, j, lon_count)[1:]


def pack_first(*refs):
    sources, far, held, arrived = refs[:4], refs[4], refs[5:9], refs[9]
    bring(sources, held, arrived)
    fill_far(0, far, held)


def pack_fields(*refs):
    parts, near_parts = len(PIECES) - 2, len(NEAR_PIECES) - 1
    sources, (own, own_maps) = refs[:4], refs[4:6]
    nears, refs = refs[6 : 6 + near_parts], refs[6 + near_parts :]
    fars, held, arrived = refs[:parts], refs[parts : 4 + parts], refs[4 + parts]
    bring(sources, held, arrived)
    tracer = held[0]
    levels, rows, lon_count = tracer.shape
    strips = lon_count // OWN
    odd = is_odd()
    for i, far in enumerate(fars):
        fill_far(i + 1, far, held)
    for t in range(rows):
        field = oriented(tracer, t, odd)
        for j in range(strips):
            strip = strip_of(field, j, lon_count)
            own[j, t * levels : (t + 1) * levels, :] = strip
            if t > 0:
                near, local, _ = near_place(nears, j)
                at = (local * STEPS + rows - 1 - t) * levels
                near[at : at + levels, :] = strip
    for a, ref in enumerate(held[1:]):
        down, up = flipped_map(ref, odd)
        for j in range(strips):
            own_maps[j, a * 4 : a * 4 + 4, :] = strip_of(up, j, lon_count)
            near, local, count = near_place(nears, j)
            at = count * STEPS * levels + (3 * local + a) * STEPS
            near[at : at + STEPS, :] = strip_of(down, j, lon_count)[:STEPS]
    own_maps[:, 12:, :] = jnp.zeros_like(own_maps[:, 12:, :])


def pack_classes(*refs):
    sources, (own, scales), held, arrived = refs[:3], refs[3:5], refs[5:8], refs[8]
    bring(sources, held, arrived)
    classes, weights, band_of_row = held
    levels, rows, lon_count = classes.shape
    strips = lon_count // OWN
    odd = is_odd()
    for t in range(rows):
        field = oriented(classes, t, odd)
        for j in range(strips):
            strip = strip_of(field, j, lon_count)
            own[j, t * levels : (t + 1) * levels, :] = strip
    class_count = weights.shape[1]
    label = lax.broadcasted_iota(jnp.int32, (1, LANES), 1)
    scale_rows, band_rows = [], []
    for pair in range(2):
        band = band_of_row[jnp.where(odd, 3 - 2 * pair, 2 * pair)]
        scale = weights[pl.ds(band, 1), :]
        scale_rows.append(jnp.concatenate([scale, jnp.zeros((1, LANES - class_count), jnp.float32)], axis=1))
        band_rows.append(jnp.where(label == LANES - 1, band.astype(jnp.float32), 0.0))
    blank = jnp.zeros((2, LANES), jnp.float32)
    scales[...] = jnp.concatenate(scale_rows + [blank] + band_rows + [blank], axis=0)


def east(x):
    return pltpu.roll(x, LANES - 1, 1)


def west(x):
    return pltpu.roll(x, 1, 1)


MAP_FIELDS = 7


def level_order(levels):
    half = levels // 2
    return [2 * (i % half) + i // half for i in range(levels)]


class Coefficients:
    blocks = {
        "wet": 0, "east_open": 1, "north_open": 2,
        "east_mix": 3, "north_mix": 4, "east_dir": 5, "north_dir": 6,
    }

    def __init__(self, maps, j, levels):
        order = lax.broadcasted_iota(jnp.int32, (levels, LANES), 0)
        half = levels // 2
        self.level = (2 * (order & (half - 1)) + jnp.where(order < half, 0, 1)).astype(jnp.float32)
        self.levels = levels
        self.maps = maps
        self.j = j
        self.cache = {}

    def row(self, kind, t):
        at = 16 * self.blocks[kind] + t + STEPS
        return jnp.broadcast_to(self.maps[self.j, at : at + 1, :], (self.levels, LANES))

    def get(self, kind, t):
        if (kind, t) not in self.cache:
            side, _, what = kind.partition("_")
            if kind == "column":
                value = jnp.where(self.level + 1.0 < self.row("wet", t), vertical_mix, 0.0)
            elif kind == "wet" or what == "open":
                value = self.level < self.row(kind, t)
            else:
                value = jnp.where(self.get(side + "_open", t), self.row(kind, t), 0.0)
            self.cache[kind, t] = value
        return self.cache[kind, t]


def column(field, coefficient):
    half = field.shape[0] // 2
    even, odd = field[:half], field[half:]
    after_even = coefficient[:half] * (odd - even)
    after_odd = coefficient[half:] * (pltpu.roll(even, half - 1, 0) - odd)
    return jnp.concatenate([after_even - pltpu.roll(after_odd, 1, 0), after_odd - after_even], axis=0)


def gaps(fields, rows):
    turned = [{t: east(field[t]) for t in rows} for field in fields]
    to_east = [{t: turn[t] - field[t] for t in rows} for turn, field in zip(turned, fields)]
    faces = range(rows[0] - 1, rows[-1] + 1)
    to_north = [{t: field[t + 1] - field[t] for t in faces} for field in fields]
    return list(zip(to_east, to_north))


def fluxes(coefs, kind, steps):
    return [
        (
            {t: coef.get("east_" + kind, t) * to_east[t] for t in to_east},
            {t: coef.get("north_" + kind, t) * to_north[t] for t in to_north},
        )
        for coef, (to_east, to_north) in zip(coefs, steps)
    ]


def both(ones, others):
    return [
        tuple({t: a[t] + b[t] for t in a} for a, b in zip(one, other)) for one, other in zip(ones, others)
    ]


def gathered_in(flux, rows, fields=None, coefs=None):
    turned = [{t: west(across[t]) for t in rows} for across, _ in flux]
    still = [{t: along[t] - along[t - 1] for t in rows} for _, along in flux]
    if fields is not None:
        still = [
            {t: rest[t] + (field[t] + column(field[t], coef.get("column", t))) for t in rows}
            for rest, field, coef in zip(still, fields, coefs)
        ]
    return [
        {t: rest[t] + (across[t] - turn[t]) for t in rows}
        for rest, (across, _), turn in zip(still, flux, turned)
    ]


def face_maps(own_maps, nears, fars, maps, strips, levels, kinds=(0, 1, 2)):
    count, edge = lax.axis_size("lat"), lax.axis_index("lat")
    keep = jnp.where(jnp.logical_and(edge != 0, edge != count - 1), 1.0, 0.0)

    def north(x):
        return pltpu.roll(x, 15, 0)

    for i, j in enumerate(strips):
        whole = []
        piece = piece_of(j)
        for a in kinds:
            at = (PIECES[piece + 1] - PIECES[piece]) * STEPS * levels + (3 * (j - PIECES[piece]) + a) * STEPS
            low = fars[piece][at : at + STEPS, :]
            if a == 2:
                low = low * keep
            near, local, size = near_place(nears, j)
            at = size * STEPS * levels + (3 * local + a) * STEPS
            high = near[at : at + STEPS, :]
            whole.append(jnp.concatenate([low, own_maps[j, 4 * a : 4 * a + 4, :], high, high, high], axis=0))
        depth = whole.pop()
        blocks = [depth] + [jnp.minimum(depth, f(depth)) for f in (east, north)]
        blocks += [0.5 * (x + f(x)) for x in whole for f in (east, north)]
        for b, block in enumerate(blocks):
            maps[i, 16 * b : 16 * b + 16, :] = block


def class_hits(value, label, levels):
    top = value.astype(jnp.bfloat16)
    bottom = (value - top.astype(jnp.float32)).astype(jnp.bfloat16)
    high = (label >> LOW_SHIFT).astype(jnp.float32).astype(jnp.bfloat16)
    low = (label & (LOW_COUNT - 1)).astype(jnp.float32).astype(jnp.bfloat16)
    none = jnp.zeros((levels, LANES), jnp.bfloat16)
    one = jnp.ones((levels, LANES), jnp.bfloat16)
    left = [jnp.where(high == jnp.bfloat16(h), one, none) for h in range(HIGH_COUNT)]
    picks = [low == jnp.bfloat16(l) for l in range(LOW_COUNT)]
    right = [jnp.where(p, part, none) for part in (top, bottom) for p in picks]
    return jnp.concatenate(left, axis=0), jnp.concatenate(right, axis=0)


def later_row(n, t):
    return (n - 1) * 8 + t + STEPS - n


def forward(piece, *refs):
    last = piece + 2 == len(PIECES)
    refs = list(refs)
    near_parts = len(NEAR_PIECES) - 1
    own, own_maps, far, classes = refs[:4]
    nears = refs[4 : 4 + near_parts]
    del refs[: 4 + near_parts]
    before = refs.pop(0) if piece > 0 else None
    scales = refs.pop(0) if last else None
    out, later = refs[:2]
    weighted, maps = refs[2:] if last else (None, refs[2])
    levels = own.shape[1] // 4
    group = list(range(PIECES[piece], PIECES[piece + 1]))
    face_maps(own_maps, nears, {piece: far}, maps, group, levels)
    lane = lax.broadcasted_iota(jnp.int32, (levels, LANES), 1)
    inner = jnp.logical_and(lane >= GHOST, lane < LANES - GHOST)
    coefs = [Coefficients(maps, u, levels) for u in range(len(group))]
    fields, tangents = [], None
    for u, j in enumerate(group):
        field = {t: own[j, t * levels : (t + 1) * levels, :] for t in range(4)}
        for s in range(STEPS):
            at = (u * STEPS + s) * levels
            field[s - STEPS] = far[at : at + levels, :]
            near, local, _ = near_place(nears, j)
            at = (local * STEPS + s) * levels
            field[4 + s] = near[at : at + levels, :]
        fields.append(field)
    for n in range(STEPS):
        rows = list(range(n + 1 - STEPS, 4 + STEPS - n - 1))
        steps = gaps(fields, rows)
        push = fluxes(coefs, "dir", steps)
        if n == 0:
            following = gathered_in(push, rows)
        else:
            push = both(push, fluxes(coefs, "mix", gaps(tangents, rows)))
            following = gathered_in(push, rows, tangents, coefs)
        tangents = following
        if n + 1 < STEPS:
            fields = gathered_in(fluxes(coefs, "mix", steps), rows, fields, coefs)
            for u in range(len(group)):
                for t in rows:
                    at = later_row(n + 1, t) * levels
                    later[u, at : at + levels, :] = fields[u][t]
    finished = []
    for pair in range(2):
        lefts, rights = [], []
        for u, j in enumerate(group):
            for t in (2 * pair, 2 * pair + 1):
                chosen = jnp.logical_and(inner, coefs[u].get("wet", t))
                value = jnp.where(chosen, tangents[u][t], 0.0)
                left, right = class_hits(value, classes[j, t * levels : (t + 1) * levels, :], levels)
                lefts.append(left)
                rights.append(right)
        gram = lax.dot_general(
            jnp.concatenate(lefts, axis=1),
            jnp.concatenate(rights, axis=1),
            (((1,), (1,)), ((), ())),
            preferred_element_type=jnp.float32,
        )
        gram = gram if before is None else before[pair] + gram
        if last:
            finished.append(gram)
        else:
            out[pair] = gram
    if last:
        class_sums(finished, scales, out, weighted, levels)


def class_sums(grams, scales, sums, weighted, levels):
    width = 2 * LOW_COUNT * levels
    own_level = lax.broadcasted_iota(jnp.int32, (levels, width), 0)
    other_level = lax.broadcasted_iota(jnp.int32, (levels, width), 1) & (levels - 1)
    diagonal = own_level == other_level
    sheets = []
    for pair in range(2):
        for h in range(HIGH_COUNT):
            sheet = jnp.where(diagonal, grams[pair][h * levels : (h + 1) * levels, :], 0.0)
            sheets.append(jnp.sum(sheet, axis=0, keepdims=True))
        sheets.append(jnp.zeros((16 - HIGH_COUNT, width), jnp.float32))
    rest = jnp.concatenate(sheets, axis=0)
    parts = []
    for _ in range(3):
        part = rest.astype(jnp.bfloat16)
        rest = rest - part.astype(jnp.float32)
        parts.append(part)
    at_low = (lax.broadcasted_iota(jnp.int32, (width, LANES), 0) >> (levels.bit_length() - 1)) & (LOW_COUNT - 1)
    of_low = lax.broadcasted_iota(jnp.int32, (width, LANES), 1) & (LOW_COUNT - 1)
    gather = jnp.where(at_low == of_low, 1.0, 0.0).astype(jnp.bfloat16)
    added = jnp.dot(jnp.concatenate(parts, axis=0), gather, preferred_element_type=jnp.float32)
    added = (added[64:96] + added[32:64]) + added[0:32]
    here = lax.broadcasted_iota(jnp.int32, (16, LANES), 0)
    label = lax.broadcasted_iota(jnp.int32, (16, LANES), 1)
    totals = [
        jnp.sum(
            jnp.where(here == (label >> LOW_SHIFT), added[16 * p : 16 * p + 16], 0.0), axis=0, keepdims=True
        )
        for p in range(2)
    ]
    finish_sums(scales, totals, sums, weighted)


def finish_sums(scales, totals, sums, weighted):
    sums[...] = jnp.concatenate([totals[p] + scales[4 + p : 5 + p, :] for p in range(2)], axis=0)
    weighted[0:2, :] = jnp.concatenate([scales[p : p + 1, :] * totals[p] for p in range(2)], axis=0)


def finish(own_share, near_share, far_share, *refs):
    pieces, binned, gradient = refs[:-2], refs[-2], refs[-1]
    up = own_share[...] + (near_share[...] + far_share[...])
    down = jnp.concatenate([up[t : t + 1] for t in reversed(range(up.shape[0]))], axis=0)
    gradient[...] = jnp.where(is_odd(), down, up)
    band_own, class_count = binned.shape
    first = lax.axis_index("lat") * band_own
    found = [jnp.zeros((1, LANES), jnp.float32) for _ in range(band_own)]
    for piece in pieces:
        totals = piece[...]
        bands = jnp.broadcast_to(totals[:, LANES - 1 :], totals.shape)
        for m in range(band_own):
            hit = jnp.where(bands == (first + m).astype(jnp.float32), totals, 0.0)
            found[m] = found[m] + jnp.sum(hit, axis=0, keepdims=True)
    whole = jnp.concatenate(found, axis=0)
    binned[...] = whole[:, :class_count]


def base_rows(n, j, rows, own, nears, fars, laters):
    levels = own.shape[1] // 4
    piece = piece_of(j)
    local = j - PIECES[piece]
    field = {}
    for t in rows:
        if n > 0:
            at = later_row(n, t) * levels
            field[t] = laters[piece][local, at : at + levels, :]
        elif t < 0:
            at = (local * STEPS + t + STEPS) * levels
            field[t] = fars[piece][at : at + levels, :]
        elif t < 4:
            field[t] = own[j, t * levels : (t + 1) * levels, :]
        else:
            near, place, _ = near_place(nears, j)
            at = (place * STEPS + t - 4) * levels
            field[t] = near[at : at + levels, :]
    return field


def kept_row(n, t):
    if n == STEPS - 1:
        return t
    return 4 + t + 1 if n > 0 else 10 + {-1: 0, 0: 1, 3: 2, 4: 3}[t]


def add_terms(total, basis, steps, places, shift):
    for t in places:
        gap = (shift(basis[t]) if shift else basis[t + 1]) - basis[t]
        term = gap * steps[t]
        total[t] = total[t] + term if t in total else term


def shares(coefs, east_total, north_total, rows):
    none = jnp.zeros((1, LANES), jnp.float32)
    pad = [none] * (-len(rows) % 8)

    def summed(coef, kind, total):
        return {
            t: jnp.sum(jnp.where(coef.get(kind, t), x, 0.0), axis=0, keepdims=True) for t, x in total.items()
        }

    across = []
    for coef, total in zip(coefs, east_total):
        sums = summed(coef, "east_open", total)
        across.append(jnp.concatenate([sums.get(t, none) for t in rows] + pad, axis=0))
    turned = [west(x) for x in across]
    strips = []
    for coef, total, x, turn in zip(coefs, north_total, across, turned):
        sums = summed(coef, "north_open", total)
        along = [sums.get(t, none) + sums.get(t - 1, none) for t in rows]
        strips.append(-0.5 * (jnp.concatenate(along + pad, axis=0) + (x + turn)))
    whole = jnp.concatenate([x[:, GHOST : LANES - GHOST] for x in strips], axis=1)
    return {t: whole[i : i + 1] for i, t in enumerate(rows)}


def adjoint_part(own, own_maps, classes, weighted, *refs):
    parts, near_parts = len(PIECES) - 1, len(NEAR_PIECES) - 1
    nears, refs = refs[:near_parts], refs[near_parts:]
    fars, laters = refs[:parts], refs[parts : 2 * parts]
    near_share, far_share, kept, maps = refs[2 * parts :]
    strips = own.shape[0]
    levels = own.shape[1] // 4
    group = list(range(strips))
    face_maps(own_maps, nears, fars, maps, group, levels, kinds=(0, 2))
    coefs = [Coefficients(maps, j, levels) for j in group]
    adjoints = []
    for j in group:
        adjoint = {}
        for t in range(4):
            label = classes[j, t * levels : (t + 1) * levels, :]
            row = t // 2
            table = jnp.broadcast_to(weighted[row : row + 1, :], (8, LANES))
            value = jnp.concatenate(
                [jnp.take_along_axis(table, label[k : k + 8, :], axis=1) for k in range(0, levels, 8)], axis=0
            )
            adjoint[t] = jnp.where(coefs[j].get("wet", t), value, 0.0)
        adjoints.append(adjoint)
    east_total = [{} for _ in group]
    north_total = [{} for _ in group]
    for n in reversed(range(STEPS)):
        rows = list(range(n + 1 - STEPS, 3 + STEPS - n))
        low, high = rows[0], rows[-1]
        for j in group:
            for t in [t for t in adjoints[j] if -1 <= t <= 4]:
                at = kept_row(n, t) * levels
                kept[j, at : at + levels, :] = adjoints[j][t]
        outer = [t for t in rows if t < 0 or t > 3]
        made = [t for t in rows if n != 1 or t < 1 or t > 2]
        turning = made if n > 0 else outer
        turned = [{t: east(field[t]) for t in turning} for field in adjoints]
        to_east = [{t: turn[t] - field[t] for t in turn} for turn, field in zip(turned, adjoints)]
        to_north = [
            {
                low - 1: field[low],
                high: -field[high],
                **{t: field[t + 1] - field[t] for t in rows[:-1] if t in field and t + 1 in field},
            }
            for field in adjoints
        ]
        if n > 0:
            across = [{t: coef.get("east_mix", t) * x[t] for t in made} for coef, x in zip(coefs, to_east)]
            turned = [{t: west(x[t]) for t in made} for x in across]
            along = [{t: coef.get("north_mix", t) * x[t] for t in x} for coef, x in zip(coefs, to_north)]
            following = []
            for j in group:
                field, flux = adjoints[j], along[j]
                new = {low - 1: flux[low - 1], high + 1: -flux[high]}
                for t in made:
                    still = field[t] + column(field[t], coefs[j].get("column", t)) + (flux[t] - flux[t - 1])
                    new[t] = still + (across[j][t] - turned[j][t])
                following.append(new)
            adjoints = following
        for j in group:
            needed = [t for t in range(low - 1, high + 2) if t <= 0 or t >= 3]
            basis = base_rows(n, j, needed, own, nears, fars, laters)
            faces = [t for t in to_north[j] if t < 0 or t > 2]
            add_terms(east_total[j], basis, to_east[j], outer, east)
            add_terms(north_total[j], basis, to_north[j], faces, None)
    low_rows, high_rows = [-3, -2, -1], [4, 5, 6]
    share = shares(coefs, east_total, north_total, low_rows + high_rows)
    blank = jnp.zeros_like(share[-1])
    far_share[...] = jnp.concatenate([share[-1], share[-2], share[-3], blank], axis=0)
    near_share[...] = jnp.concatenate([blank, share[6], share[5], share[4]], axis=0)


def own_part(own, own_maps, kept, *refs):
    parts, near_parts = len(PIECES) - 1, len(NEAR_PIECES) - 1
    nears, refs = refs[:near_parts], refs[near_parts:]
    fars, laters = refs[:parts], refs[parts : 2 * parts]
    own_share, maps = refs[2 * parts :]
    levels = own.shape[1] // 4
    group = list(range(own.shape[0]))
    face_maps(own_maps, nears, fars, maps, group, levels, kinds=(0, 2))
    coefs = [Coefficients(maps, j, levels) for j in group]
    east_total = [{} for _ in group]
    north_total = [{} for _ in group]

    def adjoint_of(n, j, rows):
        return {t: kept[j, kept_row(n, t) * levels : (kept_row(n, t) + 1) * levels, :] for t in rows}

    middle = [adjoint_of(1, j, range(4)) for j in group]
    across, along = zip(*fluxes(coefs, "mix", gaps(middle, [1, 2])))
    inner = gathered_in(list(zip(across, along)), [1, 2], middle, coefs)
    for n in range(STEPS):
        last = n == STEPS - 1
        adjoints = []
        for j in group:
            if n == 0:
                adjoints.append({**adjoint_of(0, j, (-1, 0, 3, 4)), **inner[j]})
            else:
                adjoints.append(adjoint_of(n, j, range(4) if last else range(-1, 5)))
        for j, adjoint in zip(group, adjoints):
            to_east = {t: east(adjoint[t]) - adjoint[t] for t in range(4)}
            faces = range(3) if last else range(-1, 4)
            to_north = {t: adjoint[t + 1] - adjoint[t] for t in faces}
            if last:
                to_north.update({-1: adjoint[0], 3: -adjoint[3]})
            basis = base_rows(n, j, range(-1, 5), own, nears, fars, laters)
            add_terms(east_total[j], basis, to_east, range(4), east)
            add_terms(north_total[j], basis, to_north, range(-1, 4), None)
    share = shares(coefs, east_total, north_total, list(range(4)))
    own_share[...] = jnp.concatenate([share[t] for t in range(4)], axis=0)


def near_pairs(count):
    return [(i, i ^ 1) for i in range(count)]


def far_pairs(members, count):
    pairs = []
    for m in range(members):
        for i in range(1, count - 1, 2):
            pairs += [(m * count + i, m * count + i + 1), (m * count + i + 1, m * count + i)]
        for i in (0, count - 1):
            pairs.append((m * count + i, (m ^ 1) * count + i))
    return pairs


def routes(count):
    bits = count.bit_length() - 1
    groups = []
    for bit in range(bits - 2, -1, -2):
        one, two = 1 << bit, 2 << bit
        groups.append([one, one + two, two] if bit > 0 else [3, 2, 1])
    return groups + ([[1]] if bits % 2 else [])


def vmem(count):
    return [pl.BlockSpec(memory_space=pltpu.VMEM)] * count


def cost(nanoseconds):
    return pl.CostEstimate(flops=1153500 * nanoseconds, bytes_accessed=3690 * nanoseconds, transcendentals=0)


def body(tracer, diffusivity, direction, column_depth, density_class, band_of_row, weights):
    levels, rows, lon_count = tracer.shape
    strips = lon_count // OWN
    count = lax.axis_size("lat")
    members = lax.axis_size("members")
    params = pltpu.CompilerParams(vmem_limit_bytes=VMEM_LIMIT)
    f32, i32 = jnp.float32, jnp.int32
    halo = strips * STEPS * levels
    payload = halo + strips * 9

    def to_near(x):
        return lax.ppermute(x, "lat", near_pairs(count))

    def to_far(x):
        return lax.ppermute(x, ("members", "lat"), far_pairs(members, count))

    sizes = [b - a for a, b in zip(PIECES, PIECES[1:])]
    near_sizes = [b - a for a, b in zip(NEAR_PIECES, NEAR_PIECES[1:])]
    fields = (tracer, diffusivity, direction, column_depth)
    in_place = [pltpu.with_memory_space_constraint(x, pltpu.HBM) for x in fields]
    taken = dict(
        in_specs=[pl.BlockSpec(memory_space=pltpu.HBM)] * 4,
        scratch_shapes=[pltpu.VMEM(x.shape, x.dtype) for x in fields] + [pltpu.SemaphoreType.DMA((4,))],
        compiler_params=params,
    )
    far_shapes = [jax.ShapeDtypeStruct((payload // strips * size, LANES), f32) for size in sizes]
    first_out = pl.pallas_call(
        pack_first,
        name="pack_first",
        out_shape=far_shapes[0],
        out_specs=pl.BlockSpec(memory_space=pltpu.VMEM),
        **taken,
    )(*in_place)
    fars = [to_far(first_out)]
    late_fields = lax.optimization_barrier((*fields, first_out))[: len(fields)]
    in_place = [pltpu.with_memory_space_constraint(x, pltpu.HBM) for x in late_fields]
    own, own_maps, *outs = pl.pallas_call(
        pack_fields,
        name="pack_fields",
        out_shape=(
            jax.ShapeDtypeStruct((strips, rows * levels, LANES), f32),
            jax.ShapeDtypeStruct((strips, 16, LANES), f32),
            *[jax.ShapeDtypeStruct((payload // strips * size, LANES), f32) for size in near_sizes],
            *far_shapes[1:],
        ),
        out_specs=tuple(vmem(1 + len(near_sizes) + len(sizes))),
        **taken,
    )(*in_place)
    nears = [to_near(x) for x in outs[: len(near_sizes)]]
    fars += [to_far(x) for x in outs[len(near_sizes) :]]

    own_classes, scales = pl.pallas_call(
        pack_classes,
        name="pack_classes",
        out_shape=(
            jax.ShapeDtypeStruct((strips, rows * levels, LANES), i32),
            jax.ShapeDtypeStruct((8, LANES), f32),
        ),
        in_specs=[pl.BlockSpec(memory_space=pltpu.HBM)] * 3,
        out_specs=tuple(vmem(2)),
        scratch_shapes=[
            pltpu.VMEM(density_class.shape, i32),
            pltpu.VMEM(weights.shape, f32),
            pltpu.SMEM(band_of_row.shape, i32),
            pltpu.SemaphoreType.DMA((3,)),
        ],
        compiler_params=params,
    )(*[pltpu.with_memory_space_constraint(x, pltpu.HBM) for x in (density_class, weights, band_of_row)])
    laters, sums = [], None
    gram_shape = (2, HIGH_COUNT * levels, 2 * LOW_COUNT * levels)
    for piece, size in enumerate(sizes):
        last = piece + 1 == len(sizes)
        given = [own, own_maps, fars[piece], own_classes, *nears]
        given += ([sums] if piece > 0 else []) + ([scales] if last else [])
        sums, later, *weighted = pl.pallas_call(
            functools.partial(forward, piece),
            name="forward",
            out_shape=(
                jax.ShapeDtypeStruct((2, LANES) if last else gram_shape, f32),
                jax.ShapeDtypeStruct((size, 14 * levels, LANES), f32),
            )
            + ((jax.ShapeDtypeStruct((8, LANES), f32),) if last else ()),
            in_specs=vmem(len(given)),
            out_specs=tuple(vmem(3 if last else 2)),
            cost_estimate=cost(2000),
            scratch_shapes=[pltpu.VMEM((size, 16 * MAP_FIELDS, LANES), f32)],
            compiler_params=params,
        )(*given)
        laters.append(later)

    gathered = sums
    groups = routes(count)
    for i, group in enumerate(groups):
        others = [lax.ppermute(gathered, "lat", [(d, d ^ k) for d in range(count)]) for k in group]
        pieces = [gathered] + others
        if i == 0:
            near_share, far_share, kept = pl.pallas_call(
                adjoint_part,
                name="adjoint_part",
                out_shape=(
                    jax.ShapeDtypeStruct((rows, lon_count), f32),
                    jax.ShapeDtypeStruct((rows, lon_count), f32),
                    jax.ShapeDtypeStruct((strips, 14 * levels, LANES), f32),
                ),
                in_specs=vmem(4 + len(nears) + 2 * len(sizes)),
                out_specs=tuple(vmem(3)),
                scratch_shapes=[pltpu.VMEM((strips, 16 * 5, LANES), f32)],
                compiler_params=params,
            )(own, own_maps, own_classes, weighted[0], *nears, *fars, *laters)
            near_share, far_share = to_near(near_share), to_far(far_share)
        if i + 1 < len(groups):
            gathered = jnp.concatenate(pieces, axis=0)
    own_share = pl.pallas_call(
        own_part,
        name="own_part",
        out_shape=jax.ShapeDtypeStruct((rows, lon_count), f32),
        in_specs=vmem(3 + len(nears) + 2 * len(sizes)),
        out_specs=pl.BlockSpec(memory_space=pltpu.VMEM),
        scratch_shapes=[pltpu.VMEM((strips, 16 * 5, LANES), f32)],
        compiler_params=params,
    )(own, own_maps, kept, *nears, *fars, *laters)
    binned, gradient = pl.pallas_call(
        finish,
        name="finish",
        out_shape=(
            jax.ShapeDtypeStruct((weights.shape[0] // count, weights.shape[1]), f32),
            jax.ShapeDtypeStruct((rows, lon_count), f32),
        ),
        in_specs=vmem(3 + len(pieces)),
        out_specs=tuple(vmem(2)),
        compiler_params=params,
    )(own_share, near_share, far_share, *pieces)
    return binned, gradient


def solution(mesh):
    placed = (
        P(None, ("members", "lat"), None),
        P("lat", None),
        P(("members", "lat"), None),
        P("lat", None),
        P(None, ("members", "lat"), None),
        P("lat"),
        P(),
    )
    return jax.shard_map(
        body,
        mesh=mesh,
        in_specs=placed,
        out_specs=(P(("members", "lat"), None), P(("members", "lat"), None)),
        check_vma=False,
    )
```

```python
import functools

import jax
import jax.numpy as jnp
from jax import lax
from jax.experimental import pallas as pl
from jax.experimental.pallas import tpu as pltpu
from jax.sharding import PartitionSpec as P

STEPS = 3
vertical_mix = 0.05

LANES = 128
GHOST = 4
OWN = LANES - 2 * GHOST
HIGH_COUNT = 9
LOW_COUNT = 8
LOW_SHIFT = 3
PIECES = (0, 7, 12)
NEAR_PIECES = (0, 6, 12)
VMEM_LIMIT = 16 * 1024 * 1024


def strip_of(row, j, lon_count):
    first = OWN * j - GHOST
    last = first + LANES
    if first < 0:
        return jnp.concatenate([row[:, first + lon_count :], row[:, :last]], axis=1)
    if last > lon_count:
        return jnp.concatenate([row[:, first:], row[:, : last - lon_count]], axis=1)
    return row[:, first:last]


def piece_of(j, bounds=None):
    bounds = PIECES if bounds is None else bounds
    return max(p for p in range(len(bounds) - 1) if bounds[p] <= j)


def near_place(nears, j):
    piece = piece_of(j, NEAR_PIECES)
    first, last = NEAR_PIECES[piece : piece + 2]
    return nears[piece], j - first, last - first


def is_odd():
    return lax.rem(lax.axis_index("lat"), 2) == 1


def oriented(ref, t, odd):
    last = ref.shape[1] - 1
    order = level_order(ref.shape[0])
    up = jnp.concatenate([ref[k, t : t + 1, :] for k in order], axis=0)
    down = jnp.concatenate([ref[k, last - t : last - t + 1, :] for k in order], axis=0)
    return jnp.where(odd, down, up)


def bring(sources, held, arrived):
    copies = [pltpu.make_async_copy(a, b, arrived.at[i]) for i, (a, b) in enumerate(zip(sources, held))]
    for copy in copies:
        copy.start()
    for copy in copies:
        copy.wait()


def flipped_map(ref, odd):
    field = ref[...].astype(jnp.float32)
    flipped = jnp.concatenate([field[r : r + 1] for r in reversed(range(field.shape[0]))], axis=0)
    return jnp.where(odd, field, flipped), jnp.where(odd, flipped, field)


def fill_far(piece, far, held):
    tracer, maps = held[0], held[1:]
    levels, _, lon_count = tracer.shape
    odd = is_odd()
    group = range(PIECES[piece], PIECES[piece + 1])
    for t in range(STEPS):
        field = oriented(tracer, t, odd)
        for u, j in enumerate(group):
            at = (u * STEPS + STEPS - 1 - t) * levels
            far[at : at + levels, :] = strip_of(field, j, lon_count)
    for a, ref in enumerate(maps):
        down, _ = flipped_map(ref, odd)
        for u, j in enumerate(group):
            at = len(group) * STEPS * levels + (3 * u + a) * STEPS
            far[at : at + STEPS, :] = strip_of(down, j, lon_count)[1:]


def pack_first(*refs):
    sources, far, held, arrived = refs[:4], refs[4], refs[5:9], refs[9]
    bring(sources, held, arrived)
    fill_far(0, far, held)


def pack_fields(*refs):
    parts, near_parts = len(PIECES) - 2, len(NEAR_PIECES) - 1
    sources, (own, own_maps) = refs[:4], refs[4:6]
    nears, refs = refs[6 : 6 + near_parts], refs[6 + near_parts :]
    fars, held, arrived = refs[:parts], refs[parts : 4 + parts], refs[4 + parts]
    bring(sources, held, arrived)
    tracer = held[0]
    levels, rows, lon_count = tracer.shape
    strips = lon_count // OWN
    odd = is_odd()
    for i, far in enumerate(fars):
        fill_far(i + 1, far, held)
    for t in range(rows):
        field = oriented(tracer, t, odd)
        for j in range(strips):
            strip = strip_of(field, j, lon_count)
            own[j, t * levels : (t + 1) * levels, :] = strip
            if t > 0:
                near, local, _ = near_place(nears, j)
                at = (local * STEPS + rows - 1 - t) * levels
                near[at : at + levels, :] = strip
    for a, ref in enumerate(held[1:]):
        down, up = flipped_map(ref, odd)
        for j in range(strips):
            own_maps[j, a * 4 : a * 4 + 4, :] = strip_of(up, j, lon_count)
            near, local, count = near_place(nears, j)
            at = count * STEPS * levels + (3 * local + a) * STEPS
            near[at : at + STEPS, :] = strip_of(down, j, lon_count)[:STEPS]
    own_maps[:, 12:, :] = jnp.zeros_like(own_maps[:, 12:, :])


def pack_classes(*refs):
    sources, (own, scales), held, arrived = refs[:3], refs[3:5], refs[5:8], refs[8]
    bring(sources, held, arrived)
    classes, weights, band_of_row = held
    levels, rows, lon_count = classes.shape
    strips = lon_count // OWN
    odd = is_odd()
    for t in range(rows):
        field = oriented(classes, t, odd)
        for j in range(strips):
            strip = strip_of(field, j, lon_count)
            own[j, t * levels : (t + 1) * levels, :] = strip
    class_count = weights.shape[1]
    label = lax.broadcasted_iota(jnp.int32, (1, LANES), 1)
    scale_rows, band_rows = [], []
    for pair in range(2):
        band = band_of_row[jnp.where(odd, 3 - 2 * pair, 2 * pair)]
        scale = weights[pl.ds(band, 1), :]
        scale_rows.append(jnp.concatenate([scale, jnp.zeros((1, LANES - class_count), jnp.float32)], axis=1))
        band_rows.append(jnp.where(label == LANES - 1, band.astype(jnp.float32), 0.0))
    blank = jnp.zeros((2, LANES), jnp.float32)
    scales[...] = jnp.concatenate(scale_rows + [blank] + band_rows + [blank], axis=0)


def east(x):
    return pltpu.roll(x, LANES - 1, 1)


def west(x):
    return pltpu.roll(x, 1, 1)


MAP_FIELDS = 7


def level_order(levels):
    half = levels // 2
    return [2 * (i % half) + i // half for i in range(levels)]


class Coefficients:
    blocks = {
        "wet": 0, "east_open": 1, "north_open": 2,
        "east_mix": 3, "north_mix": 4, "east_dir": 5, "north_dir": 6,
    }

    def __init__(self, maps, j, levels):
        order = lax.broadcasted_iota(jnp.int32, (levels, LANES), 0)
        half = levels // 2
        self.level = (2 * (order & (half - 1)) + jnp.where(order < half, 0, 1)).astype(jnp.float32)
        self.levels = levels
        self.maps = maps
        self.j = j
        self.cache = {}

    def row(self, kind, t):
        at = 16 * self.blocks[kind] + t + STEPS
        return jnp.broadcast_to(self.maps[self.j, at : at + 1, :], (self.levels, LANES))

    def get(self, kind, t):
        if (kind, t) not in self.cache:
            side, _, what = kind.partition("_")
            if kind == "column":
                value = jnp.where(self.level + 1.0 < self.row("wet", t), vertical_mix, 0.0)
            elif kind == "wet" or what == "open":
                value = self.level < self.row(kind, t)
            else:
                value = jnp.where(self.get(side + "_open", t), self.row(kind, t), 0.0)
            self.cache[kind, t] = value
        return self.cache[kind, t]


def column(field, coefficient):
    half = field.shape[0] // 2
    even, odd = field[:half], field[half:]
    after_even = coefficient[:half] * (odd - even)
    after_odd = coefficient[half:] * (pltpu.roll(even, half - 1, 0) - odd)
    return jnp.concatenate([after_even - pltpu.roll(after_odd, 1, 0), after_odd - after_even], axis=0)


def gaps(fields, rows):
    turned = [{t: east(field[t]) for t in rows} for field in fields]
    to_east = [{t: turn[t] - field[t] for t in rows} for turn, field in zip(turned, fields)]
    faces = range(rows[0] - 1, rows[-1] + 1)
    to_north = [{t: field[t + 1] - field[t] for t in faces} for field in fields]
    return list(zip(to_east, to_north))


def fluxes(coefs, kind, steps):
    return [
        (
            {t: coef.get("east_" + kind, t) * to_east[t] for t in to_east},
            {t: coef.get("north_" + kind, t) * to_north[t] for t in to_north},
        )
        for coef, (to_east, to_north) in zip(coefs, steps)
    ]


def both(ones, others):
    return [
        tuple({t: a[t] + b[t] for t in a} for a, b in zip(one, other)) for one, other in zip(ones, others)
    ]


def gathered_in(flux, rows, fields=None, coefs=None):
    turned = [{t: west(across[t]) for t in rows} for across, _ in flux]
    still = [{t: along[t] - along[t - 1] for t in rows} for _, along in flux]
    if fields is not None:
        still = [
            {t: rest[t] + (field[t] + column(field[t], coef.get("column", t))) for t in rows}
            for rest, field, coef in zip(still, fields, coefs)
        ]
    return [
        {t: rest[t] + (across[t] - turn[t]) for t in rows}
        for rest, (across, _), turn in zip(still, flux, turned)
    ]


def face_maps(own_maps, nears, fars, maps, strips, levels, kinds=(0, 1, 2)):
    count, edge = lax.axis_size("lat"), lax.axis_index("lat")
    keep = jnp.where(jnp.logical_and(edge != 0, edge != count - 1), 1.0, 0.0)

    def north(x):
        return pltpu.roll(x, 15, 0)

    for i, j in enumerate(strips):
        whole = []
        piece = piece_of(j)
        for a in kinds:
            at = (PIECES[piece + 1] - PIECES[piece]) * STEPS * levels + (3 * (j - PIECES[piece]) + a) * STEPS
            low = fars[piece][at : at + STEPS, :]
            if a == 2:
                low = low * keep
            near, local, size = near_place(nears, j)
            at = size * STEPS * levels + (3 * local + a) * STEPS
            high = near[at : at + STEPS, :]
            whole.append(jnp.concatenate([low, own_maps[j, 4 * a : 4 * a + 4, :], high, high, high], axis=0))
        depth = whole.pop()
        blocks = [depth] + [jnp.minimum(depth, f(depth)) for f in (east, north)]
        blocks += [0.5 * (x + f(x)) for x in whole for f in (east, north)]
        for b, block in enumerate(blocks):
            maps[i, 16 * b : 16 * b + 16, :] = block


def class_hits(value, label, levels):
    top = value.astype(jnp.bfloat16)
    bottom = (value - top.astype(jnp.float32)).astype(jnp.bfloat16)
    high = (label >> LOW_SHIFT).astype(jnp.float32).astype(jnp.bfloat16)
    low = (label & (LOW_COUNT - 1)).astype(jnp.float32).astype(jnp.bfloat16)
    none = jnp.zeros((levels, LANES), jnp.bfloat16)
    one = jnp.ones((levels, LANES), jnp.bfloat16)
    left = [jnp.where(high == jnp.bfloat16(h), one, none) for h in range(HIGH_COUNT)]
    picks = [low == jnp.bfloat16(l) for l in range(LOW_COUNT)]
    right = [jnp.where(p, part, none) for part in (top, bottom) for p in picks]
    return jnp.concatenate(left, axis=0), jnp.concatenate(right, axis=0)


def later_row(n, t):
    return (n - 1) * 8 + t + STEPS - n


def forward(piece, *refs):
    last = piece + 2 == len(PIECES)
    refs = list(refs)
    near_parts = len(NEAR_PIECES) - 1
    own, own_maps, far, classes = refs[:4]
    nears = refs[4 : 4 + near_parts]
    del refs[: 4 + near_parts]
    before = refs.pop(0) if piece > 0 else None
    scales = refs.pop(0) if last else None
    out, later = refs[:2]
    weighted, maps = refs[2:] if last else (None, refs[2])
    levels = own.shape[1] // 4
    group = list(range(PIECES[piece], PIECES[piece + 1]))
    face_maps(own_maps, nears, {piece: far}, maps, group, levels)
    lane = lax.broadcasted_iota(jnp.int32, (levels, LANES), 1)
    inner = jnp.logical_and(lane >= GHOST, lane < LANES - GHOST)
    coefs = [Coefficients(maps, u, levels) for u in range(len(group))]
    fields, tangents = [], None
    for u, j in enumerate(group):
        field = {t: own[j, t * levels : (t + 1) * levels, :] for t in range(4)}
        for s in range(STEPS):
            at = (u * STEPS + s) * levels
            field[s - STEPS] = far[at : at + levels, :]
            near, local, _ = near_place(nears, j)
            at = (local * STEPS + s) * levels
            field[4 + s] = near[at : at + levels, :]
        fields.append(field)
    for n in range(STEPS):
        rows = list(range(n + 1 - STEPS, 4 + STEPS - n - 1))
        steps = gaps(fields, rows)
        push = fluxes(coefs, "dir", steps)
        if n == 0:
            following = gathered_in(push, rows)
        else:
            push = both(push, fluxes(coefs, "mix", gaps(tangents, rows)))
            following = gathered_in(push, rows, tangents, coefs)
        tangents = following
        if n + 1 < STEPS:
            fields = gathered_in(fluxes(coefs, "mix", steps), rows, fields, coefs)
            for u in range(len(group)):
                for t in rows:
                    at = later_row(n + 1, t) * levels
                    later[u, at : at + levels, :] = fields[u][t]
    finished = []
    for pair in range(2):
        lefts, rights = [], []
        for u, j in enumerate(group):
            for t in (2 * pair, 2 * pair + 1):
                chosen = jnp.logical_and(inner, coefs[u].get("wet", t))
                value = jnp.where(chosen, tangents[u][t], 0.0)
                left, right = class_hits(value, classes[j, t * levels : (t + 1) * levels, :], levels)
                lefts.append(left)
                rights.append(right)
        gram = lax.dot_general(
            jnp.concatenate(lefts, axis=1),
            jnp.concatenate(rights, axis=1),
            (((1,), (1,)), ((), ())),
            preferred_element_type=jnp.float32,
        )
        gram = gram if before is None else before[pair] + gram
        if last:
            finished.append(gram)
        else:
            out[pair] = gram
    if last:
        class_sums(finished, scales, out, weighted, levels)


def class_sums(grams, scales, sums, weighted, levels):
    width = 2 * LOW_COUNT * levels
    own_level = lax.broadcasted_iota(jnp.int32, (levels, width), 0)
    other_level = lax.broadcasted_iota(jnp.int32, (levels, width), 1) & (levels - 1)
    diagonal = own_level == other_level
    sheets = []
    for pair in range(2):
        for h in range(HIGH_COUNT):
            sheet = jnp.where(diagonal, grams[pair][h * levels : (h + 1) * levels, :], 0.0)
            sheets.append(jnp.sum(sheet, axis=0, keepdims=True))
        sheets.append(jnp.zeros((16 - HIGH_COUNT, width), jnp.float32))
    rest = jnp.concatenate(sheets, axis=0)
    parts = []
    for _ in range(3):
        part = rest.astype(jnp.bfloat16)
        rest = rest - part.astype(jnp.float32)
        parts.append(part)
    at_low = (lax.broadcasted_iota(jnp.int32, (width, LANES), 0) >> (levels.bit_length() - 1)) & (LOW_COUNT - 1)
    of_low = lax.broadcasted_iota(jnp.int32, (width, LANES), 1) & (LOW_COUNT - 1)
    gather = jnp.where(at_low == of_low, 1.0, 0.0).astype(jnp.bfloat16)
    added = jnp.dot(jnp.concatenate(parts, axis=0), gather, preferred_element_type=jnp.float32)
    added = (added[64:96] + added[32:64]) + added[0:32]
    here = lax.broadcasted_iota(jnp.int32, (16, LANES), 0)
    label = lax.broadcasted_iota(jnp.int32, (16, LANES), 1)
    totals = [
        jnp.sum(
            jnp.where(here == (label >> LOW_SHIFT), added[16 * p : 16 * p + 16], 0.0), axis=0, keepdims=True
        )
        for p in range(2)
    ]
    finish_sums(scales, totals, sums, weighted)


def finish_sums(scales, totals, sums, weighted):
    sums[...] = jnp.concatenate([totals[p] + scales[4 + p : 5 + p, :] for p in range(2)], axis=0)
    weighted[0:2, :] = jnp.concatenate([scales[p : p + 1, :] * totals[p] for p in range(2)], axis=0)


def finish(own_share, near_share, far_share, *refs):
    pieces, binned, gradient = refs[:-2], refs[-2], refs[-1]
    up = own_share[...] + (near_share[...] + far_share[...])
    down = jnp.concatenate([up[t : t + 1] for t in reversed(range(up.shape[0]))], axis=0)
    gradient[...] = jnp.where(is_odd(), down, up)
    band_own, class_count = binned.shape
    first = lax.axis_index("lat") * band_own
    found = [jnp.zeros((1, LANES), jnp.float32) for _ in range(band_own)]
    for piece in pieces:
        totals = piece[...]
        bands = jnp.broadcast_to(totals[:, LANES - 1 :], totals.shape)
        for m in range(band_own):
            hit = jnp.where(bands == (first + m).astype(jnp.float32), totals, 0.0)
            found[m] = found[m] + jnp.sum(hit, axis=0, keepdims=True)
    whole = jnp.concatenate(found, axis=0)
    binned[...] = whole[:, :class_count]


def base_rows(n, j, rows, own, nears, fars, laters):
    levels = own.shape[1] // 4
    piece = piece_of(j)
    local = j - PIECES[piece]
    field = {}
    for t in rows:
        if n > 0:
            at = later_row(n, t) * levels
            field[t] = laters[piece][local, at : at + levels, :]
        elif t < 0:
            at = (local * STEPS + t + STEPS) * levels
            field[t] = fars[piece][at : at + levels, :]
        elif t < 4:
            field[t] = own[j, t * levels : (t + 1) * levels, :]
        else:
            near, place, _ = near_place(nears, j)
            at = (place * STEPS + t - 4) * levels
            field[t] = near[at : at + levels, :]
    return field


def kept_row(n, t):
    if n == STEPS - 1:
        return t
    return 4 + t + 1 if n > 0 else 10 + {-1: 0, 0: 1, 3: 2, 4: 3}[t]


def add_terms(total, basis, steps, places, shift):
    for t in places:
        gap = (shift(basis[t]) if shift else basis[t + 1]) - basis[t]
        term = gap * steps[t]
        total[t] = total[t] + term if t in total else term


def shares(coefs, east_total, north_total, rows):
    none = jnp.zeros((1, LANES), jnp.float32)
    pad = [none] * (-len(rows) % 8)

    def summed(coef, kind, total):
        return {
            t: jnp.sum(jnp.where(coef.get(kind, t), x, 0.0), axis=0, keepdims=True) for t, x in total.items()
        }

    across = []
    for coef, total in zip(coefs, east_total):
        sums = summed(coef, "east_open", total)
        across.append(jnp.concatenate([sums.get(t, none) for t in rows] + pad, axis=0))
    turned = [west(x) for x in across]
    strips = []
    for coef, total, x, turn in zip(coefs, north_total, across, turned):
        sums = summed(coef, "north_open", total)
        along = [sums.get(t, none) + sums.get(t - 1, none) for t in rows]
        strips.append(-0.5 * (jnp.concatenate(along + pad, axis=0) + (x + turn)))
    whole = jnp.concatenate([x[:, GHOST : LANES - GHOST] for x in strips], axis=1)
    return {t: whole[i : i + 1] for i, t in enumerate(rows)}


def adjoint_part(own, own_maps, classes, weighted, *refs):
    parts, near_parts = len(PIECES) - 1, len(NEAR_PIECES) - 1
    nears, refs = refs[:near_parts], refs[near_parts:]
    fars, laters = refs[:parts], refs[parts : 2 * parts]
    near_share, far_share, kept, maps = refs[2 * parts :]
    strips = own.shape[0]
    levels = own.shape[1] // 4
    group = list(range(strips))
    face_maps(own_maps, nears, fars, maps, group, levels, kinds=(0, 2))
    coefs = [Coefficients(maps, j, levels) for j in group]
    adjoints = []
    for j in group:
        adjoint = {}
        for t in range(4):
            label = classes[j, t * levels : (t + 1) * levels, :]
            row = t // 2
            table = jnp.broadcast_to(weighted[row : row + 1, :], (8, LANES))
            value = jnp.concatenate(
                [jnp.take_along_axis(table, label[k : k + 8, :], axis=1) for k in range(0, levels, 8)], axis=0
            )
            adjoint[t] = jnp.where(coefs[j].get("wet", t), value, 0.0)
        adjoints.append(adjoint)
    east_total = [{} for _ in group]
    north_total = [{} for _ in group]
    for n in reversed(range(STEPS)):
        rows = list(range(n + 1 - STEPS, 3 + STEPS - n))
        low, high = rows[0], rows[-1]
        for j in group:
            for t in [t for t in adjoints[j] if -1 <= t <= 4]:
                at = kept_row(n, t) * levels
                kept[j, at : at + levels, :] = adjoints[j][t]
        outer = [t for t in rows if t < 0 or t > 3]
        made = [t for t in rows if n != 1 or t < 1 or t > 2]
        turning = made if n > 0 else outer
        turned = [{t: east(field[t]) for t in turning} for field in adjoints]
        to_east = [{t: turn[t] - field[t] for t in turn} for turn, field in zip(turned, adjoints)]
        to_north = [
            {
                low - 1: field[low],
                high: -field[high],
                **{t: field[t + 1] - field[t] for t in rows[:-1] if t in field and t + 1 in field},
            }
            for field in adjoints
        ]
        if n > 0:
            across = [{t: coef.get("east_mix", t) * x[t] for t in made} for coef, x in zip(coefs, to_east)]
            turned = [{t: west(x[t]) for t in made} for x in across]
            along = [{t: coef.get("north_mix", t) * x[t] for t in x} for coef, x in zip(coefs, to_north)]
            following = []
            for j in group:
                field, flux = adjoints[j], along[j]
                new = {low - 1: flux[low - 1], high + 1: -flux[high]}
                for t in made:
                    still = field[t] + column(field[t], coefs[j].get("column", t)) + (flux[t] - flux[t - 1])
                    new[t] = still + (across[j][t] - turned[j][t])
                following.append(new)
            adjoints = following
        for j in group:
            needed = [t for t in range(low - 1, high + 2) if t <= 0 or t >= 3]
            basis = base_rows(n, j, needed, own, nears, fars, laters)
            faces = [t for t in to_north[j] if t < 0 or t > 2]
            add_terms(east_total[j], basis, to_east[j], outer, east)
            add_terms(north_total[j], basis, to_north[j], faces, None)
    low_rows, high_rows = [-3, -2, -1], [4, 5, 6]
    share = shares(coefs, east_total, north_total, low_rows + high_rows)
    blank = jnp.zeros_like(share[-1])
    far_share[...] = jnp.concatenate([share[-1], share[-2], share[-3], blank], axis=0)
    near_share[...] = jnp.concatenate([blank, share[6], share[5], share[4]], axis=0)


def own_part(own, own_maps, kept, *refs):
    parts, near_parts = len(PIECES) - 1, len(NEAR_PIECES) - 1
    nears, refs = refs[:near_parts], refs[near_parts:]
    fars, laters = refs[:parts], refs[parts : 2 * parts]
    own_share, maps = refs[2 * parts :]
    levels = own.shape[1] // 4
    group = list(range(own.shape[0]))
    face_maps(own_maps, nears, fars, maps, group, levels, kinds=(0, 2))
    coefs = [Coefficients(maps, j, levels) for j in group]
    east_total = [{} for _ in group]
    north_total = [{} for _ in group]

    def adjoint_of(n, j, rows):
        return {t: kept[j, kept_row(n, t) * levels : (kept_row(n, t) + 1) * levels, :] for t in rows}

    middle = [adjoint_of(1, j, range(4)) for j in group]
    across, along = zip(*fluxes(coefs, "mix", gaps(middle, [1, 2])))
    inner = gathered_in(list(zip(across, along)), [1, 2], middle, coefs)
    for n in range(STEPS):
        last = n == STEPS - 1
        adjoints = []
        for j in group:
            if n == 0:
                adjoints.append({**adjoint_of(0, j, (-1, 0, 3, 4)), **inner[j]})
            else:
                adjoints.append(adjoint_of(n, j, range(4) if last else range(-1, 5)))
        for j, adjoint in zip(group, adjoints):
            to_east = {t: east(adjoint[t]) - adjoint[t] for t in range(4)}
            faces = range(3) if last else range(-1, 4)
            to_north = {t: adjoint[t + 1] - adjoint[t] for t in faces}
            if last:
                to_north.update({-1: adjoint[0], 3: -adjoint[3]})
            basis = base_rows(n, j, range(-1, 5), own, nears, fars, laters)
            add_terms(east_total[j], basis, to_east, range(4), east)
            add_terms(north_total[j], basis, to_north, range(-1, 4), None)
    share = shares(coefs, east_total, north_total, list(range(4)))
    own_share[...] = jnp.concatenate([share[t] for t in range(4)], axis=0)


def near_pairs(count):
    return [(i, i ^ 1) for i in range(count)]


def far_pairs(members, count):
    pairs = []
    for m in range(members):
        for i in range(1, count - 1, 2):
            pairs += [(m * count + i, m * count + i + 1), (m * count + i + 1, m * count + i)]
        for i in (0, count - 1):
            pairs.append((m * count + i, (m ^ 1) * count + i))
    return pairs


def routes(count):
    bits = count.bit_length() - 1
    groups = []
    for bit in range(bits - 2, -1, -2):
        one, two = 1 << bit, 2 << bit
        groups.append([one, two, one + two] if bit > 0 else [3, 2, 1])
    return groups + ([[1]] if bits % 2 else [])


def vmem(count):
    return [pl.BlockSpec(memory_space=pltpu.VMEM)] * count


def cost(nanoseconds):
    return pl.CostEstimate(flops=1153500 * nanoseconds, bytes_accessed=3690 * nanoseconds, transcendentals=0)


def body(tracer, diffusivity, direction, column_depth, density_class, band_of_row, weights):
    levels, rows, lon_count = tracer.shape
    strips = lon_count // OWN
    count = lax.axis_size("lat")
    members = lax.axis_size("members")
    params = pltpu.CompilerParams(vmem_limit_bytes=VMEM_LIMIT)
    f32, i32 = jnp.float32, jnp.int32
    halo = strips * STEPS * levels
    payload = halo + strips * 9

    def to_near(x):
        return lax.ppermute(x, "lat", near_pairs(count))

    def to_far(x):
        return lax.ppermute(x, ("members", "lat"), far_pairs(members, count))

    sizes = [b - a for a, b in zip(PIECES, PIECES[1:])]
    near_sizes = [b - a for a, b in zip(NEAR_PIECES, NEAR_PIECES[1:])]
    fields = (tracer, diffusivity, direction, column_depth)
    in_place = [pltpu.with_memory_space_constraint(x, pltpu.HBM) for x in fields]
    taken = dict(
        in_specs=[pl.BlockSpec(memory_space=pltpu.HBM)] * 4,
        scratch_shapes=[pltpu.VMEM(x.shape, x.dtype) for x in fields] + [pltpu.SemaphoreType.DMA((4,))],
        compiler_params=params,
    )
    far_shapes = [jax.ShapeDtypeStruct((payload // strips * size, LANES), f32) for size in sizes]
    first_out = pl.pallas_call(
        pack_first,
        name="pack_first",
        out_shape=far_shapes[0],
        out_specs=pl.BlockSpec(memory_space=pltpu.VMEM),
        **taken,
    )(*in_place)
    fars = [to_far(first_out)]
    late_fields = lax.optimization_barrier((*fields, first_out))[: len(fields)]
    in_place = [pltpu.with_memory_space_constraint(x, pltpu.HBM) for x in late_fields]
    own, own_maps, *outs = pl.pallas_call(
        pack_fields,
        name="pack_fields",
        out_shape=(
            jax.ShapeDtypeStruct((strips, rows * levels, LANES), f32),
            jax.ShapeDtypeStruct((strips, 16, LANES), f32),
            *[jax.ShapeDtypeStruct((payload // strips * size, LANES), f32) for size in near_sizes],
            *far_shapes[1:],
        ),
        out_specs=tuple(vmem(1 + len(near_sizes) + len(sizes))),
        **taken,
    )(*in_place)
    nears = [to_near(x) for x in outs[: len(near_sizes)]]
    fars += [to_far(x) for x in outs[len(near_sizes) :]]

    own_classes, scales = pl.pallas_call(
        pack_classes,
        name="pack_classes",
        out_shape=(
            jax.ShapeDtypeStruct((strips, rows * levels, LANES), i32),
            jax.ShapeDtypeStruct((8, LANES), f32),
        ),
        in_specs=[pl.BlockSpec(memory_space=pltpu.HBM)] * 3,
        out_specs=tuple(vmem(2)),
        scratch_shapes=[
            pltpu.VMEM(density_class.shape, i32),
            pltpu.VMEM(weights.shape, f32),
            pltpu.SMEM(band_of_row.shape, i32),
            pltpu.SemaphoreType.DMA((3,)),
        ],
        compiler_params=params,
    )(*[pltpu.with_memory_space_constraint(x, pltpu.HBM) for x in (density_class, weights, band_of_row)])
    laters, sums = [], None
    gram_shape = (2, HIGH_COUNT * levels, 2 * LOW_COUNT * levels)
    for piece, size in enumerate(sizes):
        last = piece + 1 == len(sizes)
        given = [own, own_maps, fars[piece], own_classes, *nears]
        given += ([sums] if piece > 0 else []) + ([scales] if last else [])
        sums, later, *weighted = pl.pallas_call(
            functools.partial(forward, piece),
            name="forward",
            out_shape=(
                jax.ShapeDtypeStruct((2, LANES) if last else gram_shape, f32),
                jax.ShapeDtypeStruct((size, 14 * levels, LANES), f32),
            )
            + ((jax.ShapeDtypeStruct((8, LANES), f32),) if last else ()),
            in_specs=vmem(len(given)),
            out_specs=tuple(vmem(3 if last else 2)),
            cost_estimate=cost(2000),
            scratch_shapes=[pltpu.VMEM((size, 16 * MAP_FIELDS, LANES), f32)],
            compiler_params=params,
        )(*given)
        laters.append(later)

    gathered = sums
    groups = routes(count)
    for i, group in enumerate(groups):
        others = [lax.ppermute(gathered, "lat", [(d, d ^ k) for d in range(count)]) for k in group]
        pieces = [gathered] + others
        if i == 0:
            near_share, far_share, kept = pl.pallas_call(
                adjoint_part,
                name="adjoint_part",
                out_shape=(
                    jax.ShapeDtypeStruct((rows, lon_count), f32),
                    jax.ShapeDtypeStruct((rows, lon_count), f32),
                    jax.ShapeDtypeStruct((strips, 14 * levels, LANES), f32),
                ),
                in_specs=vmem(4 + len(nears) + 2 * len(sizes)),
                out_specs=tuple(vmem(3)),
                scratch_shapes=[pltpu.VMEM((strips, 16 * 5, LANES), f32)],
                compiler_params=params,
            )(own, own_maps, own_classes, weighted[0], *nears, *fars, *laters)
            near_share, far_share = to_near(near_share), to_far(far_share)
        if i + 1 < len(groups):
            gathered = jnp.concatenate(pieces, axis=0)
    own_share = pl.pallas_call(
        own_part,
        name="own_part",
        out_shape=jax.ShapeDtypeStruct((rows, lon_count), f32),
        in_specs=vmem(3 + len(nears) + 2 * len(sizes)),
        out_specs=pl.BlockSpec(memory_space=pltpu.VMEM),
        scratch_shapes=[pltpu.VMEM((strips, 16 * 5, LANES), f32)],
        compiler_params=params,
    )(own, own_maps, kept, *nears, *fars, *laters)
    binned, gradient = pl.pallas_call(
        finish,
        name="finish",
        out_shape=(
            jax.ShapeDtypeStruct((weights.shape[0] // count, weights.shape[1]), f32),
            jax.ShapeDtypeStruct((rows, lon_count), f32),
        ),
        in_specs=vmem(3 + len(pieces)),
        out_specs=tuple(vmem(2)),
        compiler_params=params,
    )(own_share, near_share, far_share, *pieces)
    return binned, gradient


def solution(mesh):
    placed = (
        P(None, ("members", "lat"), None),
        P("lat", None),
        P(("members", "lat"), None),
        P("lat", None),
        P(None, ("members", "lat"), None),
        P("lat"),
        P(),
    )
    return jax.shard_map(
        body,
        mesh=mesh,
        in_specs=placed,
        out_specs=(P(("members", "lat"), None), P(("members", "lat"), None)),
        check_vma=False,
    )
```
